128 devices in a mesh: dp: 4 (over y), ha: 4 (over z), wa: 8 (over x, core).
Axes of the slice: x: 4, y: 4, z: 4, core: 2. Of those that a mesh axis runs over, the one named last changes fastest.
Arguments:
- left_feat: bfloat16 [4, 32, 192, 128], P('dp', 'ha', 'wa'), may hold values from -512 to 512
- right_feat: bfloat16 [4, 32, 192, 128], P('dp', 'ha', 'wa'), may hold values from -512 to 512
- conv_weight: float32 [8, 3, 3, 3], replicated, may hold values from -1.6 to 1.6
- disparity_gt: int32 [4, 32, 192], P('dp', 'ha', 'wa'), may hold values from 0 to 191
- valid_mask: int32 [4, 32, 192], P('dp', 'ha', 'wa'), may hold values 0 or 1
Outputs:
- loss: float32 [], replicated
- grad_left: float32 [4, 32, 192, 128], P('dp', 'ha', 'wa')
- grad_right: float32 [4, 32, 192, 128], P('dp', 'ha', 'wa')
- grad_weight: float32 [8, 3, 3, 3], replicated
The draws below stay inside these ranges and needn't reach their ends.
All inputs are finite; a program needn't handle non-finite values. No bound on the sum of `valid_mask` on one device may be relied on, other than what follows from the above.
Results may differ from the reference program's by a relative error of at most 0.009.
Values may be sent and summed in bfloat16 or wider, within the bound.
No kernel may reach another device: no remote copies, remote signals or barrier semaphores. Data moves between devices by JAX's collectives and lax.ppermute only.
A program may use at most 256 MiB of HBM per device.

```python
import jax
import jax.numpy as jnp
from jax import lax

C = 128
G = 8
D = 192
IMAGES = 4
HT = 32
WT = 192


def feature_pair(key):
    keys = jax.random.split(key, 2)
    shape = (IMAGES, HT, WT, C)
    left_values = jnp.clip(jax.random.normal(keys[0], shape, jnp.float32), -4.0, 4.0)
    right_values = jnp.clip(jax.random.normal(keys[1], shape, jnp.float32), -4.0, 4.0)
    return (left_values, right_values)


def draw_left_feat(key, part):
    left_values, right_values = feature_pair(key)
    return left_values.astype(jnp.bfloat16)


def draw_right_feat(key, part):
    left_values, right_values = feature_pair(key)
    return right_values.astype(jnp.bfloat16)


def plant(array, rng, smallest, top_value):
    longest = array.shape.index(max(array.shape))
    spots = []
    for shift in (0, 1):
        where = [jax.random.randint(jax.random.fold_in(rng, axis), (), 0, length) for axis, length in enumerate(array.shape)]
        where[longest] = (where[longest] + shift) % array.shape[longest]
        spots.append(tuple(where))
    return array.at[spots[0]].set(smallest).at[spots[1]].set(top_value)


def gaussian(own_key, dims, deviation, reach, held_as=jnp.bfloat16):
    return jnp.clip(deviation * jax.random.normal(own_key, dims, jnp.float32), -reach, reach).astype(held_as)


def setup_inputs(seed: int = 0) -> dict:
    splits = jax.random.split(jax.random.key(seed), 6)
    left_feat = draw_left_feat(jax.random.fold_in(splits[5], 71), 0)
    right_feat = draw_right_feat(jax.random.fold_in(splits[5], 71), 0)
    conv_weight = gaussian(splits[2], (G, 3, 3, 3), 0.4, 1.6, jnp.float32)
    disparity_gt = plant(jax.random.randint(splits[3], (IMAGES, HT, WT), 0, D), jax.random.fold_in(splits[3], 1), 0, D - 1).astype(jnp.int32)
    valid_mask = plant((jax.random.randint(splits[4], (IMAGES, HT, WT), 0, 4) < 3).astype(jnp.int32), jax.random.fold_in(splits[4], 1), 0, 1)
    return dict(left_feat=left_feat, right_feat=right_feat, conv_weight=conv_weight, disparity_gt=disparity_gt, valid_mask=valid_mask)


precise = lax.Precision.HIGHEST

def build_cost(left_values, right_values):
    height, width_all, channels = left_values.shape
    per_group = channels // G
    left_groups = left_values.reshape(height, width_all, G, per_group)
    right_padded = jnp.pad(right_values, ((0, 0), (D - 1, 0), (0, 0))).reshape(height, width_all + D - 1, G, per_group)

    def level_slice(level_index):
        shifted = lax.dynamic_slice_in_dim(right_padded, (D - 1 - level_index).astype(jnp.int32), width_all, 1)
        return lax.optimization_barrier(jnp.sum(left_groups * shifted, axis=3)) / per_group
    stacked = lax.map(level_slice, jnp.arange(D, dtype=jnp.int32))
    return jnp.transpose(stacked, (1, 2, 3, 0))

def aggregate(cost_volume, weight):
    height, width_all = (cost_volume.shape[0], cost_volume.shape[1])
    padded = jnp.pad(cost_volume, ((1, 1), (1, 1), (0, 0), (1, 1)))
    running = jnp.zeros((height, width_all, D), jnp.float32)
    for row_tap in range(3):
        for col_tap in range(3):
            for lev_tap in range(3):
                window = padded[row_tap:row_tap + height, col_tap:col_tap + width_all, :, lev_tap:lev_tap + D]
                running = running + jnp.einsum('hwgd,g->hwd', window, weight[:, row_tap, col_tap, lev_tap], precision=precise)
    return running

def cost_loss(cost_volume, weight, target, usable):
    logits = aggregate(cost_volume, weight)
    probability = jax.nn.softmax(logits, axis=-1)
    estimate = lax.optimization_barrier(jnp.sum(probability * jnp.arange(D, dtype=jnp.float32), axis=-1))
    residual = estimate - target
    smooth_loss = jnp.where(jnp.abs(residual) < 1.0, 0.5 * residual * residual, jnp.abs(residual) - 0.5)
    return jnp.sum(usable * smooth_loss)

def feature_grads(gcost_low, left_image, right_image):
    height, width_all, channels = left_image.shape
    per_group = channels // G
    left_groups = left_image.astype(jnp.float32).reshape(height, width_all, G, per_group)
    right_groups = right_image.astype(jnp.float32).reshape(height, width_all, G, per_group)
    right_padded = jnp.pad(right_groups, ((0, 0), (D - 1, 0), (0, 0), (0, 0)))
    gcost_values = gcost_low.astype(jnp.float32)

    def level_step(carry, level_index):
        left_acc, right_acc = carry
        start = (D - 1 - level_index).astype(jnp.int32)
        shifted = lax.dynamic_slice_in_dim(right_padded, start, width_all, 1)
        factor = lax.dynamic_index_in_dim(gcost_values, level_index, 3, keepdims=False)[..., None]
        left_acc = left_acc + factor * shifted
        current = lax.dynamic_slice_in_dim(right_acc, start, width_all, 1)
        right_acc = lax.dynamic_update_slice_in_dim(right_acc, current + factor * left_groups, start, 1)
        return ((left_acc, right_acc), None)
    initial = (jnp.zeros((height, width_all, G, per_group), jnp.float32), jnp.zeros((height, width_all + D - 1, G, per_group), jnp.float32))
    (left_acc, right_acc), unused = lax.scan(level_step, initial, jnp.arange(D, dtype=jnp.int32))
    return (left_acc.reshape(height, width_all, channels), right_acc[:, D - 1:].reshape(height, width_all, channels))

def reference(left_feat, right_feat, conv_weight, disparity_gt, valid_mask):
    columns = jnp.arange(disparity_gt.shape[2], dtype=jnp.int32)
    usable = (valid_mask * (disparity_gt <= columns).astype(jnp.int32)).astype(jnp.float32)
    normaliser = 1.0 / jnp.maximum(jnp.sum(usable), 1.0)
    target = disparity_gt.astype(jnp.float32)
    per_group = left_feat.shape[3] // G

    def per_image(entries):
        left_image, right_image, target_image, usable_image = entries
        cost_volume = build_cost(left_image.astype(jnp.float32), right_image.astype(jnp.float32))

        def objective(cost_values, weight):
            return cost_loss(cost_values, weight, target_image, usable_image)
        value, pullback = jax.vjp(objective, cost_volume, conv_weight)
        gcost, grad_kernel = pullback(jnp.ones_like(value))
        gcost_low = (gcost / per_group).astype(jnp.bfloat16)
        grad_left, grad_right = feature_grads(gcost_low, left_image, right_image)
        return (value, grad_left, grad_right, grad_kernel)
    values, grad_left, grad_right, grad_kernel = lax.map(per_image, (left_feat, right_feat, target, usable))
    return (jnp.sum(values) * normaliser, grad_left * normaliser, grad_right * normaliser, lax.optimization_barrier(jnp.sum(grad_kernel, axis=0)) * normaliser)
```

```python
import jax
import jax.numpy as jnp
from jax import lax
from jax.experimental import pallas as pl
from jax.experimental.pallas import tpu as pltpu
from jax.sharding import PartitionSpec as P

F32 = jnp.float32
BF16 = jnp.bfloat16
ROWS, TILE, CH = 8, 24, 128
WA = 8
WT = 192
JP = 256
GT_LANE, VALID_LANE = 0, 16
LOSS_LANE, COUNT_LANE = 9, 10
VMEM = pltpu.CompilerParams(vmem_limit_bytes=48 * 1024 * 1024)
NT = (((1,), (1,)), ((), ()))
NN = (((1,), (0,)), ((), ()))
TN = (((0,), (0,)), ((), ()))


def dot(lhs, rhs, dims=NN, precision=None):
    return lax.dot_general(lhs, rhs, dims, precision=precision, preferred_element_type=F32)


def meta_block(gt, valid, first, count, lane_of_first):
    row = lax.broadcasted_iota(jnp.int32, (ROWS, CH), 0)
    lane = lax.broadcasted_iota(jnp.int32, (ROWS, CH), 1)
    chosen = (row >= first) & (row < first + count)
    at = row - first + lane_of_first
    pick_gt = (chosen & (lane == at + GT_LANE)).astype(F32)
    pick_valid = (chosen & (lane == at + VALID_LANE)).astype(F32)
    return dot(gt, pick_gt, TN) + dot(valid, pick_valid, TN)


def halo_kernel(left_ref, right_ref, gt_ref, valid_ref, up_ref, down_ref):
    gt = gt_ref[...].astype(F32)
    valid = valid_ref[...].astype(F32)
    for i in range(2):
        up_ref[i] = left_ref[ROWS - 2 + i]
        up_ref[2 + i] = right_ref[ROWS - 2 + i]
        down_ref[i] = left_ref[i]
        down_ref[2 + i] = right_ref[i]
    up_ref[4] = meta_block(gt, valid, ROWS - 2, 2, 0).astype(BF16)
    down_ref[4] = meta_block(gt, valid, 0, 2, ROWS + 2).astype(BF16)


def pack_kernel(left_ref, right_ref, gt_ref, valid_ref, prev_ref, next_ref, out_ref):
    gt = gt_ref[...].astype(F32)
    valid = valid_ref[...].astype(F32)
    meta = meta_block(gt, valid, 0, ROWS, 2)
    meta = meta + prev_ref[4].astype(F32) + next_ref[4].astype(F32)
    for side, ref in ((0, left_ref), (1, right_ref)):
        for ext in range(ROWS + 4):
            if ext < 2:
                block = prev_ref[2 * side + ext]
            elif ext < ROWS + 2:
                block = ref[ext - 2]
            else:
                block = next_ref[2 * side + ext - ROWS - 2]
            for k in range(max(0, ext - 4), min(WA - 1, ext) + 1):
                out_ref[k, 5 * side + ext - k] = block
    for k in range(WA):
        rolled = meta if k == 0 else pltpu.roll(meta, CH - k, 1)
        out_ref[k, 10] = rolled.astype(BF16)


def split3(value):
    high = value.astype(BF16)
    rest = value - high.astype(F32)
    middle = rest.astype(BF16)
    low = (rest - middle.astype(F32)).astype(BF16)
    return high, middle, low


def main_kernel(recv_ref, wc_ref, out_ref, ls, rs, rb, lb, ab, ub, utb, xs, ys, zs, ks):
    ks[...] = jnp.zeros(ks.shape, F32)
    xs[...] = jnp.zeros(xs.shape, F32)
    ys[...] = jnp.zeros(ys.shape, F32)
    zs[...] = jnp.zeros(zs.shape, F32)

    @pl.loop(0, 5)
    def fill(rho):
        ls[rho, 0:8] = jnp.zeros((8, CH), F32)
        ls[rho, 8 + WT :] = jnp.zeros((8, CH), F32)
        rs[rho, 0:8] = jnp.zeros((8, CH), F32)
        rs[rho, 8 + WT :] = jnp.zeros((72, CH), F32)
        for src in range(WA):
            at = 8 + TILE * src
            ls[rho, at : at + TILE] = recv_ref[src, rho].astype(F32)
            rs[rho, at : at + TILE] = recv_ref[src, rho + 5].astype(F32)
        for si in range(5):
            rb[rho, :, si * CH : (si + 1) * CH] = rs[rho, 4 + si : 4 + si + JP].astype(BF16)

    lb[WT:] = jnp.zeros((JP - WT, 3 * CH), BF16)
    for b in range(3):
        lb[0:WT, b * CH : (b + 1) * CH] = ls[2, 7 + b : 7 + b + WT].astype(BF16)

    meta = jnp.concatenate([recv_ref[src, 10].astype(F32) for src in range(WA)], axis=0)
    lane = lax.broadcasted_iota(jnp.int32, (WT, CH), 1)
    ww = lax.broadcasted_iota(jnp.int32, (WT, JP), 0)
    jj = lax.broadcasted_iota(jnp.int32, (WT, JP), 1)
    level = (ww - jj + 2).astype(F32)
    inside = (jj <= ww + 2) & (jj >= ww - (WT - 3))
    on_diag = jj == ww + 2
    wcol = lax.broadcasted_iota(jnp.int32, (WT, 1), 0).astype(F32)
    zeros_count = jnp.maximum(float(WT - 3) - wcol, 0.0)
    zeros_mean = (wcol + float(WT + 2)) * 0.5

    def step(q, carry):
        loss_sum, count_sum = carry
        acc = None
        diag = jnp.zeros((WT, CH), F32)
        for a in range(3):
            rho = q + a
            shifted = [ls[rho, 7 + b : 7 + b + WT] for b in range(3)]
            for si in range(5):
                s = si - 2
                value = None
                for b in range(3):
                    e = b - s
                    if 0 <= e <= 2:
                        term = wc_ref[a, 3 * b + e : 3 * b + e + 1] * shifted[b]
                        value = term if value is None else value + term
                for i, part in enumerate(split3(value)):
                    ab[i * WT : (i + 1) * WT, (a * 5 + si) * CH : (a * 5 + si + 1) * CH] = part
            for b in range(3):
                diag = diag + wc_ref[a, 3 * b : 3 * b + 1] * shifted[b] * rs[rho, 8 + b : 8 + b + WT]
            part = dot(ab[:, a * 5 * CH : (a + 1) * 5 * CH], rb[rho], NT)
            acc = part if acc is None else acc + part
        diag_col = jnp.sum(diag, axis=1, keepdims=True)
        logits = acc[0:WT] + acc[WT : 2 * WT] + acc[2 * WT : 3 * WT]
        logits = logits - jnp.where(on_diag, diag_col, 0.0)
        top = jnp.max(jnp.where(inside, logits, -3e38), axis=1, keepdims=True)
        top = jnp.where(zeros_count > 0.0, jnp.maximum(top, 0.0), top)
        expd = jnp.where(inside, jnp.exp(logits - top), 0.0)
        zero_exp = jnp.where(zeros_count > 0.0, zeros_count * jnp.exp(-top), 0.0)
        denom = jnp.sum(expd, axis=1, keepdims=True) + zero_exp
        first = jnp.sum(expd * level, axis=1, keepdims=True) + zero_exp * zeros_mean
        inv = 1.0 / denom
        estimate = first * inv
        target = jnp.sum(jnp.where(lane == GT_LANE + 1 + q, meta, 0.0), axis=1, keepdims=True)
        valid = jnp.sum(jnp.where(lane == VALID_LANE + 1 + q, meta, 0.0), axis=1, keepdims=True)
        usable = jnp.where(target <= wcol, valid, 0.0)
        resid = estimate - target
        size = jnp.abs(resid)
        smooth = jnp.where(size < 1.0, 0.5 * resid * resid, size - 0.5)
        own = jnp.where(q == 1, 1.0, 0.0)
        loss_sum = loss_sum + own * jnp.sum(usable * smooth, axis=0, keepdims=True)
        count_sum = count_sum + own * jnp.sum(usable, axis=0, keepdims=True)
        factor = jnp.clip(resid, -1.0, 1.0) * usable * inv
        up = expd * (level - estimate) * factor
        up_diag = jnp.sum(jnp.where(on_diag, up, 0.0), axis=1, keepdims=True)
        high = up.astype(BF16)
        ub[0:WT] = high
        ub[WT : 2 * WT] = (up - high.astype(F32)).astype(BF16)
        flipped = jnp.concatenate([up, jnp.zeros((JP - WT, JP), F32)], axis=0).T
        high = flipped.astype(BF16)
        utb[0:JP] = high
        utb[JP : 2 * JP] = (flipped - high.astype(F32)).astype(BF16)
        left_terms = dot(ub[...], rb[2])
        left_terms = left_terms[0:WT] + left_terms[WT : 2 * WT]
        right_terms = dot(utb[...], lb[...])
        right_terms = right_terms[0:JP] + right_terms[JP : 2 * JP]
        a = 2 - q
        taps = [[wc_ref[a, 3 * b + e : 3 * b + e + 1] for e in range(3)] for b in range(3)]
        for b in range(3):
            own_left = ls[2, 7 + b : 7 + b + WT]
            lost = up_diag * rs[2, 8 + b : 8 + b + WT]
            total = None
            for e in range(3):
                si = b - e + 2
                value = left_terms[:, si * CH : (si + 1) * CH]
                if e == 0:
                    value = value - lost
                term = taps[b][e] * value
                total = term if total is None else total + term
                ks[a, 3 * b + e : 3 * b + e + 1] = jnp.sum(own_left * value, axis=0, keepdims=True)
            xs[b, 8 : 8 + WT] += total
            zs[b, 8 : 8 + WT] += taps[b][0] * up_diag * own_left
        for si in range(5):
            s = si - 2
            total = None
            for b in range(3):
                e = b - s
                if 0 <= e <= 2:
                    term = taps[b][e] * right_terms[:, b * CH : (b + 1) * CH]
                    total = term if total is None else total + term
            ys[si] += total
        return loss_sum, count_sum

    zero = jnp.zeros((1, 1), F32)
    loss_sum, count_sum = lax.fori_loop(0, 3, step, (zero, zero))

    grad_left = xs[0, 9 : 9 + WT] + xs[1, 8 : 8 + WT] + xs[2, 7 : 7 + WT]
    grad_right = ys[0, 4 : 4 + WT]
    for si in range(1, 5):
        grad_right = grad_right + ys[si, 4 - si : 4 - si + WT]
    for b in range(3):
        grad_right = grad_right - zs[b, 8 - b : 8 - b + WT]
    for dst in range(WA):
        out_ref[dst, 0] = grad_left[TILE * dst : TILE * (dst + 1)].astype(BF16)
        out_ref[dst, 1] = grad_right[TILE * dst : TILE * (dst + 1)].astype(BF16)

    group = lax.broadcasted_iota(jnp.int32, (8, CH), 0)
    channel = lax.broadcasted_iota(jnp.int32, (8, CH), 1)
    member = (channel // 16 == group).astype(F32)
    by_tap = jnp.concatenate([ks[0], ks[1], ks[2], jnp.zeros((CH - 48, CH), F32)], axis=0)
    sums = dot(member, by_tap, NT, precision=lax.Precision.HIGHEST) * (1.0 / 16.0)
    sums = jnp.where(channel == LOSS_LANE, loss_sum, sums)
    sums = jnp.where(channel == COUNT_LANE, count_sum, sums)
    high, middle, low = split3(sums)
    packed = jnp.concatenate([high.astype(F32), middle.astype(F32), low.astype(F32)], axis=0).astype(BF16)
    for dst in range(WA):
        out_ref[dst, 2] = packed


def partial_kernel(recv_ref, out_ref):
    total = recv_ref[0, 2].astype(F32)
    for src in range(1, WA):
        total = total + recv_ref[src, 2].astype(F32)
    total = total[0:8] + total[8:16] + total[16:24]
    for i in range(out_ref.shape[0]):
        out_ref[i] = total


def finish_kernel(recv_ref, sums_ref, left_ref, right_ref, weight_ref, loss_ref):
    total = sums_ref[0]
    for i in range(1, sums_ref.shape[0]):
        total = total + sums_ref[i]
    norm = 1.0 / jnp.maximum(total[0:1, COUNT_LANE : COUNT_LANE + 1], 1.0)
    for src in range(WA):
        left_ref[src] = recv_ref[src, 0].astype(F32) * norm
        right_ref[src] = recv_ref[src, 1].astype(F32) * norm
    weight_ref[...] = total * norm
    loss_ref[...] = total[0:1, LOSS_LANE : LOSS_LANE + 1] * norm


def call(kernel, out_shape, *args, scratch=()):
    return pl.pallas_call(kernel, out_shape=out_shape, scratch_shapes=list(scratch), compiler_params=VMEM)(*args)


def shards(left_feat, right_feat, conv_weight, disparity_gt, valid_mask):
    left, right = left_feat[0], right_feat[0]
    gt, valid = disparity_gt[0], valid_mask[0]
    ha_count = lax.axis_size("ha")
    halo = jax.ShapeDtypeStruct((5, TILE, CH), BF16)
    up, down = call(halo_kernel, (halo, halo), left, right, gt, valid)
    before = lax.ppermute(up, "ha", [(i, i + 1) for i in range(ha_count - 1)])
    after = lax.ppermute(down, "ha", [(i + 1, i) for i in range(ha_count - 1)])
    taps = jnp.repeat(conv_weight.reshape(8, 27).T, 16, axis=1) * (1.0 / 16.0)
    taps = jnp.pad(taps.reshape(3, 9, CH), ((0, 0), (0, 7), (0, 0)))
    packed = call(
        pack_kernel, jax.ShapeDtypeStruct((WA, 11, TILE, CH), BF16), left, right, gt, valid, before, after
    )
    rows = lax.all_to_all(packed, "wa", 0, 0, tiled=True)
    grads = call(
        main_kernel,
        jax.ShapeDtypeStruct((WA, 3, TILE, CH), BF16),
        rows,
        taps,
        scratch=(
            pltpu.VMEM((5, WT + 16, CH), F32),
            pltpu.VMEM((5, WT + 80, CH), F32),
            pltpu.VMEM((5, JP, 5 * CH), BF16),
            pltpu.VMEM((JP, 3 * CH), BF16),
            pltpu.VMEM((3 * WT, 15 * CH), BF16),
            pltpu.VMEM((2 * WT, JP), BF16),
            pltpu.VMEM((2 * JP, JP), BF16),
            pltpu.VMEM((3, WT + 16, CH), F32),
            pltpu.VMEM((5, JP, CH), F32),
            pltpu.VMEM((3, WT + 16, CH), F32),
            pltpu.VMEM((3, 16, CH), F32),
        ),
    )
    back = lax.all_to_all(grads, "wa", 0, 0, tiled=True)
    others = lax.axis_size("dp") * ha_count
    partial = call(partial_kernel, jax.ShapeDtypeStruct((others, 8, CH), F32), back)
    sums = lax.all_to_all(partial, ("dp", "ha"), 0, 0, tiled=True)
    tile = jax.ShapeDtypeStruct((ROWS, TILE, CH), F32)
    grad_left, grad_right, weight, loss = call(
        finish_kernel,
        (tile, tile, jax.ShapeDtypeStruct((8, CH), F32), jax.ShapeDtypeStruct((1, 1), F32)),
        back,
        sums,
    )
    grad_weight = weight[:, :48].reshape(8, 3, 16)[:, :, :9].reshape(8, 3, 3, 3)
    return (loss[0, 0], grad_left[None], grad_right[None], grad_weight)


def solution(mesh):
    placed = (
        P("dp", "ha", "wa", None),
        P("dp", "ha", "wa", None),
        P(),
        P("dp", "ha", "wa"),
        P("dp", "ha", "wa"),
    )
    return jax.shard_map(
        shards,
        mesh=mesh,
        in_specs=placed,
        out_specs=(P(), P("dp", "ha", "wa", None), P("dp", "ha", "wa", None), P()),
        check_vma=False,
    )
```

```python
import jax
import jax.numpy as jnp
from jax import lax
from jax.experimental import pallas as pl
from jax.experimental.pallas import tpu as pltpu
from jax.sharding import PartitionSpec as P

F32 = jnp.float32
BF16 = jnp.bfloat16
ROWS, TILE, CH = 8, 24, 128
WA, CHIPS = 8, 4
WT = 192
JP = 256
GT_LANE, VALID_LANE = 0, 16
LOSS_LANE, COUNT_LANE = 9, 10
VMEM = pltpu.CompilerParams(vmem_limit_bytes=48 * 1024 * 1024)
FIRST = pltpu.CompilerParams(vmem_limit_bytes=60 * 1024 * 1024)
NT = (((1,), (1,)), ((), ()))
NN = (((1,), (0,)), ((), ()))
TN = (((0,), (0,)), ((), ()))


def dot(lhs, rhs, dims=NN, precision=None):
    return lax.dot_general(lhs, rhs, dims, precision=precision, preferred_element_type=F32)


def meta_block(gt, valid, first, count, lane_of_first):
    row = lax.broadcasted_iota(jnp.int32, (ROWS, CH), 0)
    lane = lax.broadcasted_iota(jnp.int32, (ROWS, CH), 1)
    chosen = (row >= first) & (row < first + count)
    at = row - first + lane_of_first
    pick_gt = (chosen & (lane == at + GT_LANE)).astype(F32)
    pick_valid = (chosen & (lane == at + VALID_LANE)).astype(F32)
    return dot(gt, pick_gt, TN) + dot(valid, pick_valid, TN)


def halo_kernel(left_ref, right_ref, gt_ref, valid_ref, up_ref, down_ref):
    gt = gt_ref[...].astype(F32)
    valid = valid_ref[...].astype(F32)
    for i in range(2):
        up_ref[i] = left_ref[ROWS - 2 + i]
        up_ref[2 + i] = right_ref[ROWS - 2 + i]
        down_ref[i] = left_ref[i]
        down_ref[2 + i] = right_ref[i]
    up_ref[4] = meta_block(gt, valid, ROWS - 2, 2, 0).astype(BF16)
    down_ref[4] = meta_block(gt, valid, 0, 2, ROWS + 2).astype(BF16)


def position():
    index = lax.axis_index("wa")
    return lax.shift_right_logical(index, 1), index & 1


def pack_kernel(left_ref, right_ref, gt_ref, valid_ref, prev_ref, next_ref, *refs):
    outs, ext = refs[:CHIPS], refs[CHIPS]
    chip, _ = position()
    gt = gt_ref[...].astype(F32)
    valid = valid_ref[...].astype(F32)
    meta = meta_block(gt, valid, 0, ROWS, 2)
    meta = (meta + prev_ref[4].astype(F32) + next_ref[4].astype(F32)).astype(BF16)
    for side, ref in ((0, left_ref), (1, right_ref)):
        for i in range(2):
            ext[12 * side + i] = prev_ref[2 * side + i]
            ext[12 * side + ROWS + 2 + i] = next_ref[2 * side + i]
        for i in range(ROWS):
            ext[12 * side + 2 + i] = ref[i]
    for hop in range(CHIPS):
        first = 2 * ((chip + hop) & (CHIPS - 1))
        for i in range(6):
            outs[hop][i] = ext[first + i]
            outs[hop][6 + i] = ext[first + 12 + i]
        outs[hop][12] = meta


def split3(value):
    high = value.astype(BF16)
    rest = value - high.astype(F32)
    middle = rest.astype(BF16)
    low = (rest - middle.astype(F32)).astype(BF16)
    return high, middle, low


def fill(refs, first, count, ls, rs, rb):
    chip, core = position()
    tiles = []
    for hop in range(CHIPS):
        tile = 2 * ((chip - hop) & (CHIPS - 1))
        tiles.append((refs[hop], pl.multiple_of(8 + TILE * (tile + core), 8)))
        tiles.append((refs[CHIPS + hop], pl.multiple_of(8 + TILE * (tile + 1 - core), 8)))

    @pl.loop(first, first + count)
    def row(rho):
        ls[rho, 0:8] = jnp.zeros((8, CH), F32)
        ls[rho, 8 + WT :] = jnp.zeros((8, CH), F32)
        rs[rho, 0:8] = jnp.zeros((8, CH), F32)
        rs[rho, 8 + WT :] = jnp.zeros((72, CH), F32)
        for ref, at in tiles:
            ls[rho, pl.ds(at, TILE)] = ref[core + rho].astype(F32)
            rs[rho, pl.ds(at, TILE)] = ref[6 + core + rho].astype(F32)
        for si in range(5):
            rb[rho, :, si * CH : (si + 1) * CH] = rs[rho, 4 + si : 4 + si + JP].astype(BF16)

    return tiles


def fill_meta(tiles, ms):
    for ref, at in tiles:
        ms[pl.ds(at - 8, TILE)] = ref[12].astype(F32)


def row_gradient(q, wc_ref, ls, rs, rb, ab, ms):
    lane = lax.broadcasted_iota(jnp.int32, (WT, CH), 1)
    ww = lax.broadcasted_iota(jnp.int32, (WT, JP), 0)
    jj = lax.broadcasted_iota(jnp.int32, (WT, JP), 1)
    level = (ww - jj + 2).astype(F32)
    inside = (jj <= ww + 2) & (jj >= ww - (WT - 3))
    on_diag = jj == ww + 2
    wcol = lax.broadcasted_iota(jnp.int32, (WT, 1), 0).astype(F32)
    zeros_count = jnp.maximum(float(WT - 3) - wcol, 0.0)
    zeros_mean = (wcol + float(WT + 2)) * 0.5
    acc = None
    diag = jnp.zeros((WT, CH), F32)
    for a in range(3):
        rho = q + a
        shifted = [ls[rho, 7 + b : 7 + b + WT] for b in range(3)]
        for si in range(5):
            value = None
            for b in range(3):
                e = b - (si - 2)
                if 0 <= e <= 2:
                    term = wc_ref[a, 3 * b + e : 3 * b + e + 1] * shifted[b]
                    value = term if value is None else value + term
            for i, part in enumerate(split3(value)):
                ab[i * WT : (i + 1) * WT, (a * 5 + si) * CH : (a * 5 + si + 1) * CH] = part
        for b in range(3):
            diag = diag + wc_ref[a, 3 * b : 3 * b + 1] * shifted[b] * rs[rho, 8 + b : 8 + b + WT]
        part = dot(ab[:, a * 5 * CH : (a + 1) * 5 * CH], rb[rho], NT)
        acc = part if acc is None else acc + part
    diag_col = jnp.sum(diag, axis=1, keepdims=True)
    logits = acc[0:WT] + acc[WT : 2 * WT] + acc[2 * WT : 3 * WT]
    logits = logits - jnp.where(on_diag, diag_col, 0.0)
    top = jnp.max(jnp.where(inside, logits, -3e38), axis=1, keepdims=True)
    top = jnp.where(zeros_count > 0.0, jnp.maximum(top, 0.0), top)
    expd = jnp.where(inside, jnp.exp(logits - top), 0.0)
    zero_exp = jnp.where(zeros_count > 0.0, zeros_count * jnp.exp(-top), 0.0)
    denom = jnp.sum(expd, axis=1, keepdims=True) + zero_exp
    first = jnp.sum(expd * level, axis=1, keepdims=True) + zero_exp * zeros_mean
    inv = 1.0 / denom
    estimate = first * inv
    ext = lax.axis_index("wa") + 1 + q
    meta = ms[...]
    target = jnp.sum(jnp.where(lane == GT_LANE + ext, meta, 0.0), axis=1, keepdims=True)
    valid = jnp.sum(jnp.where(lane == VALID_LANE + ext, meta, 0.0), axis=1, keepdims=True)
    usable = jnp.where(target <= wcol, valid, 0.0)
    resid = estimate - target
    factor = jnp.clip(resid, -1.0, 1.0) * usable * inv
    up = expd * (level - estimate) * factor
    up_diag = jnp.sum(jnp.where(on_diag, up, 0.0), axis=1, keepdims=True)
    return up, up_diag, resid, usable


def split2(value):
    high = value.astype(BF16)
    return high, (value - high.astype(F32)).astype(BF16)


def sums_kernel(*refs):
    recv, (wc_ref, out_ref, ls, rs, rb, ab, ms, ub, ks) = refs[:8], refs[8:]
    fill_meta(fill(recv, 1, 3, ls, rs, rb), ms)
    ks[...] = jnp.zeros(ks.shape, F32)
    up, up_diag, resid, usable = row_gradient(1, wc_ref, ls, rs, rb, ab, ms)
    size = jnp.abs(resid)
    smooth = jnp.where(size < 1.0, 0.5 * resid * resid, size - 0.5)
    loss_sum = jnp.sum(usable * smooth, axis=0, keepdims=True)
    count_sum = jnp.sum(usable, axis=0, keepdims=True)
    ub[0:WT], ub[WT : 2 * WT] = split2(up)
    for a in range(3):
        terms = dot(ub[...], rb[1 + a])
        terms = terms[0:WT] + terms[WT : 2 * WT]
        for b in range(3):
            left = ls[1 + a, 7 + b : 7 + b + WT]
            for e in range(3):
                si = b - e + 2
                value = terms[:, si * CH : (si + 1) * CH]
                if e == 0:
                    value = value - up_diag * rs[1 + a, 8 + b : 8 + b + WT]
                at = 16 * a + 3 * b + e
                ks[at : at + 1] = jnp.sum(left * value, axis=0, keepdims=True)
    group = lax.broadcasted_iota(jnp.int32, (8, CH), 0)
    channel = lax.broadcasted_iota(jnp.int32, (8, CH), 1)
    member = (channel // 16 == group).astype(F32)
    sums = dot(member, ks[...], NT, precision=lax.Precision.HIGHEST) * (1.0 / 16.0)
    sums = jnp.where(channel == LOSS_LANE, loss_sum, sums)
    sums = jnp.where(channel == COUNT_LANE, count_sum, sums)
    for i in range(out_ref.shape[0]):
        out_ref[i] = sums


def grads_kernel(*refs):
    recv, (wc_ref, out_ref, ls, rs, rb, ab, ms, ub, utb, lb, xs, ys, zs) = refs[:8], refs[8:]
    fill_meta(fill(recv, 0, 5, ls, rs, rb), ms)
    xs[...] = jnp.zeros(xs.shape, F32)
    ys[...] = jnp.zeros(ys.shape, F32)
    zs[...] = jnp.zeros(zs.shape, F32)
    lb[WT:] = jnp.zeros((JP - WT, 3 * CH), BF16)
    for b in range(3):
        lb[0:WT, b * CH : (b + 1) * CH] = ls[2, 7 + b : 7 + b + WT].astype(BF16)

    @pl.loop(0, 3)
    def step(q):
        up, up_diag, _, _ = row_gradient(q, wc_ref, ls, rs, rb, ab, ms)
        ub[0:WT], ub[WT : 2 * WT] = split2(up)
        flipped = jnp.concatenate([up, jnp.zeros((JP - WT, JP), F32)], axis=0).T
        utb[0:JP], utb[JP : 2 * JP] = split2(flipped)
        left_terms = dot(ub[...], rb[2])
        left_terms = left_terms[0:WT] + left_terms[WT : 2 * WT]
        right_terms = dot(utb[...], lb[...])
        right_terms = right_terms[0:JP] + right_terms[JP : 2 * JP]
        a = 2 - q
        taps = [[wc_ref[a, 3 * b + e : 3 * b + e + 1] for e in range(3)] for b in range(3)]
        for b in range(3):
            total = -taps[b][0] * up_diag * rs[2, 8 + b : 8 + b + WT]
            for e in range(3):
                si = b - e + 2
                total = total + taps[b][e] * left_terms[:, si * CH : (si + 1) * CH]
            xs[b, 8 : 8 + WT] += total
            zs[b, 8 : 8 + WT] += taps[b][0] * up_diag * ls[2, 7 + b : 7 + b + WT]
        for si in range(5):
            total = None
            for b in range(3):
                e = b - (si - 2)
                if 0 <= e <= 2:
                    term = taps[b][e] * right_terms[:, b * CH : (b + 1) * CH]
                    total = term if total is None else total + term
            ys[si] += total

    grad_left = xs[0, 9 : 9 + WT] + xs[1, 8 : 8 + WT] + xs[2, 7 : 7 + WT]
    grad_right = ys[0, 4 : 4 + WT]
    for si in range(1, 5):
        grad_right = grad_right + ys[si, 4 - si : 4 - si + WT]
    for b in range(3):
        grad_right = grad_right - zs[b, 8 - b : 8 - b + WT]
    for dst in range(WA):
        out_ref[dst, 0] = grad_left[TILE * dst : TILE * (dst + 1)].astype(BF16)
        out_ref[dst, 1] = grad_right[TILE * dst : TILE * (dst + 1)].astype(BF16)


def payload_kernel(grads_ref, sums_ref, out_ref):
    total = sums_ref[0]
    for i in range(1, sums_ref.shape[0]):
        total = total + sums_ref[i]
    parts = [part.astype(F32) for part in split3(total)]
    packed = jnp.concatenate(parts, axis=0).astype(BF16)
    for dst in range(WA):
        out_ref[dst, 0] = grads_ref[dst, 0]
        out_ref[dst, 1] = grads_ref[dst, 1]
        out_ref[dst, 2] = packed


def finish_kernel(recv_ref, left_ref, right_ref, weight_ref, loss_ref):
    total = recv_ref[0, 2].astype(F32)
    for src in range(1, WA):
        total = total + recv_ref[src, 2].astype(F32)
    total = total[0:8] + total[8:16] + total[16:24]
    norm = 1.0 / jnp.maximum(total[0:1, COUNT_LANE : COUNT_LANE + 1], 1.0)
    for src in range(WA):
        left_ref[src] = recv_ref[src, 0].astype(F32) * norm
        right_ref[src] = recv_ref[src, 1].astype(F32) * norm
    loss_ref[...] = total[0:1, LOSS_LANE : LOSS_LANE + 1] * norm
    by_tap = jnp.concatenate([total * norm, jnp.zeros((CH - 8, CH), F32)], axis=0).T
    for a in range(3):
        for b in range(3):
            at = 16 * a + 3 * b
            weight_ref[a, b] = by_tap[at : at + 3, 0:8]


def call(kernel, out_shape, *args, scratch=(), flops=0, params=VMEM):
    cost = pl.CostEstimate(flops=flops, bytes_accessed=1 << 20, transcendentals=0)
    return pl.pallas_call(
        kernel, out_shape=out_shape, scratch_shapes=list(scratch), compiler_params=params, cost_estimate=cost
    )(*args)


def shards(left_feat, right_feat, conv_weight, disparity_gt, valid_mask):
    left, right = left_feat[0], right_feat[0]
    gt, valid = disparity_gt[0], valid_mask[0]
    ha_count = lax.axis_size("ha")
    halo = jax.ShapeDtypeStruct((5, TILE, CH), BF16)
    up, down = call(halo_kernel, (halo, halo), left, right, gt, valid, params=FIRST)
    before = lax.ppermute(up, "ha", [(i, i + 1) for i in range(ha_count - 1)])
    after = lax.ppermute(down, "ha", [(i + 1, i) for i in range(ha_count - 1)])
    taps = jnp.repeat(conv_weight.reshape(8, 27).T, 16, axis=1) * (1.0 / 16.0)
    taps = jnp.pad(taps.reshape(3, 9, CH), ((0, 0), (0, 7), (0, 0)))
    block = jax.ShapeDtypeStruct((13, TILE, CH), BF16)
    blocks = call(
        pack_kernel,
        (block,) * CHIPS,
        left,
        right,
        gt,
        valid,
        before,
        after,
        scratch=(pltpu.VMEM((24, TILE, CH), BF16),),
    )
    same_core = [blocks[0]]
    for hop in range(1, CHIPS):
        same_core.append(lax.ppermute(blocks[hop], "wa", [(i, (i + 2 * hop) % WA) for i in range(WA)]))
    other_core = [lax.ppermute(value, "wa", [(i, i ^ 1) for i in range(WA)]) for value in same_core]
    tiles = same_core + other_core
    shared = (
        pltpu.VMEM((5, WT + 16, CH), F32),
        pltpu.VMEM((5, WT + 80, CH), F32),
        pltpu.VMEM((5, JP, 5 * CH), BF16),
        pltpu.VMEM((3 * WT, 15 * CH), BF16),
        pltpu.VMEM((WT, CH), F32),
        pltpu.VMEM((2 * WT, JP), BF16),
    )
    others = lax.axis_size("dp") * ha_count
    sums = call(
        sums_kernel,
        jax.ShapeDtypeStruct((others, 8, CH), F32),
        *tiles,
        taps,
        scratch=shared + (pltpu.VMEM((CH, CH), F32),),
        flops=1 << 30,
    )
    sums = lax.all_to_all(sums, ("dp", "ha"), 0, 0, tiled=True)
    grads = call(
        grads_kernel,
        jax.ShapeDtypeStruct((WA, 2, TILE, CH), BF16),
        *tiles,
        taps,
        scratch=shared
        + (
            pltpu.VMEM((2 * JP, JP), BF16),
            pltpu.VMEM((JP, 3 * CH), BF16),
            pltpu.VMEM((3, WT + 16, CH), F32),
            pltpu.VMEM((5, JP, CH), F32),
            pltpu.VMEM((3, WT + 16, CH), F32),
        ),
        flops=5 << 30,
    )
    payload = call(payload_kernel, jax.ShapeDtypeStruct((WA, 3, TILE, CH), BF16), grads, sums)
    back = lax.all_to_all(payload, "wa", 0, 0, tiled=True)
    tile = jax.ShapeDtypeStruct((ROWS, TILE, CH), F32)
    grad_left, grad_right, weight, loss = call(
        finish_kernel,
        (tile, tile, jax.ShapeDtypeStruct((3, 3, 3, 8), F32), jax.ShapeDtypeStruct((1, 1), F32)),
        back,
    )
    return (loss[0, 0], grad_left[None], grad_right[None], jnp.transpose(weight, (3, 0, 1, 2)))


def solution(mesh):
    placed = (
        P("dp", "ha", "wa", None),
        P("dp", "ha", "wa", None),
        P(),
        P("dp", "ha", "wa"),
        P("dp", "ha", "wa"),
    )
    return jax.shard_map(
        shards,
        mesh=mesh,
        in_specs=placed,
        out_specs=(P(), P("dp", "ha", "wa", None), P("dp", "ha", "wa", None), P()),
        check_vma=False,
    )
```

```python
import jax
import jax.numpy as jnp
from jax import lax
from jax.experimental import pallas as pl
from jax.experimental.pallas import tpu as pltpu
from jax.sharding import PartitionSpec as P

F32 = jnp.float32
BF16 = jnp.bfloat16
ROWS, TILE, CH = 8, 24, 128
WA, CHIPS = 8, 4
WT = 192
JP = 256
GT_LANE, VALID_LANE = 0, 16
LOSS_LANE, COUNT_LANE = 9, 10
VMEM = pltpu.CompilerParams(vmem_limit_bytes=48 * 1024 * 1024)
FIRST = pltpu.CompilerParams(vmem_limit_bytes=60 * 1024 * 1024)
NT = (((1,), (1,)), ((), ()))
NN = (((1,), (0,)), ((), ()))
TN = (((0,), (0,)), ((), ()))


def dot(lhs, rhs, dims=NN, precision=None):
    return lax.dot_general(lhs, rhs, dims, precision=precision, preferred_element_type=F32)


def meta_block(gt, valid, first, count, lane_of_first):
    row = lax.broadcasted_iota(jnp.int32, (ROWS, CH), 0)
    lane = lax.broadcasted_iota(jnp.int32, (ROWS, CH), 1)
    chosen = (row >= first) & (row < first + count)
    at = row - first + lane_of_first
    pick_gt = (chosen & (lane == at + GT_LANE)).astype(F32)
    pick_valid = (chosen & (lane == at + VALID_LANE)).astype(F32)
    return dot(gt, pick_gt, TN) + dot(valid, pick_valid, TN)


def halo_kernel(left_ref, right_ref, gt_ref, valid_ref, up_ref, down_ref):
    gt = gt_ref[...].astype(F32)
    valid = valid_ref[...].astype(F32)
    for i in range(2):
        up_ref[i] = left_ref[ROWS - 2 + i]
        up_ref[2 + i] = right_ref[ROWS - 2 + i]
        down_ref[i] = left_ref[i]
        down_ref[2 + i] = right_ref[i]
    up_ref[4] = meta_block(gt, valid, ROWS - 2, 2, 0).astype(BF16)
    down_ref[4] = meta_block(gt, valid, 0, 2, ROWS + 2).astype(BF16)


def position():
    index = lax.axis_index("wa")
    return lax.shift_right_logical(index, 1), index & 1


def pack_kernel(left_ref, right_ref, gt_ref, valid_ref, prev_ref, next_ref, *refs):
    outs, ext = refs[:CHIPS], refs[CHIPS]
    chip, _ = position()
    band = lax.axis_index("ha")
    has_prev = band > 0
    has_next = band < lax.axis_size("ha") - 1

    def of_prev(i):
        return jnp.where(has_prev, prev_ref[i], jnp.zeros((TILE, CH), BF16))

    def of_next(i):
        return jnp.where(has_next, next_ref[i], jnp.zeros((TILE, CH), BF16))

    gt = gt_ref[...].astype(F32)
    valid = valid_ref[...].astype(F32)
    meta = meta_block(gt, valid, 0, ROWS, 2)
    meta = (meta + of_prev(4).astype(F32) + of_next(4).astype(F32)).astype(BF16)
    for side, ref in ((0, left_ref), (1, right_ref)):
        for i in range(2):
            ext[12 * side + i] = of_prev(2 * side + i)
            ext[12 * side + ROWS + 2 + i] = of_next(2 * side + i)
        for i in range(ROWS):
            ext[12 * side + 2 + i] = ref[i]
    for hop in range(CHIPS):
        first = 2 * ((chip + hop) & (CHIPS - 1))
        for i in range(6):
            outs[hop][i] = ext[first + i]
            outs[hop][6 + i] = ext[first + 12 + i]
        outs[hop][12] = meta


def split3(value):
    high = value.astype(BF16)
    rest = value - high.astype(F32)
    middle = rest.astype(BF16)
    low = (rest - middle.astype(F32)).astype(BF16)
    return high, middle, low


def fill(refs, first, count, ls, rs, rb):
    chip, core = position()
    tiles = []
    for hop in range(CHIPS):
        tile = 2 * ((chip - hop) & (CHIPS - 1))
        tiles.append((refs[hop], pl.multiple_of(8 + TILE * (tile + core), 8)))
        tiles.append((refs[CHIPS + hop], pl.multiple_of(8 + TILE * (tile + 1 - core), 8)))

    @pl.loop(first, first + count)
    def row(rho):
        ls[rho, 0:8] = jnp.zeros((8, CH), F32)
        ls[rho, 8 + WT :] = jnp.zeros((8, CH), F32)
        rs[rho, 0:8] = jnp.zeros((8, CH), F32)
        rs[rho, 8 + WT :] = jnp.zeros((72, CH), F32)
        for ref, at in tiles:
            ls[rho, pl.ds(at, TILE)] = ref[core + rho].astype(F32)
            rs[rho, pl.ds(at, TILE)] = ref[6 + core + rho].astype(F32)
        for si in range(5):
            rb[:, pl.ds(pl.multiple_of((5 * rho + si) * CH, CH), CH)] = rs[rho, 4 + si : 4 + si + JP].astype(BF16)

    return tiles


def fill_meta(tiles, ms):
    for ref, at in tiles:
        ms[pl.ds(at - 8, TILE)] = ref[12].astype(F32)


def split2(value):
    high = value.astype(BF16)
    return high, (value - high.astype(F32)).astype(BF16)


def weighted(a, left, wc_ref, ab):
    for si in range(5):
        value = None
        for b in range(3):
            e = b - (si - 2)
            if 0 <= e <= 2:
                term = wc_ref[a, 3 * b + e : 3 * b + e + 1] * left[b]
                value = term if value is None else value + term
        for i, part in enumerate(split3(value)):
            ab[i * WT : (i + 1) * WT, (5 * a + si) * CH : (5 * a + si + 1) * CH] = part


def row_gradient(q, logits, diag_col, ms, masks):
    lane, level, inside, on_diag, wcol, zeros_count, zeros_mean = masks
    logits = logits - jnp.where(on_diag, diag_col, 0.0)
    top = jnp.max(jnp.where(inside, logits, -3e38), axis=1, keepdims=True)
    top = jnp.where(zeros_count > 0.0, jnp.maximum(top, 0.0), top)
    expd = jnp.where(inside, jnp.exp(logits - top), 0.0)
    zero_exp = jnp.where(zeros_count > 0.0, zeros_count * jnp.exp(-top), 0.0)
    denom = jnp.sum(expd, axis=1, keepdims=True) + zero_exp
    first = jnp.sum(expd * level, axis=1, keepdims=True) + zero_exp * zeros_mean
    inv = 1.0 / denom
    estimate = first * inv
    ext = lax.axis_index("wa") + 1 + q
    meta = ms[...]
    target = jnp.sum(jnp.where(lane == GT_LANE + ext, meta, 0.0), axis=1, keepdims=True)
    valid = jnp.sum(jnp.where(lane == VALID_LANE + ext, meta, 0.0), axis=1, keepdims=True)
    usable = jnp.where(target <= wcol, valid, 0.0)
    resid = estimate - target
    factor = jnp.clip(resid, -1.0, 1.0) * usable * inv
    return expd * (level - estimate) * factor, resid, usable


def diagonal(up, on_diag):
    return jnp.sum(jnp.where(on_diag, up, 0.0), axis=1, keepdims=True)


def row_masks():
    lane = lax.broadcasted_iota(jnp.int32, (WT, CH), 1)
    ww = lax.broadcasted_iota(jnp.int32, (WT, JP), 0)
    jj = lax.broadcasted_iota(jnp.int32, (WT, JP), 1)
    level = (ww - jj + 2).astype(F32)
    inside = (jj <= ww + 2) & (jj >= ww - (WT - 3))
    on_diag = jj == ww + 2
    wcol = lax.broadcasted_iota(jnp.int32, (WT, 1), 0).astype(F32)
    zeros_count = jnp.maximum(float(WT - 3) - wcol, 0.0)
    zeros_mean = (wcol + float(WT + 2)) * 0.5
    return lane, level, inside, on_diag, wcol, zeros_count, zeros_mean


def forward(q, ls, rs, rb, wc_ref, ab, ms):
    masks = row_masks()
    diag = None
    for a in range(3):
        left = [ls[q + a, 7 + b : 7 + b + WT] for b in range(3)]
        weighted(a, left, wc_ref, ab)
        for b in range(3):
            term = wc_ref[a, 3 * b : 3 * b + 1] * left[b] * rs[q + a, 8 + b : 8 + b + WT]
            diag = term if diag is None else diag + term
    parts = dot(ab[...], rb[:, 5 * q * CH : (5 * q + 15) * CH], NT)
    logits = parts[0:WT] + parts[WT : 2 * WT] + parts[2 * WT : 3 * WT]
    up, resid, usable = row_gradient(q, logits, jnp.sum(diag, axis=1, keepdims=True), ms, masks)
    return up, diagonal(up, masks[3]), resid, usable


def own_kernel(*refs):
    recv, wc_ref = refs[:8], refs[8]
    sums_ref, ub, diag_ref, ls, rs, rb, ms, ab, ks = refs[9:]
    fill_meta(fill(recv, 1, 3, ls, rs, rb), ms)
    ks[...] = jnp.zeros(ks.shape, F32)
    up, up_diag, resid, usable = forward(1, ls, rs, rb, wc_ref, ab, ms)
    ub[0:WT], ub[WT : 2 * WT] = split2(up)
    diag_ref[...] = jnp.broadcast_to(up_diag, (WT, CH))
    size = jnp.abs(resid)
    smooth = jnp.where(size < 1.0, 0.5 * resid * resid, size - 0.5)
    loss_sum = jnp.sum(usable * smooth, axis=0, keepdims=True)
    count_sum = jnp.sum(usable, axis=0, keepdims=True)
    for a in range(3):
        terms = dot(ub[...], rb[:, 5 * (1 + a) * CH : 5 * (2 + a) * CH])
        terms = terms[0:WT] + terms[WT : 2 * WT]
        for b in range(3):
            left = ls[1 + a, 7 + b : 7 + b + WT]
            for e in range(3):
                si = b - e + 2
                value = terms[:, si * CH : (si + 1) * CH]
                if e == 0:
                    value = value - up_diag * rs[1 + a, 8 + b : 8 + b + WT]
                at = 16 * a + 3 * b + e
                ks[at : at + 1] = jnp.sum(left * value, axis=0, keepdims=True)
    channel = lax.broadcasted_iota(jnp.int32, (8, CH), 1)
    group = lax.broadcasted_iota(jnp.int32, (8, CH), 0)
    member = (lax.shift_right_logical(channel, 4) == group).astype(F32)
    sums = dot(member, ks[...], NT, precision=lax.Precision.HIGHEST) * (1.0 / 16.0)
    sums = jnp.where(channel == LOSS_LANE, loss_sum, sums)
    sums = jnp.where(channel == COUNT_LANE, count_sum, sums)
    for i in range(sums_ref.shape[0]):
        sums_ref[i] = sums


def rest_kernel(*refs):
    recv, (wc_ref, own_ub, own_diag, out_ref) = refs[:8], refs[8:12]
    ls, rs, rb, ms, ab, ub, diags, lb, xs, ys = refs[12:]
    fill_meta(fill(recv, 0, 5, ls, rs, rb), ms)
    xs[...] = jnp.zeros(xs.shape, F32)
    for q in (0, 2):
        up, up_diag, _, _ = forward(q, ls, rs, rb, wc_ref, ab, ms)
        ub[2 * WT * q : 2 * WT * q + WT], ub[2 * WT * q + WT : 2 * WT * (q + 1)] = split2(up)
        diags[q] = jnp.broadcast_to(up_diag, (WT, CH))
    ub[2 * WT : 4 * WT] = own_ub[...]
    diags[1] = own_diag[...]
    for b in range(3):
        shifted = ls[2, 7 + b : 7 + b + WT].astype(BF16)
        lb[0:WT, b * CH : (b + 1) * CH] = shifted
        lb[WT:, b * CH : (b + 1) * CH] = shifted

    def tap(q, b, e):
        return wc_ref[2 - q, 3 * b + e : 3 * b + e + 1]

    terms = dot(ub[...], rb[:, 10 * CH : 15 * CH])
    for b in range(3):
        total = None
        spread = None
        for q in range(3):
            term = tap(q, b, 0) * diags[q]
            spread = term if spread is None else spread + term
            for e in range(3):
                at, si = 2 * WT * q, b - e + 2
                value = terms[at : at + WT, si * CH : (si + 1) * CH]
                value = value + terms[at + WT : at + 2 * WT, si * CH : (si + 1) * CH]
                term = tap(q, b, e) * value
                total = term if total is None else total + term
        xs[b, 8 : 8 + WT] = total - spread * rs[2, 8 + b : 8 + b + WT]
        xs[3 + b, 8 : 8 + WT] = spread * ls[2, 7 + b : 7 + b + WT]
    for q in range(3):
        terms = dot(ub[2 * WT * q : 2 * WT * (q + 1)], lb[...], TN)
        for si in range(5):
            total = None
            for b in range(3):
                e = b - (si - 2)
                if 0 <= e <= 2:
                    term = tap(q, b, e) * terms[:, b * CH : (b + 1) * CH]
                    total = term if total is None else total + term
            ys[si] = total if q == 0 else ys[si] + total
    grad_left = xs[0, 9 : 9 + WT] + xs[1, 8 : 8 + WT] + xs[2, 7 : 7 + WT]
    grad_right = ys[0, 4 : 4 + WT]
    for si in range(1, 5):
        grad_right = grad_right + ys[si, 4 - si : 4 - si + WT]
    for b in range(3):
        grad_right = grad_right - xs[3 + b, 8 - b : 8 - b + WT]
    for dst in range(WA):
        out_ref[dst, 0] = grad_left[TILE * dst : TILE * (dst + 1)].astype(BF16)
        out_ref[dst, 1] = grad_right[TILE * dst : TILE * (dst + 1)].astype(BF16)


def payload_kernel(grads_ref, sums_ref, out_ref):
    total = sums_ref[0]
    for i in range(1, sums_ref.shape[0]):
        total = total + sums_ref[i]
    parts = jnp.concatenate([part.astype(F32) for part in split3(total)], axis=0).astype(BF16)
    for dst in range(WA):
        out_ref[dst, 0] = grads_ref[dst, 0]
        out_ref[dst, 1] = grads_ref[dst, 1]
        out_ref[dst, 2] = parts


def finish_kernel(recv_ref, left_ref, right_ref, weight_ref, loss_ref):
    total = recv_ref[0, 2].astype(F32)
    for src in range(1, WA):
        total = total + recv_ref[src, 2].astype(F32)
    total = total[0:8] + total[8:16] + total[16:24]
    norm = 1.0 / jnp.maximum(total[0:1, COUNT_LANE : COUNT_LANE + 1], 1.0)
    for src in range(WA):
        left_ref[src] = recv_ref[src, 0].astype(F32) * norm
        right_ref[src] = recv_ref[src, 1].astype(F32) * norm
    loss_ref[...] = total[0:1, LOSS_LANE : LOSS_LANE + 1] * norm
    by_tap = jnp.concatenate([total * norm, jnp.zeros((CH - 8, CH), F32)], axis=0).T
    for a in range(3):
        for b in range(3):
            at = 16 * a + 3 * b
            weight_ref[a, b] = by_tap[at : at + 3, 0:8]


def call(kernel, out_shape, *args, scratch=(), flops=0, params=VMEM):
    cost = pl.CostEstimate(flops=flops, bytes_accessed=1 << 20, transcendentals=0)
    return pl.pallas_call(
        kernel, out_shape=out_shape, scratch_shapes=list(scratch), compiler_params=params, cost_estimate=cost
    )(*args)


def shards(left_feat, right_feat, conv_weight, disparity_gt, valid_mask):
    left, right = left_feat[0], right_feat[0]
    gt, valid = disparity_gt[0], valid_mask[0]
    ha_count = lax.axis_size("ha")
    halo = jax.ShapeDtypeStruct((5, TILE, CH), BF16)
    up, down = call(halo_kernel, (halo, halo), left, right, gt, valid, params=FIRST)
    before = lax.ppermute(up, "ha", [(i, (i + 1) % ha_count) for i in range(ha_count)])
    after = lax.ppermute(down, "ha", [((i + 1) % ha_count, i) for i in range(ha_count)])
    taps = jnp.repeat(conv_weight.reshape(8, 27).T, 16, axis=1) * (1.0 / 16.0)
    taps = jnp.pad(taps.reshape(3, 9, CH), ((0, 0), (0, 7), (0, 0)))
    block = jax.ShapeDtypeStruct((13, TILE, CH), BF16)
    blocks = call(
        pack_kernel,
        (block,) * CHIPS,
        left,
        right,
        gt,
        valid,
        before,
        after,
        scratch=(pltpu.VMEM((24, TILE, CH), BF16),),
    )
    same_core = [blocks[0]]
    for hop in range(1, CHIPS):
        same_core.append(lax.ppermute(blocks[hop], "wa", [(i, (i + 2 * hop) % WA) for i in range(WA)]))
    other_core = [lax.ppermute(value, "wa", [(i, i ^ 1) for i in range(WA)]) for value in same_core]
    tiles = same_core + other_core
    others = lax.axis_size("dp") * ha_count
    rows = (
        pltpu.VMEM((5, WT + 16, CH), F32),
        pltpu.VMEM((5, WT + 80, CH), F32),
        pltpu.VMEM((JP, 25 * CH), BF16),
        pltpu.VMEM((WT, CH), F32),
        pltpu.VMEM((3 * WT, 15 * CH), BF16),
    )
    sums, own_ub, own_diag = call(
        own_kernel,
        (
            jax.ShapeDtypeStruct((others, 8, CH), F32),
            jax.ShapeDtypeStruct((2 * WT, JP), BF16),
            jax.ShapeDtypeStruct((WT, CH), F32),
        ),
        *tiles,
        taps,
        scratch=rows + (pltpu.VMEM((CH, CH), F32),),
        flops=2 << 30,
    )
    sums = lax.all_to_all(sums, ("dp", "ha"), 0, 0, tiled=True)
    grads = call(
        rest_kernel,
        jax.ShapeDtypeStruct((WA, 2, TILE, CH), BF16),
        *tiles,
        taps,
        own_ub,
        own_diag,
        scratch=rows
        + (
            pltpu.VMEM((6 * WT, JP), BF16),
            pltpu.VMEM((3, WT, CH), F32),
            pltpu.VMEM((2 * WT, 3 * CH), BF16),
            pltpu.VMEM((6, WT + 16, CH), F32),
            pltpu.VMEM((5, JP, CH), F32),
        ),
        flops=3 << 30,
    )
    payload = call(payload_kernel, jax.ShapeDtypeStruct((WA, 3, TILE, CH), BF16), grads, sums)
    back = lax.all_to_all(payload, "wa", 0, 0, tiled=True)
    tile = jax.ShapeDtypeStruct((ROWS, TILE, CH), F32)
    grad_left, grad_right, weight, loss = call(
        finish_kernel,
        (tile, tile, jax.ShapeDtypeStruct((3, 3, 3, 8), F32), jax.ShapeDtypeStruct((1, 1), F32)),
        back,
    )
    return (loss[0, 0], grad_left[None], grad_right[None], jnp.transpose(weight, (3, 0, 1, 2)))


def solution(mesh):
    placed = (
        P("dp", "ha", "wa", None),
        P("dp", "ha", "wa", None),
        P(),
        P("dp", "ha", "wa"),
        P("dp", "ha", "wa"),
    )
    return jax.shard_map(
        shards,
        mesh=mesh,
        in_specs=placed,
        out_specs=(P(), P("dp", "ha", "wa", None), P("dp", "ha", "wa", None), P()),
        check_vma=False,
    )
```

```python
import jax
import jax.numpy as jnp
from jax import lax
from jax.experimental import pallas as pl
from jax.experimental.pallas import tpu as pltpu
from jax.sharding import PartitionSpec as P

F32 = jnp.float32
BF16 = jnp.bfloat16
ROWS, TILE, CH = 8, 24, 128
WA, CHIPS = 8, 4
WT = 192
JP = 256
GT_LANE, VALID_LANE = 0, 16
LOSS_LANE, COUNT_LANE, THIRD = 27, 28, 32
VMEM = pltpu.CompilerParams(vmem_limit_bytes=48 * 1024 * 1024)
NT = (((1,), (1,)), ((), ()))
NN = (((1,), (0,)), ((), ()))
TN = (((0,), (0,)), ((), ()))


def dot(lhs, rhs, dims=NN, precision=None):
    return lax.dot_general(lhs, rhs, dims, precision=precision, preferred_element_type=F32)


def meta_block(gt, valid, first, count, lane_of_first):
    row = lax.broadcasted_iota(jnp.int32, (ROWS, CH), 0)
    lane = lax.broadcasted_iota(jnp.int32, (ROWS, CH), 1)
    chosen = (row >= first) & (row < first + count)
    at = row - first + lane_of_first
    pick_gt = (chosen & (lane == at + GT_LANE)).astype(F32)
    pick_valid = (chosen & (lane == at + VALID_LANE)).astype(F32)
    return dot(gt, pick_gt, TN) + dot(valid, pick_valid, TN)


def halo_kernel(left_any, right_any, gt_any, valid_any, weight_any, up_ref, down_ref, own_ref, taps_ref, *scratch):
    refs, sems = scratch[:5], scratch[5]
    sources = (left_any, right_any, gt_any, valid_any, weight_any)
    copies = [pltpu.make_async_copy(src, dst, sems.at[i]) for i, (src, dst) in enumerate(zip(sources, refs))]
    for copy in copies:
        copy.start()
    for copy in copies:
        copy.wait()
    left_ref, right_ref, gt_ref, valid_ref, weight_ref = refs
    gt = gt_ref[...].astype(F32)
    valid = valid_ref[...].astype(F32)
    for side, ref in ((0, left_ref), (1, right_ref)):
        for i in range(2):
            up_ref[2 * side + i] = ref[ROWS - 2 + i]
            down_ref[2 * side + i] = ref[i]
        for i in range(ROWS):
            own_ref[ROWS * side + i] = ref[i]
    up_ref[4] = meta_block(gt, valid, ROWS - 2, 2, 0).astype(BF16)
    down_ref[4] = meta_block(gt, valid, 0, 2, ROWS + 2).astype(BF16)
    own_ref[2 * ROWS] = meta_block(gt, valid, 0, ROWS, 2).astype(BF16)
    member = group_member() * (1.0 / 16.0)
    for a in range(3):
        taps = jnp.concatenate([weight_ref[a, b] for b in range(3)], axis=0)
        taps_ref[a, 0:9] = dot(taps, member, precision=lax.Precision.HIGHEST)


def group_member():
    group = lax.broadcasted_iota(jnp.int32, (8, CH), 0)
    channel = lax.broadcasted_iota(jnp.int32, (8, CH), 1)
    return (lax.shift_right_logical(channel, 4) == group).astype(F32)


def position():
    index = lax.axis_index("wa")
    return lax.shift_right_logical(index, 1), index & 1


def pack_kernel(own_ref, prev_ref, next_ref, *refs):
    outs, ext = refs[:CHIPS], refs[CHIPS]
    chip, _ = position()
    band = lax.axis_index("ha")
    has_prev = band > 0
    has_next = band < lax.axis_size("ha") - 1

    def of_prev(i):
        return jnp.where(has_prev, prev_ref[i], jnp.zeros((TILE, CH), BF16))

    def of_next(i):
        return jnp.where(has_next, next_ref[i], jnp.zeros((TILE, CH), BF16))

    meta = own_ref[2 * ROWS].astype(F32)
    meta = (meta + of_prev(4).astype(F32) + of_next(4).astype(F32)).astype(BF16)
    for side in range(2):
        for i in range(2):
            ext[12 * side + i] = of_prev(2 * side + i)
            ext[12 * side + ROWS + 2 + i] = of_next(2 * side + i)
        for i in range(ROWS):
            ext[12 * side + 2 + i] = own_ref[ROWS * side + i]
    for hop in range(CHIPS):
        first = 2 * ((chip + hop) & (CHIPS - 1))
        for i in range(6):
            outs[hop][i] = ext[first + i]
            outs[hop][6 + i] = ext[first + 12 + i]
        outs[hop][12] = meta


def split3(value):
    high = value.astype(BF16)
    rest = value - high.astype(F32)
    middle = rest.astype(BF16)
    low = (rest - middle.astype(F32)).astype(BF16)
    return high, middle, low


def fill(refs, first, count, ls, rs, rb):
    chip, core = position()
    tiles = []
    for hop in range(CHIPS):
        tile = 2 * ((chip - hop) & (CHIPS - 1))
        tiles.append((refs[hop], pl.multiple_of(8 + TILE * (tile + core), 8)))
        tiles.append((refs[CHIPS + hop], pl.multiple_of(8 + TILE * (tile + 1 - core), 8)))

    @pl.loop(first, first + count)
    def row(rho):
        ls[rho, 0:8] = jnp.zeros((8, CH), F32)
        ls[rho, 8 + WT :] = jnp.zeros((8, CH), F32)
        rs[rho, 0:8] = jnp.zeros((8, CH), F32)
        rs[rho, 8 + WT :] = jnp.zeros((72, CH), F32)
        for ref, at in tiles:
            ls[rho, pl.ds(at, TILE)] = ref[core + rho].astype(F32)
            rs[rho, pl.ds(at, TILE)] = ref[6 + core + rho].astype(F32)
        for si in range(5):
            rb[:, pl.ds(pl.multiple_of((5 * rho + si) * CH, CH), CH)] = rs[rho, 4 + si : 4 + si + JP].astype(BF16)

    return tiles


def fill_meta(tiles, ms):
    for ref, at in tiles:
        ms[pl.ds(at - 8, TILE)] = ref[12].astype(F32)


def split2(value):
    high = value.astype(BF16)
    return high, (value - high.astype(F32)).astype(BF16)


def weighted(a, left, wc_ref, ab):
    for si in range(5):
        value = None
        for b in range(3):
            e = b - (si - 2)
            if 0 <= e <= 2:
                term = wc_ref[a, 3 * b + e : 3 * b + e + 1] * left[b]
                value = term if value is None else value + term
        for i, part in enumerate(split3(value)):
            ab[i * WT : (i + 1) * WT, (5 * a + si) * CH : (5 * a + si + 1) * CH] = part


def row_gradient(q, logits, diag_col, ms, masks):
    lane, level, inside, on_diag, wcol, zeros_count, zeros_mean = masks
    logits = logits - jnp.where(on_diag, diag_col, 0.0)
    top = jnp.max(jnp.where(inside, logits, -3e38), axis=1, keepdims=True)
    top = jnp.where(zeros_count > 0.0, jnp.maximum(top, 0.0), top)
    expd = jnp.where(inside, jnp.exp(logits - top), 0.0)
    zero_exp = jnp.where(zeros_count > 0.0, zeros_count * jnp.exp(-top), 0.0)
    denom = jnp.sum(expd, axis=1, keepdims=True) + zero_exp
    first = jnp.sum(expd * level, axis=1, keepdims=True) + zero_exp * zeros_mean
    inv = 1.0 / denom
    estimate = first * inv
    ext = lax.axis_index("wa") + 1 + q
    meta = ms[...]
    target = jnp.sum(jnp.where(lane == GT_LANE + ext, meta, 0.0), axis=1, keepdims=True)
    valid = jnp.sum(jnp.where(lane == VALID_LANE + ext, meta, 0.0), axis=1, keepdims=True)
    usable = jnp.where(target <= wcol, valid, 0.0)
    resid = estimate - target
    factor = jnp.clip(resid, -1.0, 1.0) * usable * inv
    return expd * (level - estimate) * factor, resid, usable


def diagonal(up, on_diag):
    return jnp.sum(jnp.where(on_diag, up, 0.0), axis=1, keepdims=True)


def row_masks():
    lane = lax.broadcasted_iota(jnp.int32, (WT, CH), 1)
    ww = lax.broadcasted_iota(jnp.int32, (WT, JP), 0)
    jj = lax.broadcasted_iota(jnp.int32, (WT, JP), 1)
    level = (ww - jj + 2).astype(F32)
    inside = (jj <= ww + 2) & (jj >= ww - (WT - 3))
    on_diag = jj == ww + 2
    wcol = lax.broadcasted_iota(jnp.int32, (WT, 1), 0).astype(F32)
    zeros_count = jnp.maximum(float(WT - 3) - wcol, 0.0)
    zeros_mean = (wcol + float(WT + 2)) * 0.5
    return lane, level, inside, on_diag, wcol, zeros_count, zeros_mean


def forward(q, ls, rs, rb, wc_ref, ab, ms):
    masks = row_masks()
    diag = None
    for a in range(3):
        left = [ls[q + a, 7 + b : 7 + b + WT] for b in range(3)]
        weighted(a, left, wc_ref, ab)
        for b in range(3):
            term = wc_ref[a, 3 * b : 3 * b + 1] * left[b] * rs[q + a, 8 + b : 8 + b + WT]
            diag = term if diag is None else diag + term
    parts = dot(ab[...], rb[:, 5 * q * CH : (5 * q + 15) * CH], NT)
    logits = parts[0:WT] + parts[WT : 2 * WT] + parts[2 * WT : 3 * WT]
    up, resid, usable = row_gradient(q, logits, jnp.sum(diag, axis=1, keepdims=True), ms, masks)
    return up, diagonal(up, masks[3]), resid, usable


def own_kernel(*refs):
    recv, wc_ref = refs[:8], refs[8]
    sums_ref, ub, diag_ref, ls, rs, rb, ms, ab, ks = refs[9:]
    fill_meta(fill(recv, 1, 3, ls, rs, rb), ms)
    ks[...] = jnp.zeros(ks.shape, F32)
    up, up_diag, resid, usable = forward(1, ls, rs, rb, wc_ref, ab, ms)
    ub[0:WT], ub[WT : 2 * WT] = split2(up)
    diag_ref[...] = jnp.broadcast_to(up_diag, (WT, CH))
    size = jnp.abs(resid)
    smooth = jnp.where(size < 1.0, 0.5 * resid * resid, size - 0.5)
    loss_sum = jnp.sum(usable * smooth, axis=0, keepdims=True)
    count_sum = jnp.sum(usable, axis=0, keepdims=True)
    terms = dot(ub[...], rb[:, 5 * CH : 20 * CH])
    for a in range(3):
        for b in range(3):
            left = ls[1 + a, 7 + b : 7 + b + WT]
            for e in range(3):
                si = 5 * a + b - e + 2
                value = terms[0:WT, si * CH : (si + 1) * CH] + terms[WT:, si * CH : (si + 1) * CH]
                if e == 0:
                    value = value - up_diag * rs[1 + a, 8 + b : 8 + b + WT]
                at = 9 * a + 3 * b + e
                ks[at : at + 1] = jnp.sum(left * value, axis=0, keepdims=True)
    channel = lax.broadcasted_iota(jnp.int32, (8, CH), 1)
    member = group_member().astype(BF16)
    parts = [dot(member, part, NT) for part in split3(ks[...])]
    sums = (parts[0] + (parts[1] + parts[2])) * (1.0 / 16.0)
    sums = jnp.where(channel == LOSS_LANE, loss_sum, sums)
    sums = jnp.where(channel == COUNT_LANE, count_sum, sums)
    for i in range(sums_ref.shape[0]):
        sums_ref[i] = sums


def rest_kernel(*refs):
    recv, (wc_ref, own_ub, own_diag, out_ref) = refs[:8], refs[8:12]
    ls, rs, rb, ms, ab, ub, diags, lb, xs, ys = refs[12:]
    fill_meta(fill(recv, 0, 5, ls, rs, rb), ms)
    xs[...] = jnp.zeros(xs.shape, F32)
    for q in (0, 2):
        up, up_diag, _, _ = forward(q, ls, rs, rb, wc_ref, ab, ms)
        ub[2 * WT * q : 2 * WT * q + WT], ub[2 * WT * q + WT : 2 * WT * (q + 1)] = split2(up)
        diags[q] = jnp.broadcast_to(up_diag, (WT, CH))
    ub[2 * WT : 4 * WT] = own_ub[...]
    diags[1] = own_diag[...]
    for b in range(3):
        shifted = ls[2, 7 + b : 7 + b + WT].astype(BF16)
        lb[0:WT, b * CH : (b + 1) * CH] = shifted
        lb[WT:, b * CH : (b + 1) * CH] = shifted

    def tap(q, b, e):
        return wc_ref[2 - q, 3 * b + e : 3 * b + e + 1]

    terms = dot(ub[...], rb[:, 10 * CH : 15 * CH])
    for b in range(3):
        total = None
        spread = None
        for q in range(3):
            term = tap(q, b, 0) * diags[q]
            spread = term if spread is None else spread + term
            for e in range(3):
                at, si = 2 * WT * q, b - e + 2
                value = terms[at : at + WT, si * CH : (si + 1) * CH]
                value = value + terms[at + WT : at + 2 * WT, si * CH : (si + 1) * CH]
                term = tap(q, b, e) * value
                total = term if total is None else total + term
        xs[b, 8 : 8 + WT] = total - spread * rs[2, 8 + b : 8 + b + WT]
        xs[3 + b, 8 : 8 + WT] = spread * ls[2, 7 + b : 7 + b + WT]
    for q in range(3):
        terms = dot(ub[2 * WT * q : 2 * WT * (q + 1)], lb[...], TN)
        for si in range(5):
            total = None
            for b in range(3):
                e = b - (si - 2)
                if 0 <= e <= 2:
                    term = tap(q, b, e) * terms[:, b * CH : (b + 1) * CH]
                    total = term if total is None else total + term
            ys[si] = total if q == 0 else ys[si] + total
    grad_left = xs[0, 9 : 9 + WT] + xs[1, 8 : 8 + WT] + xs[2, 7 : 7 + WT]
    grad_right = ys[0, 4 : 4 + WT]
    for si in range(1, 5):
        grad_right = grad_right + ys[si, 4 - si : 4 - si + WT]
    for b in range(3):
        grad_right = grad_right - xs[3 + b, 8 - b : 8 - b + WT]
    for dst in range(WA):
        out_ref[dst, 0] = grad_left[TILE * dst : TILE * (dst + 1)].astype(BF16)
        out_ref[dst, 1] = grad_right[TILE * dst : TILE * (dst + 1)].astype(BF16)


def payload_kernel(grads_ref, sums_ref, out_ref):
    total = sums_ref[0]
    for i in range(1, sums_ref.shape[0]):
        total = total + sums_ref[i]
    lane = lax.broadcasted_iota(jnp.int32, (8, CH), 1)
    high, middle, low = [jnp.where(lane < THIRD, part.astype(F32), 0.0) for part in split3(total)]
    sums = high + pltpu.roll(middle, THIRD, 1) + pltpu.roll(low, 2 * THIRD, 1)
    for dst in range(WA):
        left, right = grads_ref[dst, 0].astype(F32), grads_ref[dst, 1].astype(F32)
        out_ref[dst] = jnp.concatenate([left, right, sums], axis=0).astype(BF16)


def finish_kernel(recv_ref, left_ref, right_ref, weight_ref, loss_ref):
    total = recv_ref[0].astype(F32)[2 * TILE :]
    for src in range(1, WA):
        total = total + recv_ref[src].astype(F32)[2 * TILE :]
    total = total + pltpu.roll(total, CH - THIRD, 1) + pltpu.roll(total, CH - 2 * THIRD, 1)
    norm = 1.0 / jnp.maximum(total[0:1, COUNT_LANE : COUNT_LANE + 1], 1.0)
    for src in range(WA):
        block = recv_ref[src].astype(F32) * norm
        left_ref[src] = block[0:TILE]
        right_ref[src] = block[TILE : 2 * TILE]
    loss_ref[...] = total[0:1, LOSS_LANE : LOSS_LANE + 1] * norm
    by_tap = jnp.concatenate([total * norm, jnp.zeros((CH - 8, CH), F32)], axis=0).T
    for a in range(3):
        for b in range(3):
            at = 9 * a + 3 * b
            weight_ref[a, b] = by_tap[at : at + 3, 0:8]


def call(kernel, out_shape, *args, scratch=(), flops=0, params=VMEM):
    cost = pl.CostEstimate(flops=flops, bytes_accessed=1 << 20, transcendentals=0)
    return pl.pallas_call(
        kernel, out_shape=out_shape, scratch_shapes=list(scratch), compiler_params=params, cost_estimate=cost
    )(*args)


def shards(left_feat, right_feat, conv_weight, disparity_gt, valid_mask):
    left, right = left_feat[0], right_feat[0]
    gt, valid = disparity_gt[0], valid_mask[0]
    ha_count = lax.axis_size("ha")
    halo = jax.ShapeDtypeStruct((5, TILE, CH), BF16)
    own = jax.ShapeDtypeStruct((2 * ROWS + 1, TILE, CH), BF16)
    args = (left, right, gt, valid, jnp.transpose(conv_weight, (1, 2, 3, 0)))
    up, down, own, taps = pl.pallas_call(
        halo_kernel,
        out_shape=(halo, halo, own, jax.ShapeDtypeStruct((3, 16, CH), F32)),
        in_specs=[pl.BlockSpec(memory_space=pltpu.HBM)] * 5,
        scratch_shapes=[
            pltpu.VMEM((ROWS, TILE, CH), BF16),
            pltpu.VMEM((ROWS, TILE, CH), BF16),
            pltpu.VMEM((ROWS, TILE), jnp.int32),
            pltpu.VMEM((ROWS, TILE), jnp.int32),
            pltpu.VMEM((3, 3, 3, 8), F32),
            pltpu.SemaphoreType.DMA((5,)),
        ],
        compiler_params=VMEM,
    )(*[pltpu.with_memory_space_constraint(arg, pltpu.HBM) for arg in args])
    before = lax.ppermute(up, "ha", [(i, (i + 1) % ha_count) for i in range(ha_count)])
    after = lax.ppermute(down, "ha", [((i + 1) % ha_count, i) for i in range(ha_count)])
    block = jax.ShapeDtypeStruct((13, TILE, CH), BF16)
    blocks = call(
        pack_kernel,
        (block,) * CHIPS,
        own,
        before,
        after,
        scratch=(pltpu.VMEM((24, TILE, CH), BF16),),
    )
    same_core = [blocks[0]]
    for hop in range(1, CHIPS):
        same_core.append(lax.ppermute(blocks[hop], "wa", [(i, (i + 2 * hop) % WA) for i in range(WA)]))
    other_core = [lax.ppermute(value, "wa", [(i, i ^ 1) for i in range(WA)]) for value in same_core]
    tiles = same_core + other_core
    others = lax.axis_size("dp") * ha_count
    rows = (
        pltpu.VMEM((5, WT + 16, CH), F32),
        pltpu.VMEM((5, WT + 80, CH), F32),
        pltpu.VMEM((JP, 25 * CH), BF16),
        pltpu.VMEM((WT, CH), F32),
        pltpu.VMEM((3 * WT, 15 * CH), BF16),
    )
    sums, own_ub, own_diag = call(
        own_kernel,
        (
            jax.ShapeDtypeStruct((others, 8, CH), F32),
            jax.ShapeDtypeStruct((2 * WT, JP), BF16),
            jax.ShapeDtypeStruct((WT, CH), F32),
        ),
        *tiles,
        taps,
        scratch=rows + (pltpu.VMEM((CH, CH), F32),),
        flops=2 << 30,
    )
    sums = lax.all_to_all(sums, ("dp", "ha"), 0, 0, tiled=True)
    grads = call(
        rest_kernel,
        jax.ShapeDtypeStruct((WA, 2, TILE, CH), BF16),
        *tiles,
        taps,
        own_ub,
        own_diag,
        scratch=rows
        + (
            pltpu.VMEM((6 * WT, JP), BF16),
            pltpu.VMEM((3, WT, CH), F32),
            pltpu.VMEM((2 * WT, 3 * CH), BF16),
            pltpu.VMEM((6, WT + 16, CH), F32),
            pltpu.VMEM((5, JP, CH), F32),
        ),
        flops=3 << 30,
    )
    payload = call(payload_kernel, jax.ShapeDtypeStruct((WA, 2 * TILE + 8, CH), BF16), grads, sums)
    back = lax.all_to_all(payload, "wa", 0, 0, tiled=True)
    tile = jax.ShapeDtypeStruct((ROWS, TILE, CH), F32)
    grad_left, grad_right, weight, loss = call(
        finish_kernel,
        (tile, tile, jax.ShapeDtypeStruct((3, 3, 3, 8), F32), jax.ShapeDtypeStruct((1, 1), F32)),
        back,
    )
    return (loss[0, 0], grad_left[None], grad_right[None], jnp.transpose(weight, (3, 0, 1, 2)))


def solution(mesh):
    placed = (
        P("dp", "ha", "wa", None),
        P("dp", "ha", "wa", None),
        P(),
        P("dp", "ha", "wa"),
        P("dp", "ha", "wa"),
    )
    return jax.shard_map(
        shards,
        mesh=mesh,
        in_specs=placed,
        out_specs=(P(), P("dp", "ha", "wa", None), P("dp", "ha", "wa", None), P()),
        check_vma=False,
    )
```

```python
import jax
import jax.numpy as jnp
from jax import lax
from jax.experimental import pallas as pl
from jax.experimental.pallas import tpu as pltpu
from jax.sharding import PartitionSpec as P

F32 = jnp.float32
BF16 = jnp.bfloat16
ROWS, TILE, CH = 8, 24, 128
WA, CHIPS = 8, 4
WT = 192
JP = 256
GT_LANE, VALID_LANE = 0, 16
LOSS_LANE, COUNT_LANE, SHARE = 27, 28, 32
VMEM = pltpu.CompilerParams(vmem_limit_bytes=48 * 1024 * 1024)
NT = (((1,), (1,)), ((), ()))
NN = (((1,), (0,)), ((), ()))
TN = (((0,), (0,)), ((), ()))


def dot(lhs, rhs, dims=NN, precision=None):
    return lax.dot_general(lhs, rhs, dims, precision=precision, preferred_element_type=F32)


def meta_block(gt, valid, first, count, lane_of_first):
    row = lax.broadcasted_iota(jnp.int32, (ROWS, CH), 0)
    lane = lax.broadcasted_iota(jnp.int32, (ROWS, CH), 1)
    chosen = (row >= first) & (row < first + count)
    at = row - first + lane_of_first
    pick_gt = (chosen & (lane == at + GT_LANE)).astype(F32)
    pick_valid = (chosen & (lane == at + VALID_LANE)).astype(F32)
    return dot(gt, pick_gt, TN) + dot(valid, pick_valid, TN)


def halo_kernel(left_any, right_any, gt_any, valid_any, weight_any, up_ref, down_ref, own_ref, taps_ref, *scratch):
    refs, sems = scratch[:5], scratch[5]
    sources = (left_any, right_any, gt_any, valid_any, weight_any)
    copies = [pltpu.make_async_copy(src, dst, sems.at[i]) for i, (src, dst) in enumerate(zip(sources, refs))]
    for copy in copies:
        copy.start()
    for copy in copies:
        copy.wait()
    left_ref, right_ref, gt_ref, valid_ref, weight_ref = refs
    gt = gt_ref[...].astype(F32)
    valid = valid_ref[...].astype(F32)
    for side, ref in ((0, left_ref), (1, right_ref)):
        for i in range(2):
            up_ref[2 * side + i] = ref[ROWS - 2 + i]
            down_ref[2 * side + i] = ref[i]
        for i in range(ROWS):
            own_ref[ROWS * side + i] = ref[i]
    up_ref[4] = meta_block(gt, valid, ROWS - 2, 2, 0).astype(BF16)
    down_ref[4] = meta_block(gt, valid, 0, 2, ROWS + 2).astype(BF16)
    own_ref[2 * ROWS] = meta_block(gt, valid, 0, ROWS, 2).astype(BF16)
    member = group_member() * (1.0 / 16.0)
    for a in range(3):
        taps = jnp.concatenate([weight_ref[a, b] for b in range(3)], axis=0)
        taps_ref[a, 0:9] = dot(taps, member, precision=lax.Precision.HIGHEST)


def group_member():
    group = lax.broadcasted_iota(jnp.int32, (8, CH), 0)
    channel = lax.broadcasted_iota(jnp.int32, (8, CH), 1)
    return (lax.shift_right_logical(channel, 4) == group).astype(F32)


def position():
    index = lax.axis_index("wa")
    return lax.shift_right_logical(index, 1), index & 1


def pack_kernel(own_ref, prev_ref, next_ref, *refs):
    outs, ext = refs[:CHIPS], refs[CHIPS]
    chip, _ = position()
    band = lax.axis_index("ha")
    has_prev = band > 0
    has_next = band < lax.axis_size("ha") - 1

    def of_prev(i):
        return jnp.where(has_prev, prev_ref[i], jnp.zeros((TILE, CH), BF16))

    def of_next(i):
        return jnp.where(has_next, next_ref[i], jnp.zeros((TILE, CH), BF16))

    meta = own_ref[2 * ROWS].astype(F32)
    meta = (meta + of_prev(4).astype(F32) + of_next(4).astype(F32)).astype(BF16)
    for side in range(2):
        for i in range(2):
            ext[12 * side + i] = of_prev(2 * side + i)
            ext[12 * side + ROWS + 2 + i] = of_next(2 * side + i)
        for i in range(ROWS):
            ext[12 * side + 2 + i] = own_ref[ROWS * side + i]
    for hop in range(CHIPS):
        first = 2 * ((chip + hop) & (CHIPS - 1))
        for i in range(6):
            outs[hop][i] = ext[first + i]
            outs[hop][6 + i] = ext[first + 12 + i]
        outs[hop][12] = meta


def split3(value):
    high = value.astype(BF16)
    rest = value - high.astype(F32)
    middle = rest.astype(BF16)
    low = (rest - middle.astype(F32)).astype(BF16)
    return high, middle, low


def fill(refs, first, count, ls, rs, rb):
    chip, core = position()
    tiles = []
    for hop in range(CHIPS):
        tile = 2 * ((chip - hop) & (CHIPS - 1))
        tiles.append((refs[hop], pl.multiple_of(8 + TILE * (tile + core), 8)))
        tiles.append((refs[CHIPS + hop], pl.multiple_of(8 + TILE * (tile + 1 - core), 8)))

    @pl.loop(first, first + count)
    def row(rho):
        ls[rho, 0:8] = jnp.zeros((8, CH), F32)
        ls[rho, 8 + WT :] = jnp.zeros((8, CH), F32)
        rs[rho, 0:8] = jnp.zeros((8, CH), F32)
        rs[rho, 8 + WT :] = jnp.zeros((72, CH), F32)
        for ref, at in tiles:
            ls[rho, pl.ds(at, TILE)] = ref[core + rho].astype(F32)
            rs[rho, pl.ds(at, TILE)] = ref[6 + core + rho].astype(F32)
        for si in range(5):
            rb[:, pl.ds(pl.multiple_of((5 * rho + si) * CH, CH), CH)] = rs[rho, 4 + si : 4 + si + JP].astype(BF16)

    return tiles


def fill_meta(tiles, ms):
    for ref, at in tiles:
        ms[pl.ds(at - 8, TILE)] = ref[12].astype(F32)


def split2(value):
    high = value.astype(BF16)
    return high, (value - high.astype(F32)).astype(BF16)


def weighted(a, left, wc_ref, ab, at):
    for si in range(5):
        value = None
        for b in range(3):
            e = b - (si - 2)
            if 0 <= e <= 2:
                term = wc_ref[a, 3 * b + e : 3 * b + e + 1] * left[b]
                value = term if value is None else value + term
        for i, part in enumerate(split3(value)):
            ab[at + i * WT : at + (i + 1) * WT, si * CH : (si + 1) * CH] = part


def row_gradient(q, logits, diag_col, ms, masks):
    lane, level, inside, on_diag, wcol, zeros_count, zeros_mean = masks
    logits = logits - jnp.where(on_diag, diag_col, 0.0)
    top = jnp.max(jnp.where(inside, logits, -3e38), axis=1, keepdims=True)
    top = jnp.where(zeros_count > 0.0, jnp.maximum(top, 0.0), top)
    expd = jnp.where(inside, jnp.exp(logits - top), 0.0)
    zero_exp = jnp.where(zeros_count > 0.0, zeros_count * jnp.exp(-top), 0.0)
    denom = jnp.sum(expd, axis=1, keepdims=True) + zero_exp
    first = jnp.sum(expd * level, axis=1, keepdims=True) + zero_exp * zeros_mean
    inv = 1.0 / denom
    estimate = first * inv
    ext = lax.axis_index("wa") + 1 + q
    meta = ms[...]
    target = jnp.sum(jnp.where(lane == GT_LANE + ext, meta, 0.0), axis=1, keepdims=True)
    valid = jnp.sum(jnp.where(lane == VALID_LANE + ext, meta, 0.0), axis=1, keepdims=True)
    usable = jnp.where(target <= wcol, valid, 0.0)
    resid = estimate - target
    factor = jnp.clip(resid, -1.0, 1.0) * usable * inv
    return expd * (level - estimate) * factor, resid, usable


def diagonal(up, on_diag):
    return jnp.sum(jnp.where(on_diag, up, 0.0), axis=1, keepdims=True)


def row_masks():
    lane = lax.broadcasted_iota(jnp.int32, (WT, CH), 1)
    ww = lax.broadcasted_iota(jnp.int32, (WT, JP), 0)
    jj = lax.broadcasted_iota(jnp.int32, (WT, JP), 1)
    level = (ww - jj + 2).astype(F32)
    inside = (jj <= ww + 2) & (jj >= ww - (WT - 3))
    on_diag = jj == ww + 2
    wcol = lax.broadcasted_iota(jnp.int32, (WT, 1), 0).astype(F32)
    zeros_count = jnp.maximum(float(WT - 3) - wcol, 0.0)
    zeros_mean = (wcol + float(WT + 2)) * 0.5
    return lane, level, inside, on_diag, wcol, zeros_count, zeros_mean


def logits_of(ls, rb, wc_ref, ab, acc):
    for rho in range(5):
        rows = [q for q in range(3) if 0 <= rho - q <= 2]
        left = [ls[rho, 7 + b : 7 + b + WT] for b in range(3)]
        for i, q in enumerate(rows):
            weighted(rho - q, left, wc_ref, ab.at[rho], 3 * WT * i)
        part = dot(ab[rho, 0 : 3 * WT * len(rows)], rb[:, 5 * rho * CH : 5 * (rho + 1) * CH], NT)
        for i, q in enumerate(rows):
            at = 3 * WT * i
            total = part[at : at + WT] + part[at + WT : at + 2 * WT] + part[at + 2 * WT : at + 3 * WT]
            acc[q] = total if rho == q else acc[q] + total


def main_kernel(*refs):
    recv, wc_ref = refs[:8], refs[8]
    sums_ref, kept_ref, given_ref = refs[9:12]
    ls, rs, rb, ms, ab, acc, ub, diags, ks, lb, xs, ys, out_ref = refs[12:]
    fill_meta(fill(recv, 0, 5, ls, rs, rb), ms)
    ks[...] = jnp.zeros(ks.shape, F32)
    xs[...] = jnp.zeros(xs.shape, F32)
    masks = row_masks()
    logits_of(ls, rb, wc_ref, ab, acc)
    for q in range(3):
        diag = None
        for a in range(3):
            for b in range(3):
                term = wc_ref[a, 3 * b : 3 * b + 1] * ls[q + a, 7 + b : 7 + b + WT] * rs[q + a, 8 + b : 8 + b + WT]
                diag = term if diag is None else diag + term
        up, resid, usable = row_gradient(q, acc[q], jnp.sum(diag, axis=1, keepdims=True), ms, masks)
        ub[2 * WT * q : 2 * WT * q + WT], ub[2 * WT * q + WT : 2 * WT * (q + 1)] = split2(up)
        diags[q] = jnp.broadcast_to(diagonal(up, masks[3]), (WT, CH))
        if q == 1:
            size = jnp.abs(resid)
            smooth = jnp.where(size < 1.0, 0.5 * resid * resid, size - 0.5)
            loss_sum = jnp.sum(usable * smooth, axis=0, keepdims=True)
            count_sum = jnp.sum(usable, axis=0, keepdims=True)
    for b in range(3):
        shifted = ls[2, 7 + b : 7 + b + WT].astype(BF16)
        lb[0:WT, b * CH : (b + 1) * CH] = shifted
        lb[WT:, b * CH : (b + 1) * CH] = shifted

    def tap(q, b, e):
        return wc_ref[2 - q, 3 * b + e : 3 * b + e + 1]

    terms = dot(ub[...], rb[:, 10 * CH : 15 * CH])
    for b in range(3):
        own_left, own_right = ls[2, 7 + b : 7 + b + WT], rs[2, 8 + b : 8 + b + WT]
        total = None
        spread = None
        for q in range(3):
            term = tap(q, b, 0) * diags[q]
            spread = term if spread is None else spread + term
            for e in range(3):
                at, si = 2 * WT * q, b - e + 2
                value = terms[at : at + WT, si * CH : (si + 1) * CH]
                value = value + terms[at + WT : at + 2 * WT, si * CH : (si + 1) * CH]
                if e == 0:
                    value = value - diags[q] * own_right
                at = 9 * (2 - q) + 3 * b + e
                ks[at : at + 1] = jnp.sum(own_left * value, axis=0, keepdims=True)
                term = tap(q, b, e) * value
                total = term if total is None else total + term
        xs[b, 8 : 8 + WT] = total
        xs[3 + b, 8 : 8 + WT] = spread * own_left
    for q in range(3):
        terms = dot(ub[2 * WT * q : 2 * WT * (q + 1)], lb[...], TN)
        for si in range(5):
            total = None
            for b in range(3):
                e = b - (si - 2)
                if 0 <= e <= 2:
                    term = tap(q, b, e) * terms[:, b * CH : (b + 1) * CH]
                    total = term if total is None else total + term
            ys[si] = total if q == 0 else ys[si] + total
    channel = lax.broadcasted_iota(jnp.int32, (8, CH), 1)
    member = group_member().astype(BF16)
    parts = [dot(member, part, NT) for part in split3(ks[...])]
    sums = (parts[0] + (parts[1] + parts[2])) * (1.0 / 16.0)
    sums = jnp.where(channel == LOSS_LANE, loss_sum, sums)
    sums = jnp.where(channel == COUNT_LANE, count_sum, sums)
    sums = jnp.where(channel < SHARE, sums, 0.0)
    quarter = lax.broadcasted_iota(jnp.int32, (8, CH), 0) & 3
    placed = jnp.where(quarter == 0, sums, 0.0)
    for i in range(1, 4):
        placed = placed + jnp.where(quarter == i, pltpu.roll(sums, SHARE * i, 1), 0.0)
    packed = jnp.concatenate([jnp.sum(placed[4 * i : 4 * i + 4], axis=0, keepdims=True) for i in range(2)], axis=0)
    for i in range(sums_ref.shape[0]):
        sums_ref[i] = packed
    grad_left = xs[0, 9 : 9 + WT] + xs[1, 8 : 8 + WT] + xs[2, 7 : 7 + WT]
    grad_right = ys[0, 4 : 4 + WT]
    for si in range(1, 5):
        grad_right = grad_right + ys[si, 4 - si : 4 - si + WT]
    for b in range(3):
        grad_right = grad_right - xs[3 + b, 8 - b : 8 - b + WT]
    for dst in range(WA):
        out_ref[dst, 0] = grad_left[TILE * dst : TILE * (dst + 1)].astype(BF16)
        out_ref[dst, 1] = grad_right[TILE * dst : TILE * (dst + 1)].astype(BF16)
    chip, core = position()
    for ref, holder in ((kept_ref, core), (given_ref, 1 - core)):
        beside = chip_at(chip, ahead(holder))
        opposite = chip_at(chip, 2)
        places = (2 * beside + holder, 2 * beside + 1 - holder, 2 * opposite + holder, 2 * chip + holder)
        for i, tile in enumerate(places):
            for side in range(2):
                ref[2 * i + side] = out_ref[tile, side]


def ahead(core):
    return 1 - 2 * core


def chip_at(chip, step):
    return (chip + step + CHIPS) & (CHIPS - 1)


def pack_back_kernel(kept_ref, got_ref, *outs):
    for place, out_ref in zip((2, 0, 1), outs):
        for row, ref in enumerate((kept_ref, got_ref)):
            for side in range(2):
                out_ref[2 * row + side] = ref[2 * place + side]


def finish_kernel(kept, got, near, far, across, sums_ref, left_ref, right_ref, weight_ref, loss_ref):
    chip, core = position()
    other = 1 - core
    before, after, opposite = chip_at(chip, -ahead(core)), chip_at(chip, ahead(core)), chip_at(chip, 2)
    partial = [sums_ref[i] for i in range(8)]
    for i in range(8, sums_ref.shape[0]):
        partial[i % 8] = partial[i % 8] + sums_ref[i]
    while len(partial) > 1:
        partial = [x + y for x, y in zip(partial[0::2], partial[1::2])]
    placed = partial[0]
    total = jnp.concatenate(
        [pltpu.roll(jnp.broadcast_to(placed[g // 4 : g // 4 + 1], (8, CH)), (CH - SHARE * (g % 4)) % CH, 1)[0:1] for g in range(8)],
        axis=0,
    )
    norm = 1.0 / jnp.maximum(total[0:1, COUNT_LANE : COUNT_LANE + 1], 1.0)
    blocks = (
        (kept, 6, 2 * chip + core),
        (got, 6, 2 * chip + other),
        (near, 0, 2 * before + core),
        (near, 2, 2 * before + other),
        (far, 0, 2 * after + other),
        (far, 2, 2 * after + core),
        (across, 0, 2 * opposite + core),
        (across, 2, 2 * opposite + other),
    )
    for ref, at, row in blocks:
        left_ref[row] = ref[at].astype(F32) * norm
        right_ref[row] = ref[at + 1].astype(F32) * norm
    loss_ref[...] = total[0:1, LOSS_LANE : LOSS_LANE + 1] * norm
    by_tap = jnp.concatenate([total * norm, jnp.zeros((CH - 8, CH), F32)], axis=0).T
    for a in range(3):
        for b in range(3):
            at = 9 * a + 3 * b
            weight_ref[a, b] = by_tap[at : at + 3, 0:8]


def call(kernel, out_shape, *args, scratch=(), flops=0, params=VMEM):
    cost = pl.CostEstimate(flops=flops, bytes_accessed=1 << 20, transcendentals=0)
    return pl.pallas_call(
        kernel, out_shape=out_shape, scratch_shapes=list(scratch), compiler_params=params, cost_estimate=cost
    )(*args)


def swapped(value):
    return lax.ppermute(value, "wa", [(i, i ^ 1) for i in range(WA)])


def shards(left_feat, right_feat, conv_weight, disparity_gt, valid_mask):
    left, right = left_feat[0], right_feat[0]
    gt, valid = disparity_gt[0], valid_mask[0]
    ha_count = lax.axis_size("ha")
    halo = jax.ShapeDtypeStruct((5, TILE, CH), BF16)
    own = jax.ShapeDtypeStruct((2 * ROWS + 1, TILE, CH), BF16)
    args = (left, right, gt, valid, jnp.transpose(conv_weight, (1, 2, 3, 0)))
    up, down, own, taps = pl.pallas_call(
        halo_kernel,
        out_shape=(halo, halo, own, jax.ShapeDtypeStruct((3, 16, CH), F32)),
        in_specs=[pl.BlockSpec(memory_space=pltpu.HBM)] * 5,
        scratch_shapes=[
            pltpu.VMEM((ROWS, TILE, CH), BF16),
            pltpu.VMEM((ROWS, TILE, CH), BF16),
            pltpu.VMEM((ROWS, TILE), jnp.int32),
            pltpu.VMEM((ROWS, TILE), jnp.int32),
            pltpu.VMEM((3, 3, 3, 8), F32),
            pltpu.SemaphoreType.DMA((5,)),
        ],
        compiler_params=VMEM,
    )(*[pltpu.with_memory_space_constraint(arg, pltpu.HBM) for arg in args])
    before = lax.ppermute(up, "ha", [(i, (i + 1) % ha_count) for i in range(ha_count)])
    after = lax.ppermute(down, "ha", [((i + 1) % ha_count, i) for i in range(ha_count)])
    block = jax.ShapeDtypeStruct((13, TILE, CH), BF16)
    blocks = call(
        pack_kernel,
        (block,) * CHIPS,
        own,
        before,
        after,
        scratch=(pltpu.VMEM((24, TILE, CH), BF16),),
    )
    same_core = [blocks[0]]
    for hop in range(1, CHIPS):
        same_core.append(lax.ppermute(blocks[hop], "wa", [(i, (i + 2 * hop) % WA) for i in range(WA)]))
    other_core = [lax.ppermute(value, "wa", [(i, i ^ 1) for i in range(WA)]) for value in same_core]
    tiles = same_core + other_core
    others = lax.axis_size("dp") * ha_count * WA
    half = jax.ShapeDtypeStruct((8, TILE, CH), BF16)
    sums, kept, given = call(
        main_kernel,
        (jax.ShapeDtypeStruct((others, 2, CH), F32), half, half),
        *tiles,
        taps,
        scratch=(
            pltpu.VMEM((5, WT + 16, CH), F32),
            pltpu.VMEM((5, WT + 80, CH), F32),
            pltpu.VMEM((JP, 25 * CH), BF16),
            pltpu.VMEM((WT, CH), F32),
            pltpu.VMEM((5, 9 * WT, 5 * CH), BF16),
            pltpu.VMEM((3, WT, JP), F32),
            pltpu.VMEM((6 * WT, JP), BF16),
            pltpu.VMEM((3, WT, CH), F32),
            pltpu.VMEM((CH, CH), F32),
            pltpu.VMEM((2 * WT, 3 * CH), BF16),
            pltpu.VMEM((6, WT + 16, CH), F32),
            pltpu.VMEM((5, JP, CH), F32),
            pltpu.VMEM((WA, 2, TILE, CH), BF16),
        ),
        flops=5 << 30,
    )
    sums = lax.all_to_all(sums, ("dp", "ha", "wa"), 0, 0, tiled=True)
    got = swapped(given)
    block = jax.ShapeDtypeStruct((4, TILE, CH), BF16)
    opposite, beside, beside_other = call(pack_back_kernel, (block,) * 3, kept, got)
    across = lax.ppermute(opposite, "wa", [(i, (i + 4) % WA) for i in range(WA)])
    near = lax.ppermute(beside, "wa", [(i, (i + 2 - 4 * (i % 2)) % WA) for i in range(WA)])
    far = lax.ppermute(beside_other, "wa", [(i, (i + 3 - 6 * (i % 2)) % WA) for i in range(WA)])
    tile = jax.ShapeDtypeStruct((ROWS, TILE, CH), F32)
    grad_left, grad_right, weight, loss = call(
        finish_kernel,
        (tile, tile, jax.ShapeDtypeStruct((3, 3, 3, 8), F32), jax.ShapeDtypeStruct((1, 1), F32)),
        kept,
        got,
        near,
        far,
        across,
        sums,
    )
    return (loss[0, 0], grad_left[None], grad_right[None], jnp.transpose(weight, (3, 0, 1, 2)))


def solution(mesh):
    placed = (
        P("dp", "ha", "wa", None),
        P("dp", "ha", "wa", None),
        P(),
        P("dp", "ha", "wa"),
        P("dp", "ha", "wa"),
    )
    return jax.shard_map(
        shards,
        mesh=mesh,
        in_specs=placed,
        out_specs=(P(), P("dp", "ha", "wa", None), P("dp", "ha", "wa", None), P()),
        check_vma=False,
    )
```

```python
import functools

import jax
import jax.numpy as jnp
from jax import lax
from jax.experimental import pallas as pl
from jax.experimental.pallas import tpu as pltpu
from jax.sharding import PartitionSpec as P

F32 = jnp.float32
BF16 = jnp.bfloat16
ROWS, TILE, CH = 8, 24, 128
WA, CHIPS = 8, 4
WT = 192
JP = 256
GT_LANE, VALID_LANE = 0, 16
LOSS_LANE, COUNT_LANE, SHARE = 27, 28, 32
VMEM = pltpu.CompilerParams(vmem_limit_bytes=48 * 1024 * 1024)
NT = (((1,), (1,)), ((), ()))
NN = (((1,), (0,)), ((), ()))
TN = (((0,), (0,)), ((), ()))


def dot(lhs, rhs, dims=NN, precision=None):
    return lax.dot_general(lhs, rhs, dims, precision=precision, preferred_element_type=F32)


def meta_block(gt, valid, first, count, lane_of_first):
    row = lax.broadcasted_iota(jnp.int32, (ROWS, CH), 0)
    lane = lax.broadcasted_iota(jnp.int32, (ROWS, CH), 1)
    chosen = (row >= first) & (row < first + count)
    at = row - first + lane_of_first
    pick_gt = (chosen & (lane == at + GT_LANE)).astype(F32)
    pick_valid = (chosen & (lane == at + VALID_LANE)).astype(F32)
    return dot(gt, pick_gt, TN) + dot(valid, pick_valid, TN)


def halo_kernel(left_any, right_any, gt_any, valid_any, weight_any, up_ref, down_ref, own_ref, taps_ref, *scratch):
    refs, sems = scratch[:5], scratch[5]
    sources = (left_any, right_any, gt_any, valid_any, weight_any)
    copies = [pltpu.make_async_copy(src, dst, sems.at[i]) for i, (src, dst) in enumerate(zip(sources, refs))]
    for copy in copies:
        copy.start()
    for copy in copies:
        copy.wait()
    left_ref, right_ref, gt_ref, valid_ref, weight_ref = refs
    gt = gt_ref[...].astype(F32)
    valid = valid_ref[...].astype(F32)
    for side, ref in ((0, left_ref), (1, right_ref)):
        for i in range(2):
            up_ref[2 * side + i] = ref[ROWS - 2 + i]
            down_ref[2 * side + i] = ref[i]
        for i in range(ROWS):
            own_ref[ROWS * side + i] = ref[i]
    up_ref[4] = meta_block(gt, valid, ROWS - 2, 2, 0).astype(BF16)
    down_ref[4] = meta_block(gt, valid, 0, 2, ROWS + 2).astype(BF16)
    own_ref[2 * ROWS] = meta_block(gt, valid, 0, ROWS, 2).astype(BF16)
    member = group_member() * (1.0 / 16.0)
    for a in range(3):
        taps = jnp.concatenate([weight_ref[a, b] for b in range(3)], axis=0)
        taps_ref[a, 0:9] = dot(taps, member, precision=lax.Precision.HIGHEST)


def group_member():
    group = lax.broadcasted_iota(jnp.int32, (8, CH), 0)
    channel = lax.broadcasted_iota(jnp.int32, (8, CH), 1)
    return (lax.shift_right_logical(channel, 4) == group).astype(F32)


def position():
    index = lax.axis_index("wa")
    return lax.shift_right_logical(index, 1), index & 1


def pack_kernel(own_ref, prev_ref, next_ref, *refs):
    outs, ext = refs[:CHIPS], refs[CHIPS]
    chip, _ = position()
    band = lax.axis_index("ha")
    has_prev = band > 0
    has_next = band < lax.axis_size("ha") - 1

    def of_prev(i):
        return jnp.where(has_prev, prev_ref[i], jnp.zeros((TILE, CH), BF16))

    def of_next(i):
        return jnp.where(has_next, next_ref[i], jnp.zeros((TILE, CH), BF16))

    meta = own_ref[2 * ROWS].astype(F32)
    meta = (meta + of_prev(4).astype(F32) + of_next(4).astype(F32)).astype(BF16)
    for side in range(2):
        for i in range(2):
            ext[12 * side + i] = of_prev(2 * side + i)
            ext[12 * side + ROWS + 2 + i] = of_next(2 * side + i)
        for i in range(ROWS):
            ext[12 * side + 2 + i] = own_ref[ROWS * side + i]
    for hop in range(CHIPS):
        first = 2 * ((chip + hop) & (CHIPS - 1))
        for i in range(6):
            outs[hop][i] = ext[first + i]
            outs[hop][6 + i] = ext[first + 12 + i]
        outs[hop][12] = meta


def split3(value):
    high = value.astype(BF16)
    rest = value - high.astype(F32)
    middle = rest.astype(BF16)
    low = (rest - middle.astype(F32)).astype(BF16)
    return high, middle, low


def fill(refs, first, count, ls, rs, rb):
    chip, core = position()
    tiles = []
    for hop in range(CHIPS):
        tile = 2 * ((chip - hop) & (CHIPS - 1))
        tiles.append((refs[hop], pl.multiple_of(8 + TILE * (tile + core), 8)))
        tiles.append((refs[CHIPS + hop], pl.multiple_of(8 + TILE * (tile + 1 - core), 8)))

    @pl.loop(first, first + count)
    def row(rho):
        ls[rho, 0:8] = jnp.zeros((8, CH), F32)
        ls[rho, 8 + WT :] = jnp.zeros((8, CH), F32)
        rs[rho, 0:8] = jnp.zeros((8, CH), F32)
        rs[rho, 8 + WT :] = jnp.zeros((72, CH), F32)
        for ref, at in tiles:
            ls[rho, pl.ds(at, TILE)] = ref[core + rho].astype(F32)
            rs[rho, pl.ds(at, TILE)] = ref[6 + core + rho].astype(F32)
        for si in range(5):
            rb[:, pl.ds(pl.multiple_of((5 * rho + si) * CH, CH), CH)] = rs[rho, 4 + si : 4 + si + JP].astype(BF16)

    return tiles


def fill_meta(tiles, ms):
    for ref, at in tiles:
        ms[pl.ds(at - 8, TILE)] = ref[12].astype(F32)


def split2(value):
    high = value.astype(BF16)
    return high, (value - high.astype(F32)).astype(BF16)


def weighted(a, left, wc_ref, ab, at):
    for si in range(5):
        value = None
        for b in range(3):
            e = b - (si - 2)
            if 0 <= e <= 2:
                term = wc_ref[a, 3 * b + e : 3 * b + e + 1] * left[b]
                value = term if value is None else value + term
        for i, part in enumerate(split3(value)):
            ab[at + i * WT : at + (i + 1) * WT, si * CH : (si + 1) * CH] = part


def row_gradient(q, logits, diag_col, ms, masks):
    lane, level, inside, on_diag, wcol, zeros_count, zeros_mean = masks
    logits = logits - jnp.where(on_diag, diag_col, 0.0)
    top = jnp.max(jnp.where(inside, logits, -3e38), axis=1, keepdims=True)
    top = jnp.where(zeros_count > 0.0, jnp.maximum(top, 0.0), top)
    expd = jnp.where(inside, jnp.exp(logits - top), 0.0)
    zero_exp = jnp.where(zeros_count > 0.0, zeros_count * jnp.exp(-top), 0.0)
    denom = jnp.sum(expd, axis=1, keepdims=True) + zero_exp
    first = jnp.sum(expd * level, axis=1, keepdims=True) + zero_exp * zeros_mean
    inv = 1.0 / denom
    estimate = first * inv
    ext = lax.axis_index("wa") + 1 + q
    meta = ms[...]
    target = jnp.sum(jnp.where(lane == GT_LANE + ext, meta, 0.0), axis=1, keepdims=True)
    valid = jnp.sum(jnp.where(lane == VALID_LANE + ext, meta, 0.0), axis=1, keepdims=True)
    usable = jnp.where(target <= wcol, valid, 0.0)
    resid = estimate - target
    factor = jnp.clip(resid, -1.0, 1.0) * usable * inv
    return expd * (level - estimate) * factor, resid, usable


def diagonal(up, on_diag):
    return jnp.sum(jnp.where(on_diag, up, 0.0), axis=1, keepdims=True)


def row_masks():
    lane = lax.broadcasted_iota(jnp.int32, (WT, CH), 1)
    ww = lax.broadcasted_iota(jnp.int32, (WT, JP), 0)
    jj = lax.broadcasted_iota(jnp.int32, (WT, JP), 1)
    level = (ww - jj + 2).astype(F32)
    inside = (jj <= ww + 2) & (jj >= ww - (WT - 3))
    on_diag = jj == ww + 2
    wcol = lax.broadcasted_iota(jnp.int32, (WT, 1), 0).astype(F32)
    zeros_count = jnp.maximum(float(WT - 3) - wcol, 0.0)
    zeros_mean = (wcol + float(WT + 2)) * 0.5
    return lane, level, inside, on_diag, wcol, zeros_count, zeros_mean


def logits_of(ls, rb, wc_ref, ab, acc):
    for rho in range(5):
        rows = [q for q in range(3) if 0 <= rho - q <= 2]
        left = [ls[rho, 7 + b : 7 + b + WT] for b in range(3)]
        for i, q in enumerate(rows):
            weighted(rho - q, left, wc_ref, ab.at[rho], 3 * WT * i)
        part = dot(ab[rho, 0 : 3 * WT * len(rows)], rb[:, 5 * rho * CH : 5 * (rho + 1) * CH], NT)
        for i, q in enumerate(rows):
            at = 3 * WT * i
            total = part[at : at + WT] + part[at + WT : at + 2 * WT] + part[at + 2 * WT : at + 3 * WT]
            acc[q] = total if rho == q else acc[q] + total


def main_kernel(*refs):
    recv, wc_ref = refs[:8], refs[8]
    sums_ref, kept_ref, given_ref = refs[9:12]
    ls, rs, rb, ms, ab, acc, ub, diags, ks, lb, xs, ys, out_ref, fanned, sem = refs[12:]
    fill_meta(fill(recv, 0, 5, ls, rs, rb), ms)
    ks[...] = jnp.zeros(ks.shape, F32)
    xs[...] = jnp.zeros(xs.shape, F32)
    masks = row_masks()
    logits_of(ls, rb, wc_ref, ab, acc)
    for q in range(3):
        diag = None
        for a in range(3):
            for b in range(3):
                term = wc_ref[a, 3 * b : 3 * b + 1] * ls[q + a, 7 + b : 7 + b + WT] * rs[q + a, 8 + b : 8 + b + WT]
                diag = term if diag is None else diag + term
        up, resid, usable = row_gradient(q, acc[q], jnp.sum(diag, axis=1, keepdims=True), ms, masks)
        ub[2 * WT * q : 2 * WT * q + WT], ub[2 * WT * q + WT : 2 * WT * (q + 1)] = split2(up)
        diags[q] = jnp.broadcast_to(diagonal(up, masks[3]), (WT, CH))
        if q == 1:
            size = jnp.abs(resid)
            smooth = jnp.where(size < 1.0, 0.5 * resid * resid, size - 0.5)
            loss_sum = jnp.sum(usable * smooth, axis=0, keepdims=True)
            count_sum = jnp.sum(usable, axis=0, keepdims=True)
    for b in range(3):
        shifted = ls[2, 7 + b : 7 + b + WT].astype(BF16)
        lb[0:WT, b * CH : (b + 1) * CH] = shifted
        lb[WT:, b * CH : (b + 1) * CH] = shifted

    def tap(q, b, e):
        return wc_ref[2 - q, 3 * b + e : 3 * b + e + 1]

    terms = dot(ub[...], rb[:, 10 * CH : 15 * CH])
    for b in range(3):
        own_left, own_right = ls[2, 7 + b : 7 + b + WT], rs[2, 8 + b : 8 + b + WT]
        total = None
        spread = None
        for q in range(3):
            term = tap(q, b, 0) * diags[q]
            spread = term if spread is None else spread + term
            for e in range(3):
                at, si = 2 * WT * q, b - e + 2
                value = terms[at : at + WT, si * CH : (si + 1) * CH]
                value = value + terms[at + WT : at + 2 * WT, si * CH : (si + 1) * CH]
                if e == 0:
                    value = value - diags[q] * own_right
                at = 9 * (2 - q) + 3 * b + e
                ks[at : at + 1] = jnp.sum(own_left * value, axis=0, keepdims=True)
                term = tap(q, b, e) * value
                total = term if total is None else total + term
        xs[b, 8 : 8 + WT] = total
        xs[3 + b, 8 : 8 + WT] = spread * own_left
    channel = lax.broadcasted_iota(jnp.int32, (8, CH), 1)
    member = group_member().astype(BF16)
    parts = [dot(member, part, NT) for part in split3(ks[...])]
    sums = (parts[0] + (parts[1] + parts[2])) * (1.0 / 16.0)
    sums = jnp.where(channel == LOSS_LANE, loss_sum, sums)
    sums = jnp.where(channel == COUNT_LANE, count_sum, sums)
    sums = jnp.where(channel < SHARE, sums, 0.0)
    quarter = lax.broadcasted_iota(jnp.int32, (8, CH), 0) & 3
    placed = jnp.where(quarter == 0, sums, 0.0)
    for i in range(1, 4):
        placed = placed + jnp.where(quarter == i, pltpu.roll(sums, SHARE * i, 1), 0.0)
    packed = jnp.concatenate([jnp.sum(placed[4 * i : 4 * i + 4], axis=0, keepdims=True) for i in range(2)], axis=0)
    for i in range(sums_ref.shape[0]):
        fanned[i] = packed
    sending = pltpu.make_async_copy(fanned, sums_ref, sem)
    sending.start()
    for q in range(3):
        terms = dot(ub[2 * WT * q : 2 * WT * (q + 1)], lb[...], TN)
        for si in range(5):
            total = None
            for b in range(3):
                e = b - (si - 2)
                if 0 <= e <= 2:
                    term = tap(q, b, e) * terms[:, b * CH : (b + 1) * CH]
                    total = term if total is None else total + term
            ys[si] = total if q == 0 else ys[si] + total
    grad_left = xs[0, 9 : 9 + WT] + xs[1, 8 : 8 + WT] + xs[2, 7 : 7 + WT]
    grad_right = ys[0, 4 : 4 + WT]
    for si in range(1, 5):
        grad_right = grad_right + ys[si, 4 - si : 4 - si + WT]
    for b in range(3):
        grad_right = grad_right - xs[3 + b, 8 - b : 8 - b + WT]
    for dst in range(WA):
        out_ref[dst, 0] = grad_left[TILE * dst : TILE * (dst + 1)].astype(BF16)
        out_ref[dst, 1] = grad_right[TILE * dst : TILE * (dst + 1)].astype(BF16)
    chip, core = position()
    for ref, holder in ((kept_ref, core), (given_ref, 1 - core)):
        beside = chip_at(chip, ahead(holder))
        opposite = chip_at(chip, 2)
        places = (2 * beside + holder, 2 * beside + 1 - holder, 2 * opposite + holder, 2 * chip + holder)
        for i, tile in enumerate(places):
            for side in range(2):
                ref[2 * i + side] = out_ref[tile, side]
    sending.wait()


def ahead(core):
    return 1 - 2 * core


def chip_at(chip, step):
    return (chip + step + CHIPS) & (CHIPS - 1)


def pack_back_kernel(places, kept_ref, got_ref, *refs):
    for place, out_ref in zip(places, refs[-len(places) :]):
        for row, ref in enumerate((kept_ref, got_ref)):
            for side in range(2):
                out_ref[2 * row + side] = ref[2 * place + side]


def finish_kernel(kept, got, near, far, across, sums_ref, left_ref, right_ref, weight_ref, loss_ref):
    chip, core = position()
    other = 1 - core
    before, after, opposite = chip_at(chip, -ahead(core)), chip_at(chip, ahead(core)), chip_at(chip, 2)
    partial = [sums_ref[i] for i in range(8)]
    for i in range(8, sums_ref.shape[0]):
        partial[i % 8] = partial[i % 8] + sums_ref[i]
    while len(partial) > 1:
        partial = [x + y for x, y in zip(partial[0::2], partial[1::2])]
    placed = partial[0]
    total = jnp.concatenate(
        [pltpu.roll(jnp.broadcast_to(placed[g // 4 : g // 4 + 1], (8, CH)), (CH - SHARE * (g % 4)) % CH, 1)[0:1] for g in range(8)],
        axis=0,
    )
    norm = 1.0 / jnp.maximum(total[0:1, COUNT_LANE : COUNT_LANE + 1], 1.0)
    blocks = (
        (kept, 6, 2 * chip + core),
        (got, 6, 2 * chip + other),
        (near, 0, 2 * before + core),
        (near, 2, 2 * before + other),
        (far, 0, 2 * after + other),
        (far, 2, 2 * after + core),
        (across, 0, 2 * opposite + core),
        (across, 2, 2 * opposite + other),
    )
    for ref, at, row in blocks:
        left_ref[row] = ref[at].astype(F32) * norm
        right_ref[row] = ref[at + 1].astype(F32) * norm
    loss_ref[...] = total[0:1, LOSS_LANE : LOSS_LANE + 1] * norm
    by_tap = jnp.concatenate([total * norm, jnp.zeros((CH - 8, CH), F32)], axis=0).T
    for a in range(3):
        for b in range(3):
            at = 9 * a + 3 * b
            weight_ref[a, b] = by_tap[at : at + 3, 0:8]


def call(kernel, out_shape, *args, scratch=(), flops=0, params=VMEM):
    cost = pl.CostEstimate(flops=flops, bytes_accessed=1 << 20, transcendentals=0)
    return pl.pallas_call(
        kernel, out_shape=out_shape, scratch_shapes=list(scratch), compiler_params=params, cost_estimate=cost
    )(*args)


def swapped(value):
    return lax.ppermute(value, "wa", [(i, i ^ 1) for i in range(WA)])


def shards(left_feat, right_feat, conv_weight, disparity_gt, valid_mask):
    left, right = left_feat[0], right_feat[0]
    gt, valid = disparity_gt[0], valid_mask[0]
    ha_count = lax.axis_size("ha")
    halo = jax.ShapeDtypeStruct((5, TILE, CH), BF16)
    own = jax.ShapeDtypeStruct((2 * ROWS + 1, TILE, CH), BF16)
    args = (left, right, gt, valid, jnp.transpose(conv_weight, (1, 2, 3, 0)))
    up, down, own, taps = pl.pallas_call(
        halo_kernel,
        out_shape=(halo, halo, own, jax.ShapeDtypeStruct((3, 16, CH), F32)),
        in_specs=[pl.BlockSpec(memory_space=pltpu.HBM)] * 5,
        scratch_shapes=[
            pltpu.VMEM((ROWS, TILE, CH), BF16),
            pltpu.VMEM((ROWS, TILE, CH), BF16),
            pltpu.VMEM((ROWS, TILE), jnp.int32),
            pltpu.VMEM((ROWS, TILE), jnp.int32),
            pltpu.VMEM((3, 3, 3, 8), F32),
            pltpu.SemaphoreType.DMA((5,)),
        ],
        compiler_params=VMEM,
    )(*[pltpu.with_memory_space_constraint(arg, pltpu.HBM) for arg in args])
    before = lax.ppermute(up, "ha", [(i, (i + 1) % ha_count) for i in range(ha_count)])
    after = lax.ppermute(down, "ha", [((i + 1) % ha_count, i) for i in range(ha_count)])
    block = jax.ShapeDtypeStruct((13, TILE, CH), BF16)
    blocks = call(
        pack_kernel,
        (block,) * CHIPS,
        own,
        before,
        after,
        scratch=(pltpu.VMEM((24, TILE, CH), BF16),),
    )
    same_core = [blocks[0]]
    for hop in range(1, CHIPS):
        same_core.append(lax.ppermute(blocks[hop], "wa", [(i, (i + 2 * hop) % WA) for i in range(WA)]))
    other_core = [lax.ppermute(value, "wa", [(i, i ^ 1) for i in range(WA)]) for value in same_core]
    tiles = same_core + other_core
    others = lax.axis_size("dp") * ha_count * WA
    half = jax.ShapeDtypeStruct((8, TILE, CH), BF16)
    sums, kept, given = pl.pallas_call(
        main_kernel,
        out_shape=(jax.ShapeDtypeStruct((others, 2, CH), F32), half, half),
        out_specs=(pl.BlockSpec(memory_space=pltpu.HBM), pl.BlockSpec(memory_space=pltpu.VMEM), pl.BlockSpec(memory_space=pltpu.VMEM)),
        scratch_shapes=(
            pltpu.VMEM((5, WT + 16, CH), F32),
            pltpu.VMEM((5, WT + 80, CH), F32),
            pltpu.VMEM((JP, 25 * CH), BF16),
            pltpu.VMEM((WT, CH), F32),
            pltpu.VMEM((5, 9 * WT, 5 * CH), BF16),
            pltpu.VMEM((3, WT, JP), F32),
            pltpu.VMEM((6 * WT, JP), BF16),
            pltpu.VMEM((3, WT, CH), F32),
            pltpu.VMEM((CH, CH), F32),
            pltpu.VMEM((2 * WT, 3 * CH), BF16),
            pltpu.VMEM((6, WT + 16, CH), F32),
            pltpu.VMEM((5, JP, CH), F32),
            pltpu.VMEM((WA, 2, TILE, CH), BF16),
            pltpu.VMEM((others, 2, CH), F32),
            pltpu.SemaphoreType.DMA,
        ),
        compiler_params=VMEM,
        cost_estimate=pl.CostEstimate(flops=5 << 30, bytes_accessed=1 << 20, transcendentals=0),
    )(*tiles, taps)
    sums = lax.all_to_all(sums, ("dp", "ha", "wa"), 0, 0, tiled=True)
    got = swapped(given)
    block = jax.ShapeDtypeStruct((4, TILE, CH), BF16)
    (opposite,) = call(functools.partial(pack_back_kernel, (2,)), (block,), kept, got)
    across = lax.ppermute(opposite, "wa", [(i, (i + 4) % WA) for i in range(WA)])
    beside, beside_other = call(
        functools.partial(pack_back_kernel, (0, 1)), (block,) * 2, kept, got, opposite, flops=1 << 31
    )
    near = lax.ppermute(beside, "wa", [(i, (i + 2 - 4 * (i % 2)) % WA) for i in range(WA)])
    far = lax.ppermute(beside_other, "wa", [(i, (i + 3 - 6 * (i % 2)) % WA) for i in range(WA)])
    tile = jax.ShapeDtypeStruct((ROWS, TILE, CH), F32)
    grad_left, grad_right, weight, loss = call(
        finish_kernel,
        (tile, tile, jax.ShapeDtypeStruct((3, 3, 3, 8), F32), jax.ShapeDtypeStruct((1, 1), F32)),
        kept,
        got,
        near,
        far,
        across,
        sums,
    )
    return (loss[0, 0], grad_left[None], grad_right[None], jnp.transpose(weight, (3, 0, 1, 2)))


def solution(mesh):
    placed = (
        P("dp", "ha", "wa", None),
        P("dp", "ha", "wa", None),
        P(),
        P("dp", "ha", "wa"),
        P("dp", "ha", "wa"),
    )
    return jax.shard_map(
        shards,
        mesh=mesh,
        in_specs=placed,
        out_specs=(P(), P("dp", "ha", "wa", None), P("dp", "ha", "wa", None), P()),
        check_vma=False,
    )
```

```python
import functools

import jax
import jax.numpy as jnp
from jax import lax
from jax.experimental import pallas as pl
from jax.experimental.pallas import tpu as pltpu
from jax.sharding import PartitionSpec as P

F32 = jnp.float32
BF16 = jnp.bfloat16
ROWS, TILE, CH = 8, 24, 128
WA, CHIPS = 8, 4
WT = 192
JP = 256
GT_LANE, VALID_LANE = 0, 16
LOSS_LANE, COUNT_LANE, SHARE = 27, 28, 32
VMEM = pltpu.CompilerParams(vmem_limit_bytes=48 * 1024 * 1024)
NT = (((1,), (1,)), ((), ()))
NN = (((1,), (0,)), ((), ()))
TN = (((0,), (0,)), ((), ()))


def dot(lhs, rhs, dims=NN, precision=None):
    return lax.dot_general(lhs, rhs, dims, precision=precision, preferred_element_type=F32)


def meta_block(gt, valid, first, count, lane_of_first):
    row = lax.broadcasted_iota(jnp.int32, (ROWS, CH), 0)
    lane = lax.broadcasted_iota(jnp.int32, (ROWS, CH), 1)
    chosen = (row >= first) & (row < first + count)
    at = row - first + lane_of_first
    pick_gt = (chosen & (lane == at + GT_LANE)).astype(F32)
    pick_valid = (chosen & (lane == at + VALID_LANE)).astype(F32)
    return dot(gt, pick_gt, TN) + dot(valid, pick_valid, TN)


def copied_in(sources, refs, sems):
    copies = [pltpu.make_async_copy(src, dst, sems.at[i]) for i, (src, dst) in enumerate(zip(sources, refs))]
    for copy in copies:
        copy.start()
    for copy in copies:
        copy.wait()


def halo_kernel(left_any, right_any, gt_any, valid_any, up_ref, down_ref, *scratch):
    refs, sems = scratch[:4], scratch[4]
    copied_in((left_any, right_any, gt_any, valid_any), refs, sems)
    left_ref, right_ref, gt_ref, valid_ref = refs
    gt = gt_ref[...].astype(F32)
    valid = valid_ref[...].astype(F32)
    for side, ref in ((0, left_ref), (1, right_ref)):
        for i in range(2):
            up_ref[2 * side + i] = ref[ROWS - 2 + i]
            down_ref[2 * side + i] = ref[i]
    up_ref[4] = meta_block(gt, valid, ROWS - 2, 2, 0).astype(BF16)
    down_ref[4] = meta_block(gt, valid, 0, 2, ROWS + 2).astype(BF16)


def own_tile_kernel(left_any, right_any, gt_any, valid_any, weight_any, own_ref, taps_ref, *scratch):
    refs, sems = scratch[:5], scratch[5]
    copied_in((left_any, right_any, gt_any, valid_any, weight_any), refs, sems)
    left_ref, right_ref, gt_ref, valid_ref, weight_ref = refs
    for side, ref in ((0, left_ref), (1, right_ref)):
        for i in range(ROWS):
            own_ref[ROWS * side + i] = ref[i]
    own_ref[2 * ROWS] = meta_block(gt_ref[...].astype(F32), valid_ref[...].astype(F32), 0, ROWS, 2).astype(BF16)
    member = group_member() * (1.0 / 16.0)
    for a in range(3):
        taps = jnp.concatenate([weight_ref[a, b] for b in range(3)], axis=0)
        taps_ref[a, 0:9] = dot(taps, member, precision=lax.Precision.HIGHEST)


def group_member():
    group = lax.broadcasted_iota(jnp.int32, (8, CH), 0)
    channel = lax.broadcasted_iota(jnp.int32, (8, CH), 1)
    return (lax.shift_right_logical(channel, 4) == group).astype(F32)


def position():
    index = lax.axis_index("wa")
    return lax.shift_right_logical(index, 1), index & 1


def pack_kernel(own_ref, prev_ref, next_ref, *refs):
    outs, ext = refs[:CHIPS], refs[CHIPS]
    chip, _ = position()
    band = lax.axis_index("ha")
    has_prev = band > 0
    has_next = band < lax.axis_size("ha") - 1

    def of_prev(i):
        return jnp.where(has_prev, prev_ref[i], jnp.zeros((TILE, CH), BF16))

    def of_next(i):
        return jnp.where(has_next, next_ref[i], jnp.zeros((TILE, CH), BF16))

    meta = own_ref[2 * ROWS].astype(F32)
    meta = (meta + of_prev(4).astype(F32) + of_next(4).astype(F32)).astype(BF16)
    for side in range(2):
        for i in range(2):
            ext[12 * side + i] = of_prev(2 * side + i)
            ext[12 * side + ROWS + 2 + i] = of_next(2 * side + i)
        for i in range(ROWS):
            ext[12 * side + 2 + i] = own_ref[ROWS * side + i]
    for hop in range(CHIPS):
        first = 2 * ((chip + hop) & (CHIPS - 1))
        for i in range(6):
            outs[hop][i] = ext[first + i]
            outs[hop][6 + i] = ext[first + 12 + i]
        outs[hop][12] = meta


def split3(value):
    high = value.astype(BF16)
    rest = value - high.astype(F32)
    middle = rest.astype(BF16)
    low = (rest - middle.astype(F32)).astype(BF16)
    return high, middle, low


def fill(refs, first, count, ls, rs, rb):
    chip, core = position()
    tiles = []
    for hop in range(CHIPS):
        tile = 2 * ((chip - hop) & (CHIPS - 1))
        tiles.append((refs[hop], pl.multiple_of(8 + TILE * (tile + core), 8)))
        tiles.append((refs[CHIPS + hop], pl.multiple_of(8 + TILE * (tile + 1 - core), 8)))

    @pl.loop(first, first + count)
    def row(rho):
        ls[rho, 0:8] = jnp.zeros((8, CH), F32)
        ls[rho, 8 + WT :] = jnp.zeros((8, CH), F32)
        rs[rho, 0:8] = jnp.zeros((8, CH), F32)
        rs[rho, 8 + WT :] = jnp.zeros((72, CH), F32)
        for ref, at in tiles:
            ls[rho, pl.ds(at, TILE)] = ref[core + rho].astype(F32)
            rs[rho, pl.ds(at, TILE)] = ref[6 + core + rho].astype(F32)
        for si in range(5):
            rb[:, pl.ds(pl.multiple_of((5 * rho + si) * CH, CH), CH)] = rs[rho, 4 + si : 4 + si + JP].astype(BF16)

    return tiles


def fill_meta(tiles, ms):
    for ref, at in tiles:
        ms[pl.ds(at - 8, TILE)] = ref[12].astype(F32)


def split2(value):
    high = value.astype(BF16)
    return high, (value - high.astype(F32)).astype(BF16)


def weighted(a, left, wc_ref, ab, at):
    for si in range(5):
        value = None
        for b in range(3):
            e = b - (si - 2)
            if 0 <= e <= 2:
                term = wc_ref[a, 3 * b + e : 3 * b + e + 1] * left[b]
                value = term if value is None else value + term
        for i, part in enumerate(split3(value)):
            ab[at + i * WT : at + (i + 1) * WT, si * CH : (si + 1) * CH] = part


def row_gradient(q, logits, diag_col, ms, masks):
    lane, level, inside, on_diag, wcol, zeros_count, zeros_mean = masks
    logits = logits - jnp.where(on_diag, diag_col, 0.0)
    top = jnp.max(jnp.where(inside, logits, -3e38), axis=1, keepdims=True)
    top = jnp.where(zeros_count > 0.0, jnp.maximum(top, 0.0), top)
    expd = jnp.where(inside, jnp.exp(logits - top), 0.0)
    zero_exp = jnp.where(zeros_count > 0.0, zeros_count * jnp.exp(-top), 0.0)
    denom = jnp.sum(expd, axis=1, keepdims=True) + zero_exp
    first = jnp.sum(expd * level, axis=1, keepdims=True) + zero_exp * zeros_mean
    inv = 1.0 / denom
    estimate = first * inv
    ext = lax.axis_index("wa") + 1 + q
    meta = ms[...]
    target = jnp.sum(jnp.where(lane == GT_LANE + ext, meta, 0.0), axis=1, keepdims=True)
    valid = jnp.sum(jnp.where(lane == VALID_LANE + ext, meta, 0.0), axis=1, keepdims=True)
    usable = jnp.where(target <= wcol, valid, 0.0)
    resid = estimate - target
    factor = jnp.clip(resid, -1.0, 1.0) * usable * inv
    return expd * (level - estimate) * factor, resid, usable


def diagonal(up, on_diag):
    return jnp.sum(jnp.where(on_diag, up, 0.0), axis=1, keepdims=True)


def row_masks():
    lane = lax.broadcasted_iota(jnp.int32, (WT, CH), 1)
    ww = lax.broadcasted_iota(jnp.int32, (WT, JP), 0)
    jj = lax.broadcasted_iota(jnp.int32, (WT, JP), 1)
    level = (ww - jj + 2).astype(F32)
    inside = (jj <= ww + 2) & (jj >= ww - (WT - 3))
    on_diag = jj == ww + 2
    wcol = lax.broadcasted_iota(jnp.int32, (WT, 1), 0).astype(F32)
    zeros_count = jnp.maximum(float(WT - 3) - wcol, 0.0)
    zeros_mean = (wcol + float(WT + 2)) * 0.5
    return lane, level, inside, on_diag, wcol, zeros_count, zeros_mean


def logits_of(ls, rb, wc_ref, ab, acc):
    for rho in range(5):
        rows = [q for q in range(3) if 0 <= rho - q <= 2]
        left = [ls[rho, 7 + b : 7 + b + WT] for b in range(3)]
        for i, q in enumerate(rows):
            weighted(rho - q, left, wc_ref, ab.at[rho], 3 * WT * i)
        part = dot(ab[rho, 0 : 3 * WT * len(rows)], rb[:, 5 * rho * CH : 5 * (rho + 1) * CH], NT)
        for i, q in enumerate(rows):
            at = 3 * WT * i
            total = part[at : at + WT] + part[at + WT : at + 2 * WT] + part[at + 2 * WT : at + 3 * WT]
            acc[q] = total if rho == q else acc[q] + total


def main_kernel(*refs):
    recv, wc_ref = refs[:8], refs[8]
    sums_ref, kept_ref, given_ref = refs[9:12]
    ls, rs, rb, ms, ab, acc, ub, diags, ks, lb, xs, ys, out_ref, fanned, sem = refs[12:]
    fill_meta(fill(recv, 0, 5, ls, rs, rb), ms)
    ks[...] = jnp.zeros(ks.shape, F32)
    xs[...] = jnp.zeros(xs.shape, F32)
    masks = row_masks()
    logits_of(ls, rb, wc_ref, ab, acc)
    for q in range(3):
        diag = None
        for a in range(3):
            for b in range(3):
                term = wc_ref[a, 3 * b : 3 * b + 1] * ls[q + a, 7 + b : 7 + b + WT] * rs[q + a, 8 + b : 8 + b + WT]
                diag = term if diag is None else diag + term
        up, resid, usable = row_gradient(q, acc[q], jnp.sum(diag, axis=1, keepdims=True), ms, masks)
        ub[2 * WT * q : 2 * WT * q + WT], ub[2 * WT * q + WT : 2 * WT * (q + 1)] = split2(up)
        diags[q] = jnp.broadcast_to(diagonal(up, masks[3]), (WT, CH))
        if q == 1:
            size = jnp.abs(resid)
            smooth = jnp.where(size < 1.0, 0.5 * resid * resid, size - 0.5)
            loss_sum = jnp.sum(usable * smooth, axis=0, keepdims=True)
            count_sum = jnp.sum(usable, axis=0, keepdims=True)
    for b in range(3):
        shifted = ls[2, 7 + b : 7 + b + WT].astype(BF16)
        lb[0:WT, b * CH : (b + 1) * CH] = shifted
        lb[WT:, b * CH : (b + 1) * CH] = shifted

    def tap(q, b, e):
        return wc_ref[2 - q, 3 * b + e : 3 * b + e + 1]

    terms = dot(ub[...], rb[:, 10 * CH : 15 * CH])
    for b in range(3):
        own_left, own_right = ls[2, 7 + b : 7 + b + WT], rs[2, 8 + b : 8 + b + WT]
        total = None
        spread = None
        for q in range(3):
            term = tap(q, b, 0) * diags[q]
            spread = term if spread is None else spread + term
            for e in range(3):
                at, si = 2 * WT * q, b - e + 2
                value = terms[at : at + WT, si * CH : (si + 1) * CH]
                value = value + terms[at + WT : at + 2 * WT, si * CH : (si + 1) * CH]
                if e == 0:
                    value = value - diags[q] * own_right
                at = 9 * (2 - q) + 3 * b + e
                ks[at : at + 1] = jnp.sum(own_left * value, axis=0, keepdims=True)
                term = tap(q, b, e) * value
                total = term if total is None else total + term
        xs[b, 8 : 8 + WT] = total
        xs[3 + b, 8 : 8 + WT] = spread * own_left
    channel = lax.broadcasted_iota(jnp.int32, (8, CH), 1)
    member = group_member().astype(BF16)
    parts = [dot(member, part, NT) for part in split3(ks[...])]
    sums = (parts[0] + (parts[1] + parts[2])) * (1.0 / 16.0)
    sums = jnp.where(channel == LOSS_LANE, loss_sum, sums)
    sums = jnp.where(channel == COUNT_LANE, count_sum, sums)
    sums = jnp.where(channel < SHARE, sums, 0.0)
    quarter = lax.broadcasted_iota(jnp.int32, (8, CH), 0) & 3
    placed = jnp.where(quarter == 0, sums, 0.0)
    for i in range(1, 4):
        placed = placed + jnp.where(quarter == i, pltpu.roll(sums, SHARE * i, 1), 0.0)
    packed = jnp.concatenate([jnp.sum(placed[4 * i : 4 * i + 4], axis=0, keepdims=True) for i in range(2)], axis=0)
    for i in range(sums_ref.shape[0]):
        fanned[i] = packed
    sending = pltpu.make_async_copy(fanned, sums_ref, sem)
    sending.start()
    for q in range(3):
        terms = dot(ub[2 * WT * q : 2 * WT * (q + 1)], lb[...], TN)
        for si in range(5):
            total = None
            for b in range(3):
                e = b - (si - 2)
                if 0 <= e <= 2:
                    term = tap(q, b, e) * terms[:, b * CH : (b + 1) * CH]
                    total = term if total is None else total + term
            ys[si] = total if q == 0 else ys[si] + total
    grad_left = xs[0, 9 : 9 + WT] + xs[1, 8 : 8 + WT] + xs[2, 7 : 7 + WT]
    grad_right = ys[0, 4 : 4 + WT]
    for si in range(1, 5):
        grad_right = grad_right + ys[si, 4 - si : 4 - si + WT]
    for b in range(3):
        grad_right = grad_right - xs[3 + b, 8 - b : 8 - b + WT]
    for dst in range(WA):
        out_ref[dst, 0] = grad_left[TILE * dst : TILE * (dst + 1)].astype(BF16)
        out_ref[dst, 1] = grad_right[TILE * dst : TILE * (dst + 1)].astype(BF16)
    chip, core = position()
    for ref, holder in ((kept_ref, core), (given_ref, 1 - core)):
        beside = chip_at(chip, ahead(holder))
        opposite = chip_at(chip, 2)
        places = (2 * beside + holder, 2 * beside + 1 - holder, 2 * opposite + holder, 2 * chip + holder)
        for i, tile in enumerate(places):
            for side in range(2):
                ref[2 * i + side] = out_ref[tile, side]
    sending.wait()


def ahead(core):
    return 1 - 2 * core


def chip_at(chip, step):
    return (chip + step + CHIPS) & (CHIPS - 1)


def pack_back_kernel(places, kept_ref, got_ref, *refs):
    for place, out_ref in zip(places, refs[-len(places) :]):
        for row, ref in enumerate((kept_ref, got_ref)):
            for side in range(2):
                out_ref[2 * row + side] = ref[2 * place + side]


def finish_kernel(kept, got, near, far, across, sums_ref, left_ref, right_ref, weight_ref, loss_ref):
    chip, core = position()
    other = 1 - core
    before, after, opposite = chip_at(chip, -ahead(core)), chip_at(chip, ahead(core)), chip_at(chip, 2)
    partial = [sums_ref[i] for i in range(8)]
    for i in range(8, sums_ref.shape[0]):
        partial[i % 8] = partial[i % 8] + sums_ref[i]
    while len(partial) > 1:
        partial = [x + y for x, y in zip(partial[0::2], partial[1::2])]
    placed = partial[0]
    total = jnp.concatenate(
        [pltpu.roll(jnp.broadcast_to(placed[g // 4 : g // 4 + 1], (8, CH)), (CH - SHARE * (g % 4)) % CH, 1)[0:1] for g in range(8)],
        axis=0,
    )
    norm = 1.0 / jnp.maximum(total[0:1, COUNT_LANE : COUNT_LANE + 1], 1.0)
    blocks = (
        (kept, 6, 2 * chip + core),
        (got, 6, 2 * chip + other),
        (near, 0, 2 * before + core),
        (near, 2, 2 * before + other),
        (far, 0, 2 * after + other),
        (far, 2, 2 * after + core),
        (across, 0, 2 * opposite + core),
        (across, 2, 2 * opposite + other),
    )
    for ref, at, row in blocks:
        left_ref[row] = ref[at].astype(F32) * norm
        right_ref[row] = ref[at + 1].astype(F32) * norm
    loss_ref[...] = total[0:1, LOSS_LANE : LOSS_LANE + 1] * norm
    by_tap = jnp.concatenate([total * norm, jnp.zeros((CH - 8, CH), F32)], axis=0).T
    for a in range(3):
        for b in range(3):
            at = 9 * a + 3 * b
            weight_ref[a, b] = by_tap[at : at + 3, 0:8]


def call(kernel, out_shape, *args, scratch=(), flops=0, params=VMEM):
    cost = pl.CostEstimate(flops=flops, bytes_accessed=1 << 20, transcendentals=0)
    return pl.pallas_call(
        kernel, out_shape=out_shape, scratch_shapes=list(scratch), compiler_params=params, cost_estimate=cost
    )(*args)


def swapped(value):
    return lax.ppermute(value, "wa", [(i, i ^ 1) for i in range(WA)])


def shards(left_feat, right_feat, conv_weight, disparity_gt, valid_mask):
    left, right = left_feat[0], right_feat[0]
    gt, valid = disparity_gt[0], valid_mask[0]
    ha_count = lax.axis_size("ha")
    halo = jax.ShapeDtypeStruct((5, TILE, CH), BF16)
    own = jax.ShapeDtypeStruct((2 * ROWS + 1, TILE, CH), BF16)
    args = (left, right, gt, valid, jnp.transpose(conv_weight, (1, 2, 3, 0)))
    args = [pltpu.with_memory_space_constraint(arg, pltpu.HBM) for arg in args]
    arg_copies = (
        pltpu.VMEM((ROWS, TILE, CH), BF16),
        pltpu.VMEM((ROWS, TILE, CH), BF16),
        pltpu.VMEM((ROWS, TILE), jnp.int32),
        pltpu.VMEM((ROWS, TILE), jnp.int32),
        pltpu.VMEM((3, 3, 3, 8), F32),
    )
    up, down = pl.pallas_call(
        halo_kernel,
        out_shape=(halo, halo),
        in_specs=[pl.BlockSpec(memory_space=pltpu.HBM)] * 4,
        scratch_shapes=arg_copies[:4] + (pltpu.SemaphoreType.DMA((4,)),),
        compiler_params=VMEM,
    )(*args[:4])
    own, taps = pl.pallas_call(
        own_tile_kernel,
        out_shape=(own, jax.ShapeDtypeStruct((3, 16, CH), F32)),
        in_specs=[pl.BlockSpec(memory_space=pltpu.HBM)] * 5,
        scratch_shapes=arg_copies + (pltpu.SemaphoreType.DMA((5,)),),
        compiler_params=VMEM,
        cost_estimate=pl.CostEstimate(flops=1 << 30, bytes_accessed=1 << 18, transcendentals=0),
    )(*args)
    before = lax.ppermute(up, "ha", [(i, (i + 1) % ha_count) for i in range(ha_count)])
    after = lax.ppermute(down, "ha", [((i + 1) % ha_count, i) for i in range(ha_count)])
    block = jax.ShapeDtypeStruct((13, TILE, CH), BF16)
    blocks = call(
        pack_kernel,
        (block,) * CHIPS,
        own,
        before,
        after,
        scratch=(pltpu.VMEM((24, TILE, CH), BF16),),
    )
    same_core = [blocks[0]]
    for hop in range(1, CHIPS):
        same_core.append(lax.ppermute(blocks[hop], "wa", [(i, (i + 2 * hop) % WA) for i in range(WA)]))
    other_core = [lax.ppermute(value, "wa", [(i, i ^ 1) for i in range(WA)]) for value in same_core]
    tiles = same_core + other_core
    others = lax.axis_size("dp") * ha_count * WA
    half = jax.ShapeDtypeStruct((8, TILE, CH), BF16)
    sums, kept, given = pl.pallas_call(
        main_kernel,
        out_shape=(jax.ShapeDtypeStruct((others, 2, CH), F32), half, half),
        out_specs=(pl.BlockSpec(memory_space=pltpu.HBM), pl.BlockSpec(memory_space=pltpu.VMEM), pl.BlockSpec(memory_space=pltpu.VMEM)),
        scratch_shapes=(
            pltpu.VMEM((5, WT + 16, CH), F32),
            pltpu.VMEM((5, WT + 80, CH), F32),
            pltpu.VMEM((JP, 25 * CH), BF16),
            pltpu.VMEM((WT, CH), F32),
            pltpu.VMEM((5, 9 * WT, 5 * CH), BF16),
            pltpu.VMEM((3, WT, JP), F32),
            pltpu.VMEM((6 * WT, JP), BF16),
            pltpu.VMEM((3, WT, CH), F32),
            pltpu.VMEM((CH, CH), F32),
            pltpu.VMEM((2 * WT, 3 * CH), BF16),
            pltpu.VMEM((6, WT + 16, CH), F32),
            pltpu.VMEM((5, JP, CH), F32),
            pltpu.VMEM((WA, 2, TILE, CH), BF16),
            pltpu.VMEM((others, 2, CH), F32),
            pltpu.SemaphoreType.DMA,
        ),
        compiler_params=VMEM,
        cost_estimate=pl.CostEstimate(flops=5 << 30, bytes_accessed=1 << 20, transcendentals=0),
    )(*tiles, taps)
    sums = lax.all_to_all(sums, ("dp", "ha", "wa"), 0, 0, tiled=True)
    got = swapped(given)
    block = jax.ShapeDtypeStruct((4, TILE, CH), BF16)
    (opposite,) = call(functools.partial(pack_back_kernel, (2,)), (block,), kept, got)
    across = lax.ppermute(opposite, "wa", [(i, (i + 4) % WA) for i in range(WA)])
    beside, beside_other = call(
        functools.partial(pack_back_kernel, (0, 1)), (block,) * 2, kept, got, opposite, flops=1 << 31
    )
    near = lax.ppermute(beside, "wa", [(i, (i + 2 - 4 * (i % 2)) % WA) for i in range(WA)])
    far = lax.ppermute(beside_other, "wa", [(i, (i + 3 - 6 * (i % 2)) % WA) for i in range(WA)])
    tile = jax.ShapeDtypeStruct((ROWS, TILE, CH), F32)
    grad_left, grad_right, weight, loss = call(
        finish_kernel,
        (tile, tile, jax.ShapeDtypeStruct((3, 3, 3, 8), F32), jax.ShapeDtypeStruct((1, 1), F32)),
        kept,
        got,
        near,
        far,
        across,
        sums,
    )
    return (loss[0, 0], grad_left[None], grad_right[None], jnp.transpose(weight, (3, 0, 1, 2)))


def solution(mesh):
    placed = (
        P("dp", "ha", "wa", None),
        P("dp", "ha", "wa", None),
        P(),
        P("dp", "ha", "wa"),
        P("dp", "ha", "wa"),
    )
    return jax.shard_map(
        shards,
        mesh=mesh,
        in_specs=placed,
        out_specs=(P(), P("dp", "ha", "wa", None), P("dp", "ha", "wa", None), P()),
        check_vma=False,
    )
```

```python
import functools

import jax
import jax.numpy as jnp
from jax import lax
from jax.experimental import pallas as pl
from jax.experimental.pallas import tpu as pltpu
from jax.sharding import PartitionSpec as P

F32 = jnp.float32
BF16 = jnp.bfloat16
ROWS, TILE, CH = 8, 24, 128
WA, CHIPS = 8, 4
WT = 192
JP = 256
GT_LANE, VALID_LANE = 0, 16
LOSS_LANE, COUNT_LANE, SHARE = 27, 28, 32
VMEM = pltpu.CompilerParams(vmem_limit_bytes=48 * 1024 * 1024)
NT = (((1,), (1,)), ((), ()))
NN = (((1,), (0,)), ((), ()))
TN = (((0,), (0,)), ((), ()))


def dot(lhs, rhs, dims=NN, precision=None):
    return lax.dot_general(lhs, rhs, dims, precision=precision, preferred_element_type=F32)


def meta_block(gt, valid, first, count, lane_of_first):
    row = lax.broadcasted_iota(jnp.int32, (ROWS, CH), 0)
    lane = lax.broadcasted_iota(jnp.int32, (ROWS, CH), 1)
    chosen = (row >= first) & (row < first + count)
    at = row - first + lane_of_first
    pick_gt = (chosen & (lane == at + GT_LANE)).astype(F32)
    pick_valid = (chosen & (lane == at + VALID_LANE)).astype(F32)
    return dot(gt, pick_gt, TN) + dot(valid, pick_valid, TN)


def halo_kernel(left_any, right_any, gt_any, valid_any, weight_any, up_ref, down_ref, own_ref, taps_ref, *scratch):
    refs, sems = scratch[:5], scratch[5]
    sources = (left_any, right_any, gt_any, valid_any, weight_any)
    copies = [pltpu.make_async_copy(src, dst, sems.at[i]) for i, (src, dst) in enumerate(zip(sources, refs))]
    for copy in copies:
        copy.start()
    for copy in copies:
        copy.wait()
    left_ref, right_ref, gt_ref, valid_ref, weight_ref = refs
    gt = gt_ref[...].astype(F32)
    valid = valid_ref[...].astype(F32)
    for side, ref in ((0, left_ref), (1, right_ref)):
        for i in range(2):
            up_ref[2 * side + i] = ref[ROWS - 2 + i]
            down_ref[2 * side + i] = ref[i]
        for i in range(ROWS):
            own_ref[ROWS * side + i] = ref[i]
    up_ref[4] = meta_block(gt, valid, ROWS - 2, 2, 0).astype(BF16)
    down_ref[4] = meta_block(gt, valid, 0, 2, ROWS + 2).astype(BF16)
    own_ref[2 * ROWS] = meta_block(gt, valid, 0, ROWS, 2).astype(BF16)
    member = group_member() * (1.0 / 16.0)
    for a in range(3):
        taps = jnp.concatenate([weight_ref[a, b] for b in range(3)], axis=0)
        taps_ref[a, 0:9] = dot(taps, member, precision=lax.Precision.HIGHEST)


def group_member():
    group = lax.broadcasted_iota(jnp.int32, (8, CH), 0)
    channel = lax.broadcasted_iota(jnp.int32, (8, CH), 1)
    return (lax.shift_right_logical(channel, 4) == group).astype(F32)


def position():
    index = lax.axis_index("wa")
    return lax.shift_right_logical(index, 1), index & 1


def pack_kernel(hops, own_ref, prev_ref, next_ref, *refs):
    outs, ext = refs[-1 - len(hops) : -1], refs[-1]
    chip, _ = position()
    band = lax.axis_index("ha")
    has_prev = band > 0
    has_next = band < lax.axis_size("ha") - 1

    def of_prev(i):
        return jnp.where(has_prev, prev_ref[i], jnp.zeros((TILE, CH), BF16))

    def of_next(i):
        return jnp.where(has_next, next_ref[i], jnp.zeros((TILE, CH), BF16))

    meta = own_ref[2 * ROWS].astype(F32)
    meta = (meta + of_prev(4).astype(F32) + of_next(4).astype(F32)).astype(BF16)
    for side in range(2):
        for i in range(2):
            ext[12 * side + i] = of_prev(2 * side + i)
            ext[12 * side + ROWS + 2 + i] = of_next(2 * side + i)
        for i in range(ROWS):
            ext[12 * side + 2 + i] = own_ref[ROWS * side + i]
    for hop, out_ref in zip(hops, outs):
        first = 2 * ((chip + hop) & (CHIPS - 1))
        for i in range(6):
            out_ref[i] = ext[first + i]
            out_ref[6 + i] = ext[first + 12 + i]
        out_ref[12] = meta


def split3(value):
    high = value.astype(BF16)
    rest = value - high.astype(F32)
    middle = rest.astype(BF16)
    low = (rest - middle.astype(F32)).astype(BF16)
    return high, middle, low


def fill(refs, first, count, ls, rs, rb):
    chip, core = position()
    tiles = []
    for hop in range(CHIPS):
        tile = 2 * ((chip - hop) & (CHIPS - 1))
        tiles.append((refs[hop], pl.multiple_of(8 + TILE * (tile + core), 8)))
        tiles.append((refs[CHIPS + hop], pl.multiple_of(8 + TILE * (tile + 1 - core), 8)))

    @pl.loop(first, first + count)
    def row(rho):
        ls[rho, 0:8] = jnp.zeros((8, CH), F32)
        ls[rho, 8 + WT :] = jnp.zeros((8, CH), F32)
        rs[rho, 0:8] = jnp.zeros((8, CH), F32)
        rs[rho, 8 + WT :] = jnp.zeros((72, CH), F32)
        for ref, at in tiles:
            ls[rho, pl.ds(at, TILE)] = ref[core + rho].astype(F32)
            rs[rho, pl.ds(at, TILE)] = ref[6 + core + rho].astype(F32)
        for si in range(5):
            rb[:, pl.ds(pl.multiple_of((5 * rho + si) * CH, CH), CH)] = rs[rho, 4 + si : 4 + si + JP].astype(BF16)

    return tiles


def fill_meta(tiles, ms):
    for ref, at in tiles:
        ms[pl.ds(at - 8, TILE)] = ref[12].astype(F32)


def split2(value):
    high = value.astype(BF16)
    return high, (value - high.astype(F32)).astype(BF16)


def weighted(a, left, wc_ref, ab, at):
    for si in range(5):
        value = None
        for b in range(3):
            e = b - (si - 2)
            if 0 <= e <= 2:
                term = wc_ref[a, 3 * b + e : 3 * b + e + 1] * left[b]
                value = term if value is None else value + term
        for i, part in enumerate(split3(value)):
            ab[at + i * WT : at + (i + 1) * WT, si * CH : (si + 1) * CH] = part


def row_gradient(q, logits, diag_col, ms, masks):
    lane, level, inside, on_diag, wcol, zeros_count, zeros_mean = masks
    logits = logits - jnp.where(on_diag, diag_col, 0.0)
    top = jnp.max(jnp.where(inside, logits, -3e38), axis=1, keepdims=True)
    top = jnp.where(zeros_count > 0.0, jnp.maximum(top, 0.0), top)
    expd = jnp.where(inside, jnp.exp(logits - top), 0.0)
    zero_exp = jnp.where(zeros_count > 0.0, zeros_count * jnp.exp(-top), 0.0)
    denom = jnp.sum(expd, axis=1, keepdims=True) + zero_exp
    first = jnp.sum(expd * level, axis=1, keepdims=True) + zero_exp * zeros_mean
    inv = 1.0 / denom
    estimate = first * inv
    ext = lax.axis_index("wa") + 1 + q
    meta = ms[...]
    target = jnp.sum(jnp.where(lane == GT_LANE + ext, meta, 0.0), axis=1, keepdims=True)
    valid = jnp.sum(jnp.where(lane == VALID_LANE + ext, meta, 0.0), axis=1, keepdims=True)
    usable = jnp.where(target <= wcol, valid, 0.0)
    resid = estimate - target
    factor = jnp.clip(resid, -1.0, 1.0) * usable * inv
    return expd * (level - estimate) * factor, resid, usable


def diagonal(up, on_diag):
    return jnp.sum(jnp.where(on_diag, up, 0.0), axis=1, keepdims=True)


def row_masks():
    lane = lax.broadcasted_iota(jnp.int32, (WT, CH), 1)
    ww = lax.broadcasted_iota(jnp.int32, (WT, JP), 0)
    jj = lax.broadcasted_iota(jnp.int32, (WT, JP), 1)
    level = (ww - jj + 2).astype(F32)
    inside = (jj <= ww + 2) & (jj >= ww - (WT - 3))
    on_diag = jj == ww + 2
    wcol = lax.broadcasted_iota(jnp.int32, (WT, 1), 0).astype(F32)
    zeros_count = jnp.maximum(float(WT - 3) - wcol, 0.0)
    zeros_mean = (wcol + float(WT + 2)) * 0.5
    return lane, level, inside, on_diag, wcol, zeros_count, zeros_mean


def logits_of(ls, rb, wc_ref, ab, acc):
    for rho in range(5):
        rows = [q for q in range(3) if 0 <= rho - q <= 2]
        left = [ls[rho, 7 + b : 7 + b + WT] for b in range(3)]
        for i, q in enumerate(rows):
            weighted(rho - q, left, wc_ref, ab.at[rho], 3 * WT * i)
        part = dot(ab[rho, 0 : 3 * WT * len(rows)], rb[:, 5 * rho * CH : 5 * (rho + 1) * CH], NT)
        for i, q in enumerate(rows):
            at = 3 * WT * i
            total = part[at : at + WT] + part[at + WT : at + 2 * WT] + part[at + 2 * WT : at + 3 * WT]
            acc[q] = total if rho == q else acc[q] + total


def main_kernel(*refs):
    recv, wc_ref = refs[:8], refs[8]
    sums_ref, kept_ref, given_ref = refs[9:12]
    ls, rs, rb, ms, ab, acc, ub, diags, ks, lb, xs, ys, out_ref, fanned, sem = refs[12:]
    fill_meta(fill(recv, 0, 5, ls, rs, rb), ms)
    ks[...] = jnp.zeros(ks.shape, F32)
    xs[...] = jnp.zeros(xs.shape, F32)
    masks = row_masks()
    logits_of(ls, rb, wc_ref, ab, acc)
    for q in range(3):
        diag = None
        for a in range(3):
            for b in range(3):
                term = wc_ref[a, 3 * b : 3 * b + 1] * ls[q + a, 7 + b : 7 + b + WT] * rs[q + a, 8 + b : 8 + b + WT]
                diag = term if diag is None else diag + term
        up, resid, usable = row_gradient(q, acc[q], jnp.sum(diag, axis=1, keepdims=True), ms, masks)
        ub[2 * WT * q : 2 * WT * q + WT], ub[2 * WT * q + WT : 2 * WT * (q + 1)] = split2(up)
        diags[q] = jnp.broadcast_to(diagonal(up, masks[3]), (WT, CH))
        if q == 1:
            size = jnp.abs(resid)
            smooth = jnp.where(size < 1.0, 0.5 * resid * resid, size - 0.5)
            loss_sum = jnp.sum(usable * smooth, axis=0, keepdims=True)
            count_sum = jnp.sum(usable, axis=0, keepdims=True)
    for b in range(3):
        shifted = ls[2, 7 + b : 7 + b + WT].astype(BF16)
        lb[0:WT, b * CH : (b + 1) * CH] = shifted
        lb[WT:, b * CH : (b + 1) * CH] = shifted

    def tap(q, b, e):
        return wc_ref[2 - q, 3 * b + e : 3 * b + e + 1]

    terms = dot(ub[...], rb[:, 10 * CH : 15 * CH])
    for b in range(3):
        own_left, own_right = ls[2, 7 + b : 7 + b + WT], rs[2, 8 + b : 8 + b + WT]
        total = None
        spread = None
        for q in range(3):
            term = tap(q, b, 0) * diags[q]
            spread = term if spread is None else spread + term
            for e in range(3):
                at, si = 2 * WT * q, b - e + 2
                value = terms[at : at + WT, si * CH : (si + 1) * CH]
                value = value + terms[at + WT : at + 2 * WT, si * CH : (si + 1) * CH]
                if e == 0:
                    value = value - diags[q] * own_right
                at = 9 * (2 - q) + 3 * b + e
                ks[at : at + 1] = jnp.sum(own_left * value, axis=0, keepdims=True)
                term = tap(q, b, e) * value
                total = term if total is None else total + term
        xs[b, 8 : 8 + WT] = total
        xs[3 + b, 8 : 8 + WT] = spread * own_left
    channel = lax.broadcasted_iota(jnp.int32, (8, CH), 1)
    member = group_member().astype(BF16)
    parts = [dot(member, part, NT) for part in split3(ks[...])]
    sums = (parts[0] + (parts[1] + parts[2])) * (1.0 / 16.0)
    sums = jnp.where(channel == LOSS_LANE, loss_sum, sums)
    sums = jnp.where(channel == COUNT_LANE, count_sum, sums)
    sums = jnp.where(channel < SHARE, sums, 0.0)
    quarter = lax.broadcasted_iota(jnp.int32, (8, CH), 0) & 3
    placed = jnp.where(quarter == 0, sums, 0.0)
    for i in range(1, 4):
        placed = placed + jnp.where(quarter == i, pltpu.roll(sums, SHARE * i, 1), 0.0)
    packed = jnp.concatenate([jnp.sum(placed[4 * i : 4 * i + 4], axis=0, keepdims=True) for i in range(2)], axis=0)
    for i in range(sums_ref.shape[0]):
        fanned[i] = packed
    sending = pltpu.make_async_copy(fanned, sums_ref, sem)
    sending.start()
    for q in range(3):
        terms = dot(ub[2 * WT * q : 2 * WT * (q + 1)], lb[...], TN)
        for si in range(5):
            total = None
            for b in range(3):
                e = b - (si - 2)
                if 0 <= e <= 2:
                    term = tap(q, b, e) * terms[:, b * CH : (b + 1) * CH]
                    total = term if total is None else total + term
            ys[si] = total if q == 0 else ys[si] + total
    grad_left = xs[0, 9 : 9 + WT] + xs[1, 8 : 8 + WT] + xs[2, 7 : 7 + WT]
    grad_right = ys[0, 4 : 4 + WT]
    for si in range(1, 5):
        grad_right = grad_right + ys[si, 4 - si : 4 - si + WT]
    for b in range(3):
        grad_right = grad_right - xs[3 + b, 8 - b : 8 - b + WT]
    for dst in range(WA):
        out_ref[dst, 0] = grad_left[TILE * dst : TILE * (dst + 1)].astype(BF16)
        out_ref[dst, 1] = grad_right[TILE * dst : TILE * (dst + 1)].astype(BF16)
    chip, core = position()
    for ref, holder in ((kept_ref, core), (given_ref, 1 - core)):
        beside = chip_at(chip, ahead(holder))
        opposite = chip_at(chip, 2)
        places = (2 * beside + holder, 2 * beside + 1 - holder, 2 * opposite + holder, 2 * chip + holder)
        for i, tile in enumerate(places):
            for side in range(2):
                ref[2 * i + side] = out_ref[tile, side]
    sending.wait()


def ahead(core):
    return 1 - 2 * core


def chip_at(chip, step):
    return (chip + step + CHIPS) & (CHIPS - 1)


def pack_back_kernel(places, kept_ref, got_ref, *refs):
    for place, out_ref in zip(places, refs[-len(places) :]):
        for row, ref in enumerate((kept_ref, got_ref)):
            for side in range(2):
                out_ref[2 * row + side] = ref[2 * place + side]


def finish_kernel(kept, got, near, far, across, sums_ref, left_ref, right_ref, weight_ref, loss_ref):
    chip, core = position()
    other = 1 - core
    before, after, opposite = chip_at(chip, -ahead(core)), chip_at(chip, ahead(core)), chip_at(chip, 2)
    partial = [sums_ref[i] for i in range(8)]
    for i in range(8, sums_ref.shape[0]):
        partial[i % 8] = partial[i % 8] + sums_ref[i]
    while len(partial) > 1:
        partial = [x + y for x, y in zip(partial[0::2], partial[1::2])]
    placed = partial[0]
    total = jnp.concatenate(
        [pltpu.roll(jnp.broadcast_to(placed[g // 4 : g // 4 + 1], (8, CH)), (CH - SHARE * (g % 4)) % CH, 1)[0:1] for g in range(8)],
        axis=0,
    )
    norm = 1.0 / jnp.maximum(total[0:1, COUNT_LANE : COUNT_LANE + 1], 1.0)
    blocks = (
        (kept, 6, 2 * chip + core),
        (got, 6, 2 * chip + other),
        (near, 0, 2 * before + core),
        (near, 2, 2 * before + other),
        (far, 0, 2 * after + other),
        (far, 2, 2 * after + core),
        (across, 0, 2 * opposite + core),
        (across, 2, 2 * opposite + other),
    )
    for ref, at, row in blocks:
        left_ref[row] = ref[at].astype(F32) * norm
        right_ref[row] = ref[at + 1].astype(F32) * norm
    loss_ref[...] = total[0:1, LOSS_LANE : LOSS_LANE + 1] * norm
    by_tap = jnp.concatenate([total * norm, jnp.zeros((CH - 8, CH), F32)], axis=0).T
    for a in range(3):
        for b in range(3):
            at = 9 * a + 3 * b
            weight_ref[a, b] = by_tap[at : at + 3, 0:8]


def call(kernel, out_shape, *args, scratch=(), flops=0, params=VMEM):
    cost = pl.CostEstimate(flops=flops, bytes_accessed=1 << 20, transcendentals=0)
    return pl.pallas_call(
        kernel, out_shape=out_shape, scratch_shapes=list(scratch), compiler_params=params, cost_estimate=cost
    )(*args)


def swapped(value):
    return lax.ppermute(value, "wa", [(i, i ^ 1) for i in range(WA)])


def shards(left_feat, right_feat, conv_weight, disparity_gt, valid_mask):
    left, right = left_feat[0], right_feat[0]
    gt, valid = disparity_gt[0], valid_mask[0]
    ha_count = lax.axis_size("ha")
    halo = jax.ShapeDtypeStruct((5, TILE, CH), BF16)
    own = jax.ShapeDtypeStruct((2 * ROWS + 1, TILE, CH), BF16)
    args = (left, right, gt, valid, jnp.transpose(conv_weight, (1, 2, 3, 0)))
    up, down, own, taps = pl.pallas_call(
        halo_kernel,
        out_shape=(halo, halo, own, jax.ShapeDtypeStruct((3, 16, CH), F32)),
        in_specs=[pl.BlockSpec(memory_space=pltpu.HBM)] * 5,
        scratch_shapes=[
            pltpu.VMEM((ROWS, TILE, CH), BF16),
            pltpu.VMEM((ROWS, TILE, CH), BF16),
            pltpu.VMEM((ROWS, TILE), jnp.int32),
            pltpu.VMEM((ROWS, TILE), jnp.int32),
            pltpu.VMEM((3, 3, 3, 8), F32),
            pltpu.SemaphoreType.DMA((5,)),
        ],
        compiler_params=VMEM,
    )(*[pltpu.with_memory_space_constraint(arg, pltpu.HBM) for arg in args])
    before = lax.ppermute(up, "ha", [(i, (i + 1) % ha_count) for i in range(ha_count)])
    after = lax.ppermute(down, "ha", [((i + 1) % ha_count, i) for i in range(ha_count)])
    block = jax.ShapeDtypeStruct((13, TILE, CH), BF16)
    scratch = (pltpu.VMEM((24, TILE, CH), BF16),)
    (opposite,) = call(functools.partial(pack_kernel, (2,)), (block,), own, before, after, scratch=scratch)
    hop2 = lax.ppermute(opposite, "wa", [(i, (i + 4) % WA) for i in range(WA)])
    hop0, hop1, hop3 = call(
        functools.partial(pack_kernel, (0, 1, 3)), (block,) * 3, own, before, after, opposite, scratch=scratch, flops=1 << 31
    )
    hop1 = lax.ppermute(hop1, "wa", [(i, (i + 2) % WA) for i in range(WA)])
    hop3 = lax.ppermute(hop3, "wa", [(i, (i + 6) % WA) for i in range(WA)])
    same_core = [hop0, hop1, hop2, hop3]
    tiles = same_core + [swapped(value) for value in same_core]
    others = lax.axis_size("dp") * ha_count * WA
    half = jax.ShapeDtypeStruct((8, TILE, CH), BF16)
    sums, kept, given = pl.pallas_call(
        main_kernel,
        out_shape=(jax.ShapeDtypeStruct((others, 2, CH), F32), half, half),
        out_specs=(pl.BlockSpec(memory_space=pltpu.HBM), pl.BlockSpec(memory_space=pltpu.VMEM), pl.BlockSpec(memory_space=pltpu.VMEM)),
        scratch_shapes=(
            pltpu.VMEM((5, WT + 16, CH), F32),
            pltpu.VMEM((5, WT + 80, CH), F32),
            pltpu.VMEM((JP, 25 * CH), BF16),
            pltpu.VMEM((WT, CH), F32),
            pltpu.VMEM((5, 9 * WT, 5 * CH), BF16),
            pltpu.VMEM((3, WT, JP), F32),
            pltpu.VMEM((6 * WT, JP), BF16),
            pltpu.VMEM((3, WT, CH), F32),
            pltpu.VMEM((CH, CH), F32),
            pltpu.VMEM((2 * WT, 3 * CH), BF16),
            pltpu.VMEM((6, WT + 16, CH), F32),
            pltpu.VMEM((5, JP, CH), F32),
            pltpu.VMEM((WA, 2, TILE, CH), BF16),
            pltpu.VMEM((others, 2, CH), F32),
            pltpu.SemaphoreType.DMA,
        ),
        compiler_params=VMEM,
        cost_estimate=pl.CostEstimate(flops=5 << 30, bytes_accessed=1 << 20, transcendentals=0),
    )(*tiles, taps)
    sums = lax.all_to_all(sums, ("dp", "ha", "wa"), 0, 0, tiled=True)
    got = swapped(given)
    block = jax.ShapeDtypeStruct((4, TILE, CH), BF16)
    (opposite,) = call(functools.partial(pack_back_kernel, (2,)), (block,), kept, got)
    across = lax.ppermute(opposite, "wa", [(i, (i + 4) % WA) for i in range(WA)])
    beside, beside_other = call(
        functools.partial(pack_back_kernel, (0, 1)), (block,) * 2, kept, got, opposite, flops=1 << 31
    )
    near = lax.ppermute(beside, "wa", [(i, (i + 2 - 4 * (i % 2)) % WA) for i in range(WA)])
    far = lax.ppermute(beside_other, "wa", [(i, (i + 3 - 6 * (i % 2)) % WA) for i in range(WA)])
    tile = jax.ShapeDtypeStruct((ROWS, TILE, CH), F32)
    grad_left, grad_right, weight, loss = call(
        finish_kernel,
        (tile, tile, jax.ShapeDtypeStruct((3, 3, 3, 8), F32), jax.ShapeDtypeStruct((1, 1), F32)),
        kept,
        got,
        near,
        far,
        across,
        sums,
    )
    return (loss[0, 0], grad_left[None], grad_right[None], jnp.transpose(weight, (3, 0, 1, 2)))


def solution(mesh):
    placed = (
        P("dp", "ha", "wa", None),
        P("dp", "ha", "wa", None),
        P(),
        P("dp", "ha", "wa"),
        P("dp", "ha", "wa"),
    )
    return jax.shard_map(
        shards,
        mesh=mesh,
        in_specs=placed,
        out_specs=(P(), P("dp", "ha", "wa", None), P("dp", "ha", "wa", None), P()),
        check_vma=False,
    )
```

```python
import functools

import jax
import jax.numpy as jnp
from jax import lax
from jax.experimental import pallas as pl
from jax.experimental.pallas import tpu as pltpu
from jax.sharding import PartitionSpec as P

F32 = jnp.float32
BF16 = jnp.bfloat16
ROWS, TILE, CH = 8, 24, 128
WA, CHIPS = 8, 4
WT = 192
JP = 256
GT_LANE, VALID_LANE = 0, 16
LOSS_LANE, COUNT_LANE, SHARE = 27, 28, 32
VMEM = pltpu.CompilerParams(vmem_limit_bytes=48 * 1024 * 1024)
NT = (((1,), (1,)), ((), ()))
NN = (((1,), (0,)), ((), ()))
TN = (((0,), (0,)), ((), ()))


def dot(lhs, rhs, dims=NN, precision=None):
    return lax.dot_general(lhs, rhs, dims, precision=precision, preferred_element_type=F32)


def meta_block(gt, valid, first, count, lane_of_first):
    row = lax.broadcasted_iota(jnp.int32, (ROWS, CH), 0)
    lane = lax.broadcasted_iota(jnp.int32, (ROWS, CH), 1)
    chosen = (row >= first) & (row < first + count)
    at = row - first + lane_of_first
    pick_gt = (chosen & (lane == at + GT_LANE)).astype(F32)
    pick_valid = (chosen & (lane == at + VALID_LANE)).astype(F32)
    return dot(gt, pick_gt, TN) + dot(valid, pick_valid, TN)


def halo_kernel(left_any, right_any, gt_any, valid_any, weight_any, up_ref, down_ref, own_ref, taps_ref, *scratch):
    refs, sems = scratch[:5], scratch[5]
    sources = (left_any, right_any, gt_any, valid_any, weight_any)
    copies = [pltpu.make_async_copy(src, dst, sems.at[i]) for i, (src, dst) in enumerate(zip(sources, refs))]
    for copy in copies:
        copy.start()
    for copy in copies:
        copy.wait()
    left_ref, right_ref, gt_ref, valid_ref, weight_ref = refs
    gt = gt_ref[...].astype(F32)
    valid = valid_ref[...].astype(F32)
    for side, ref in ((0, left_ref), (1, right_ref)):
        for i in range(2):
            up_ref[2 * side + i] = ref[ROWS - 2 + i]
            down_ref[2 * side + i] = ref[i]
        for i in range(ROWS):
            own_ref[ROWS * side + i] = ref[i]
    up_ref[4] = meta_block(gt, valid, ROWS - 2, 2, 0).astype(BF16)
    down_ref[4] = meta_block(gt, valid, 0, 2, ROWS + 2).astype(BF16)
    own_ref[2 * ROWS] = meta_block(gt, valid, 0, ROWS, 2).astype(BF16)
    member = group_member() * (1.0 / 16.0)
    for a in range(3):
        taps = jnp.concatenate([weight_ref[a, b] for b in range(3)], axis=0)
        taps_ref[a, 0:9] = dot(taps, member, precision=lax.Precision.HIGHEST)


def group_member():
    group = lax.broadcasted_iota(jnp.int32, (8, CH), 0)
    channel = lax.broadcasted_iota(jnp.int32, (8, CH), 1)
    return (lax.shift_right_logical(channel, 4) == group).astype(F32)


def position():
    index = lax.axis_index("wa")
    return lax.shift_right_logical(index, 1), index & 1


def pack_kernel(own_ref, prev_ref, next_ref, *refs):
    outs, ext = refs[:CHIPS], refs[CHIPS]
    chip, _ = position()
    band = lax.axis_index("ha")
    has_prev = band > 0
    has_next = band < lax.axis_size("ha") - 1

    def of_prev(i):
        return jnp.where(has_prev, prev_ref[i], jnp.zeros((TILE, CH), BF16))

    def of_next(i):
        return jnp.where(has_next, next_ref[i], jnp.zeros((TILE, CH), BF16))

    meta = own_ref[2 * ROWS].astype(F32)
    meta = (meta + of_prev(4).astype(F32) + of_next(4).astype(F32)).astype(BF16)
    for side in range(2):
        for i in range(2):
            ext[12 * side + i] = of_prev(2 * side + i)
            ext[12 * side + ROWS + 2 + i] = of_next(2 * side + i)
        for i in range(ROWS):
            ext[12 * side + 2 + i] = own_ref[ROWS * side + i]
    for hop in range(CHIPS):
        first = 2 * ((chip + hop) & (CHIPS - 1))
        for i in range(6):
            outs[hop][i] = ext[first + i]
            outs[hop][6 + i] = ext[first + 12 + i]
        outs[hop][12] = meta


def split3(value):
    high = value.astype(BF16)
    rest = value - high.astype(F32)
    middle = rest.astype(BF16)
    low = (rest - middle.astype(F32)).astype(BF16)
    return high, middle, low


def fill(refs, first, count, ls, rs, rb):
    chip, core = position()
    tiles = []
    for hop in range(CHIPS):
        tile = 2 * ((chip - hop) & (CHIPS - 1))
        tiles.append((refs[hop], pl.multiple_of(8 + TILE * (tile + core), 8)))
        tiles.append((refs[CHIPS + hop], pl.multiple_of(8 + TILE * (tile + 1 - core), 8)))

    @pl.loop(first, first + count)
    def row(rho):
        ls[rho, 0:8] = jnp.zeros((8, CH), F32)
        ls[rho, 8 + WT :] = jnp.zeros((8, CH), F32)
        rs[rho, 0:8] = jnp.zeros((8, CH), F32)
        rs[rho, 8 + WT :] = jnp.zeros((72, CH), F32)
        for ref, at in tiles:
            ls[rho, pl.ds(at, TILE)] = ref[core + rho].astype(F32)
            rs[rho, pl.ds(at, TILE)] = ref[6 + core + rho].astype(F32)
        for si in range(5):
            rb[:, pl.ds(pl.multiple_of((5 * rho + si) * CH, CH), CH)] = rs[rho, 4 + si : 4 + si + JP].astype(BF16)

    return tiles


def fill_meta(tiles, ms):
    for ref, at in tiles:
        ms[pl.ds(at - 8, TILE)] = ref[12].astype(F32)


def split2(value):
    high = value.astype(BF16)
    return high, (value - high.astype(F32)).astype(BF16)


def weighted(a, left, wc_ref, ab, at):
    for si in range(5):
        value = None
        for b in range(3):
            e = b - (si - 2)
            if 0 <= e <= 2:
                term = wc_ref[a, 3 * b + e : 3 * b + e + 1] * left[b]
                value = term if value is None else value + term
        for i, part in enumerate(split3(value)):
            ab[at + i * WT : at + (i + 1) * WT, si * CH : (si + 1) * CH] = part


def row_gradient(q, logits, diag_col, ms, masks):
    lane, level, inside, on_diag, wcol, zeros_count, zeros_mean = masks
    logits = logits - jnp.where(on_diag, diag_col, 0.0)
    top = jnp.max(jnp.where(inside, logits, -3e38), axis=1, keepdims=True)
    top = jnp.where(zeros_count > 0.0, jnp.maximum(top, 0.0), top)
    expd = jnp.where(inside, jnp.exp(logits - top), 0.0)
    zero_exp = jnp.where(zeros_count > 0.0, zeros_count * jnp.exp(-top), 0.0)
    denom = jnp.sum(expd, axis=1, keepdims=True) + zero_exp
    first = jnp.sum(expd * level, axis=1, keepdims=True) + zero_exp * zeros_mean
    inv = 1.0 / denom
    estimate = first * inv
    ext = lax.axis_index("wa") + 1 + q
    meta = ms[...]
    target = jnp.sum(jnp.where(lane == GT_LANE + ext, meta, 0.0), axis=1, keepdims=True)
    valid = jnp.sum(jnp.where(lane == VALID_LANE + ext, meta, 0.0), axis=1, keepdims=True)
    usable = jnp.where(target <= wcol, valid, 0.0)
    resid = estimate - target
    factor = jnp.clip(resid, -1.0, 1.0) * usable * inv
    return expd * (level - estimate) * factor, resid, usable


def diagonal(up, on_diag):
    return jnp.sum(jnp.where(on_diag, up, 0.0), axis=1, keepdims=True)


def row_masks():
    lane = lax.broadcasted_iota(jnp.int32, (WT, CH), 1)
    ww = lax.broadcasted_iota(jnp.int32, (WT, JP), 0)
    jj = lax.broadcasted_iota(jnp.int32, (WT, JP), 1)
    level = (ww - jj + 2).astype(F32)
    inside = (jj <= ww + 2) & (jj >= ww - (WT - 3))
    on_diag = jj == ww + 2
    wcol = lax.broadcasted_iota(jnp.int32, (WT, 1), 0).astype(F32)
    zeros_count = jnp.maximum(float(WT - 3) - wcol, 0.0)
    zeros_mean = (wcol + float(WT + 2)) * 0.5
    return lane, level, inside, on_diag, wcol, zeros_count, zeros_mean


def logits_of(ls, rb, wc_ref, ab, acc):
    for rho in range(5):
        rows = [q for q in range(3) if 0 <= rho - q <= 2]
        left = [ls[rho, 7 + b : 7 + b + WT] for b in range(3)]
        for i, q in enumerate(rows):
            weighted(rho - q, left, wc_ref, ab.at[rho], 3 * WT * i)
        part = dot(ab[rho, 0 : 3 * WT * len(rows)], rb[:, 5 * rho * CH : 5 * (rho + 1) * CH], NT)
        for i, q in enumerate(rows):
            at = 3 * WT * i
            total = part[at : at + WT] + part[at + WT : at + 2 * WT] + part[at + 2 * WT : at + 3 * WT]
            acc[q] = total if rho == q else acc[q] + total


def main_kernel(*refs):
    recv, wc_ref = refs[:8], refs[8]
    sums_ref, kept_ref, given_ref = refs[9:12]
    ls, rs, rb, ms, ab, acc, ub, diags, ks, lb, xs, ys, out_ref, fanned, sem = refs[12:]
    fill_meta(fill(recv, 0, 5, ls, rs, rb), ms)
    ks[...] = jnp.zeros(ks.shape, F32)
    xs[...] = jnp.zeros(xs.shape, F32)
    masks = row_masks()
    logits_of(ls, rb, wc_ref, ab, acc)
    for q in range(3):
        diag = None
        for a in range(3):
            for b in range(3):
                term = wc_ref[a, 3 * b : 3 * b + 1] * ls[q + a, 7 + b : 7 + b + WT] * rs[q + a, 8 + b : 8 + b + WT]
                diag = term if diag is None else diag + term
        up, resid, usable = row_gradient(q, acc[q], jnp.sum(diag, axis=1, keepdims=True), ms, masks)
        ub[2 * WT * q : 2 * WT * q + WT], ub[2 * WT * q + WT : 2 * WT * (q + 1)] = split2(up)
        diags[q] = jnp.broadcast_to(diagonal(up, masks[3]), (WT, CH))
        if q == 1:
            size = jnp.abs(resid)
            smooth = jnp.where(size < 1.0, 0.5 * resid * resid, size - 0.5)
            loss_sum = jnp.sum(usable * smooth, axis=0, keepdims=True)
            count_sum = jnp.sum(usable, axis=0, keepdims=True)
    for b in range(3):
        shifted = ls[2, 7 + b : 7 + b + WT].astype(BF16)
        lb[0:WT, b * CH : (b + 1) * CH] = shifted
        lb[WT:, b * CH : (b + 1) * CH] = shifted

    def tap(q, b, e):
        return wc_ref[2 - q, 3 * b + e : 3 * b + e + 1]

    terms = dot(ub[...], rb[:, 10 * CH : 15 * CH])
    for b in range(3):
        own_left, own_right = ls[2, 7 + b : 7 + b + WT], rs[2, 8 + b : 8 + b + WT]
        total = None
        spread = None
        for q in range(3):
            term = tap(q, b, 0) * diags[q]
            spread = term if spread is None else spread + term
            for e in range(3):
                at, si = 2 * WT * q, b - e + 2
                value = terms[at : at + WT, si * CH : (si + 1) * CH]
                value = value + terms[at + WT : at + 2 * WT, si * CH : (si + 1) * CH]
                if e == 0:
                    value = value - diags[q] * own_right
                at = 9 * (2 - q) + 3 * b + e
                ks[at : at + 1] = jnp.sum(own_left * value, axis=0, keepdims=True)
                term = tap(q, b, e) * value
                total = term if total is None else total + term
        xs[b, 8 : 8 + WT] = total
        xs[3 + b, 8 : 8 + WT] = spread * own_left
    channel = lax.broadcasted_iota(jnp.int32, (8, CH), 1)
    member = group_member().astype(BF16)
    parts = [dot(member, part, NT) for part in split3(ks[...])]
    sums = (parts[0] + (parts[1] + parts[2])) * (1.0 / 16.0)
    sums = jnp.where(channel == LOSS_LANE, loss_sum, sums)
    sums = jnp.where(channel == COUNT_LANE, count_sum, sums)
    sums = jnp.where(channel < SHARE, sums, 0.0)
    quarter = lax.broadcasted_iota(jnp.int32, (8, CH), 0) & 3
    placed = jnp.where(quarter == 0, sums, 0.0)
    for i in range(1, 4):
        placed = placed + jnp.where(quarter == i, pltpu.roll(sums, SHARE * i, 1), 0.0)
    packed = jnp.concatenate([jnp.sum(placed[4 * i : 4 * i + 4], axis=0, keepdims=True) for i in range(2)], axis=1)
    for i in range(sums_ref.shape[0]):
        fanned[i] = packed
    sending = pltpu.make_async_copy(fanned, sums_ref, sem)
    sending.start()
    for q in range(3):
        terms = dot(ub[2 * WT * q : 2 * WT * (q + 1)], lb[...], TN)
        for si in range(5):
            total = None
            for b in range(3):
                e = b - (si - 2)
                if 0 <= e <= 2:
                    term = tap(q, b, e) * terms[:, b * CH : (b + 1) * CH]
                    total = term if total is None else total + term
            ys[si] = total if q == 0 else ys[si] + total
    grad_left = xs[0, 9 : 9 + WT] + xs[1, 8 : 8 + WT] + xs[2, 7 : 7 + WT]
    grad_right = ys[0, 4 : 4 + WT]
    for si in range(1, 5):
        grad_right = grad_right + ys[si, 4 - si : 4 - si + WT]
    for b in range(3):
        grad_right = grad_right - xs[3 + b, 8 - b : 8 - b + WT]
    for dst in range(WA):
        out_ref[dst, 0] = grad_left[TILE * dst : TILE * (dst + 1)].astype(BF16)
        out_ref[dst, 1] = grad_right[TILE * dst : TILE * (dst + 1)].astype(BF16)
    chip, core = position()
    for ref, holder in ((kept_ref, core), (given_ref, 1 - core)):
        beside = chip_at(chip, ahead(holder))
        opposite = chip_at(chip, 2)
        places = (2 * beside + holder, 2 * beside + 1 - holder, 2 * opposite + holder, 2 * chip + holder)
        for i, tile in enumerate(places):
            for side in range(2):
                ref[2 * i + side] = out_ref[tile, side]
    sending.wait()


def ahead(core):
    return 1 - 2 * core


def chip_at(chip, step):
    return (chip + step + CHIPS) & (CHIPS - 1)


def pack_back_kernel(places, kept_ref, got_ref, *refs):
    for place, out_ref in zip(places, refs[-len(places) :]):
        for row, ref in enumerate((kept_ref, got_ref)):
            for side in range(2):
                out_ref[2 * row + side] = ref[2 * place + side]


def finish_kernel(kept, got, near, far, across, sums_ref, left_ref, right_ref, weight_ref, loss_ref):
    chip, core = position()
    other = 1 - core
    before, after, opposite = chip_at(chip, -ahead(core)), chip_at(chip, ahead(core)), chip_at(chip, 2)
    partial = [sums_ref[i] for i in range(8)]
    for i in range(8, sums_ref.shape[0]):
        partial[i % 8] = partial[i % 8] + sums_ref[i]
    while len(partial) > 1:
        partial = [x + y for x, y in zip(partial[0::2], partial[1::2])]
    placed = jnp.concatenate([partial[0][:, 0:CH], partial[0][:, CH:]], axis=0)
    total = jnp.concatenate(
        [pltpu.roll(jnp.broadcast_to(placed[g // 4 : g // 4 + 1], (8, CH)), (CH - SHARE * (g % 4)) % CH, 1)[0:1] for g in range(8)],
        axis=0,
    )
    norm = 1.0 / jnp.maximum(total[0:1, COUNT_LANE : COUNT_LANE + 1], 1.0)
    blocks = (
        (kept, 6, 2 * chip + core),
        (got, 6, 2 * chip + other),
        (near, 0, 2 * before + core),
        (near, 2, 2 * before + other),
        (far, 0, 2 * after + other),
        (far, 2, 2 * after + core),
        (across, 0, 2 * opposite + core),
        (across, 2, 2 * opposite + other),
    )
    for ref, at, row in blocks:
        left_ref[row] = ref[at].astype(F32) * norm
        right_ref[row] = ref[at + 1].astype(F32) * norm
    loss_ref[...] = total[0:1, LOSS_LANE : LOSS_LANE + 1] * norm
    by_tap = jnp.concatenate([total * norm, jnp.zeros((CH - 8, CH), F32)], axis=0).T
    for a in range(3):
        for b in range(3):
            at = 9 * a + 3 * b
            weight_ref[a, b] = by_tap[at : at + 3, 0:8]


def call(kernel, out_shape, *args, scratch=(), flops=0, params=VMEM):
    cost = pl.CostEstimate(flops=flops, bytes_accessed=1 << 20, transcendentals=0)
    return pl.pallas_call(
        kernel, out_shape=out_shape, scratch_shapes=list(scratch), compiler_params=params, cost_estimate=cost
    )(*args)


def swapped(value):
    return lax.ppermute(value, "wa", [(i, i ^ 1) for i in range(WA)])


def shards(left_feat, right_feat, conv_weight, disparity_gt, valid_mask):
    left, right = left_feat[0], right_feat[0]
    gt, valid = disparity_gt[0], valid_mask[0]
    ha_count = lax.axis_size("ha")
    halo = jax.ShapeDtypeStruct((5, TILE, CH), BF16)
    own = jax.ShapeDtypeStruct((2 * ROWS + 1, TILE, CH), BF16)
    args = (left, right, gt, valid, jnp.transpose(conv_weight, (1, 2, 3, 0)))
    up, down, own, taps = pl.pallas_call(
        halo_kernel,
        out_shape=(halo, halo, own, jax.ShapeDtypeStruct((3, 16, CH), F32)),
        in_specs=[pl.BlockSpec(memory_space=pltpu.HBM)] * 5,
        scratch_shapes=[
            pltpu.VMEM((ROWS, TILE, CH), BF16),
            pltpu.VMEM((ROWS, TILE, CH), BF16),
            pltpu.VMEM((ROWS, TILE), jnp.int32),
            pltpu.VMEM((ROWS, TILE), jnp.int32),
            pltpu.VMEM((3, 3, 3, 8), F32),
            pltpu.SemaphoreType.DMA((5,)),
        ],
        compiler_params=VMEM,
    )(*[pltpu.with_memory_space_constraint(arg, pltpu.HBM) for arg in args])
    before = lax.ppermute(up, "ha", [(i, (i + 1) % ha_count) for i in range(ha_count)])
    after = lax.ppermute(down, "ha", [((i + 1) % ha_count, i) for i in range(ha_count)])
    block = jax.ShapeDtypeStruct((13, TILE, CH), BF16)
    blocks = call(
        pack_kernel,
        (block,) * CHIPS,
        own,
        before,
        after,
        scratch=(pltpu.VMEM((24, TILE, CH), BF16),),
    )
    same_core = [blocks[0]]
    for hop in range(1, CHIPS):
        same_core.append(lax.ppermute(blocks[hop], "wa", [(i, (i + 2 * hop) % WA) for i in range(WA)]))
    other_core = [lax.ppermute(value, "wa", [(i, i ^ 1) for i in range(WA)]) for value in same_core]
    tiles = same_core + other_core
    others = lax.axis_size("dp") * ha_count * WA
    half = jax.ShapeDtypeStruct((8, TILE, CH), BF16)
    sums, kept, given = pl.pallas_call(
        main_kernel,
        out_shape=(jax.ShapeDtypeStruct((others, 1, 2 * CH), F32), half, half),
        out_specs=(pl.BlockSpec(memory_space=pltpu.HBM), pl.BlockSpec(memory_space=pltpu.VMEM), pl.BlockSpec(memory_space=pltpu.VMEM)),
        scratch_shapes=(
            pltpu.VMEM((5, WT + 16, CH), F32),
            pltpu.VMEM((5, WT + 80, CH), F32),
            pltpu.VMEM((JP, 25 * CH), BF16),
            pltpu.VMEM((WT, CH), F32),
            pltpu.VMEM((5, 9 * WT, 5 * CH), BF16),
            pltpu.VMEM((3, WT, JP), F32),
            pltpu.VMEM((6 * WT, JP), BF16),
            pltpu.VMEM((3, WT, CH), F32),
            pltpu.VMEM((CH, CH), F32),
            pltpu.VMEM((2 * WT, 3 * CH), BF16),
            pltpu.VMEM((6, WT + 16, CH), F32),
            pltpu.VMEM((5, JP, CH), F32),
            pltpu.VMEM((WA, 2, TILE, CH), BF16),
            pltpu.VMEM((others, 1, 2 * CH), F32),
            pltpu.SemaphoreType.DMA,
        ),
        compiler_params=VMEM,
        cost_estimate=pl.CostEstimate(flops=5 << 30, bytes_accessed=1 << 20, transcendentals=0),
    )(*tiles, taps)
    sums = lax.all_to_all(sums, ("dp", "ha", "wa"), 0, 0, tiled=True)
    got = swapped(given)
    block = jax.ShapeDtypeStruct((4, TILE, CH), BF16)
    (opposite,) = call(functools.partial(pack_back_kernel, (2,)), (block,), kept, got)
    across = lax.ppermute(opposite, "wa", [(i, (i + 4) % WA) for i in range(WA)])
    beside, beside_other = call(
        functools.partial(pack_back_kernel, (0, 1)), (block,) * 2, kept, got, opposite, flops=1 << 31
    )
    near = lax.ppermute(beside, "wa", [(i, (i + 2 - 4 * (i % 2)) % WA) for i in range(WA)])
    far = lax.ppermute(beside_other, "wa", [(i, (i + 3 - 6 * (i % 2)) % WA) for i in range(WA)])
    tile = jax.ShapeDtypeStruct((ROWS, TILE, CH), F32)
    grad_left, grad_right, weight, loss = call(
        finish_kernel,
        (tile, tile, jax.ShapeDtypeStruct((3, 3, 3, 8), F32), jax.ShapeDtypeStruct((1, 1), F32)),
        kept,
        got,
        near,
        far,
        across,
        sums,
    )
    return (loss[0, 0], grad_left[None], grad_right[None], jnp.transpose(weight, (3, 0, 1, 2)))


def solution(mesh):
    placed = (
        P("dp", "ha", "wa", None),
        P("dp", "ha", "wa", None),
        P(),
        P("dp", "ha", "wa"),
        P("dp", "ha", "wa"),
    )
    return jax.shard_map(
        shards,
        mesh=mesh,
        in_specs=placed,
        out_specs=(P(), P("dp", "ha", "wa", None), P("dp", "ha", "wa", None), P()),
        check_vma=False,
    )
```

```python
import functools

import jax
import jax.numpy as jnp
from jax import lax
from jax.experimental import pallas as pl
from jax.experimental.pallas import tpu as pltpu
from jax.sharding import PartitionSpec as P

F32 = jnp.float32
BF16 = jnp.bfloat16
ROWS, TILE, CH = 8, 24, 128
WA, CHIPS = 8, 4
WT = 192
JP = 256
GT_LANE, VALID_LANE = 0, 16
LOSS_LANE, COUNT_LANE, SHARE = 27, 28, 32
VMEM = pltpu.CompilerParams(vmem_limit_bytes=48 * 1024 * 1024)
NT = (((1,), (1,)), ((), ()))
NN = (((1,), (0,)), ((), ()))
TN = (((0,), (0,)), ((), ()))


def dot(lhs, rhs, dims=NN, precision=None):
    return lax.dot_general(lhs, rhs, dims, precision=precision, preferred_element_type=F32)


def meta_block(gt, valid, first, count, lane_of_first):
    row = lax.broadcasted_iota(jnp.int32, (ROWS, CH), 0)
    lane = lax.broadcasted_iota(jnp.int32, (ROWS, CH), 1)
    chosen = (row >= first) & (row < first + count)
    at = row - first + lane_of_first
    pick_gt = (chosen & (lane == at + GT_LANE)).astype(F32)
    pick_valid = (chosen & (lane == at + VALID_LANE)).astype(F32)
    return dot(gt, pick_gt, TN) + dot(valid, pick_valid, TN)


def copied_in(sources, refs, sems):
    copies = [pltpu.make_async_copy(src, dst, sems.at[i]) for i, (src, dst) in enumerate(zip(sources, refs))]
    for copy in copies:
        copy.start()
    for copy in copies:
        copy.wait()


def halo_kernel(left_any, right_any, gt_any, valid_any, up_ref, down_ref, *scratch):
    refs, sems = scratch[:4], scratch[4]
    copied_in((left_any, right_any, gt_any, valid_any), refs, sems)
    left_ref, right_ref, gt_ref, valid_ref = refs
    gt = gt_ref[...].astype(F32)
    valid = valid_ref[...].astype(F32)
    for side, ref in ((0, left_ref), (1, right_ref)):
        for i in range(2):
            up_ref[2 * side + i] = ref[ROWS - 2 + i]
            down_ref[2 * side + i] = ref[i]
    up_ref[4] = meta_block(gt, valid, ROWS - 2, 2, 0).astype(BF16)
    down_ref[4] = meta_block(gt, valid, 0, 2, ROWS + 2).astype(BF16)


def own_tile_kernel(left_any, right_any, gt_any, valid_any, weight_any, own_ref, taps_ref, *scratch):
    refs, sems = scratch[:5], scratch[5]
    copied_in((left_any, right_any, gt_any, valid_any, weight_any), refs, sems)
    left_ref, right_ref, gt_ref, valid_ref, weight_ref = refs
    for side, ref in ((0, left_ref), (1, right_ref)):
        for i in range(ROWS):
            own_ref[ROWS * side + i] = ref[i]
    own_ref[2 * ROWS] = meta_block(gt_ref[...].astype(F32), valid_ref[...].astype(F32), 0, ROWS, 2).astype(BF16)
    member = group_member() * (1.0 / 16.0)
    for a in range(3):
        taps = jnp.concatenate([weight_ref[a, b] for b in range(3)], axis=0)
        taps_ref[a, 0:9] = dot(taps, member, precision=lax.Precision.HIGHEST)


def group_member():
    group = lax.broadcasted_iota(jnp.int32, (8, CH), 0)
    channel = lax.broadcasted_iota(jnp.int32, (8, CH), 1)
    return (lax.shift_right_logical(channel, 4) == group).astype(F32)


def position():
    index = lax.axis_index("wa")
    return lax.shift_right_logical(index, 1), index & 1


def pack_kernel(own_ref, prev_ref, next_ref, *refs):
    outs, ext = refs[:CHIPS], refs[CHIPS]
    chip, _ = position()
    band = lax.axis_index("ha")
    has_prev = band > 0
    has_next = band < lax.axis_size("ha") - 1

    def of_prev(i):
        return jnp.where(has_prev, prev_ref[i], jnp.zeros((TILE, CH), BF16))

    def of_next(i):
        return jnp.where(has_next, next_ref[i], jnp.zeros((TILE, CH), BF16))

    meta = own_ref[2 * ROWS].astype(F32)
    meta = (meta + of_prev(4).astype(F32) + of_next(4).astype(F32)).astype(BF16)
    for side in range(2):
        for i in range(2):
            ext[12 * side + i] = of_prev(2 * side + i)
            ext[12 * side + ROWS + 2 + i] = of_next(2 * side + i)
        for i in range(ROWS):
            ext[12 * side + 2 + i] = own_ref[ROWS * side + i]
    for hop in range(CHIPS):
        first = 2 * ((chip + hop) & (CHIPS - 1))
        for i in range(6):
            outs[hop][i] = ext[first + i]
            outs[hop][6 + i] = ext[first + 12 + i]
        outs[hop][12] = meta


def split3(value):
    high = value.astype(BF16)
    rest = value - high.astype(F32)
    middle = rest.astype(BF16)
    low = (rest - middle.astype(F32)).astype(BF16)
    return high, middle, low


def fill(refs, first, count, ls, rs, rb):
    chip, core = position()
    tiles = []
    for hop in range(CHIPS):
        tile = 2 * ((chip - hop) & (CHIPS - 1))
        tiles.append((refs[hop], pl.multiple_of(8 + TILE * (tile + core), 8)))
        tiles.append((refs[CHIPS + hop], pl.multiple_of(8 + TILE * (tile + 1 - core), 8)))

    @pl.loop(first, first + count)
    def row(rho):
        ls[rho, 0:8] = jnp.zeros((8, CH), F32)
        ls[rho, 8 + WT :] = jnp.zeros((8, CH), F32)
        rs[rho, 0:8] = jnp.zeros((8, CH), F32)
        rs[rho, 8 + WT :] = jnp.zeros((72, CH), F32)
        for ref, at in tiles:
            ls[rho, pl.ds(at, TILE)] = ref[core + rho].astype(F32)
            rs[rho, pl.ds(at, TILE)] = ref[6 + core + rho].astype(F32)
        for si in range(5):
            rb[:, pl.ds(pl.multiple_of((5 * rho + si) * CH, CH), CH)] = rs[rho, 4 + si : 4 + si + JP].astype(BF16)

    return tiles


def fill_meta(tiles, ms):
    for ref, at in tiles:
        ms[pl.ds(at - 8, TILE)] = ref[12].astype(F32)


def split2(value):
    high = value.astype(BF16)
    return high, (value - high.astype(F32)).astype(BF16)


def weighted(a, left, wc_ref, ab, at):
    for si in range(5):
        value = None
        for b in range(3):
            e = b - (si - 2)
            if 0 <= e <= 2:
                term = wc_ref[a, 3 * b + e : 3 * b + e + 1] * left[b]
                value = term if value is None else value + term
        for i, part in enumerate(split3(value)):
            ab[at + i * WT : at + (i + 1) * WT, si * CH : (si + 1) * CH] = part


def row_gradient(q, logits, diag_col, ms, masks):
    lane, level, inside, on_diag, wcol, zeros_count, zeros_mean = masks
    logits = logits - jnp.where(on_diag, diag_col, 0.0)
    top = jnp.max(jnp.where(inside, logits, -3e38), axis=1, keepdims=True)
    top = jnp.where(zeros_count > 0.0, jnp.maximum(top, 0.0), top)
    expd = jnp.where(inside, jnp.exp(logits - top), 0.0)
    zero_exp = jnp.where(zeros_count > 0.0, zeros_count * jnp.exp(-top), 0.0)
    denom = jnp.sum(expd, axis=1, keepdims=True) + zero_exp
    first = jnp.sum(expd * level, axis=1, keepdims=True) + zero_exp * zeros_mean
    inv = 1.0 / denom
    estimate = first * inv
    ext = lax.axis_index("wa") + 1 + q
    meta = ms[...]
    target = jnp.sum(jnp.where(lane == GT_LANE + ext, meta, 0.0), axis=1, keepdims=True)
    valid = jnp.sum(jnp.where(lane == VALID_LANE + ext, meta, 0.0), axis=1, keepdims=True)
    usable = jnp.where(target <= wcol, valid, 0.0)
    resid = estimate - target
    factor = jnp.clip(resid, -1.0, 1.0) * usable * inv
    return expd * (level - estimate) * factor, resid, usable


def diagonal(up, on_diag):
    return jnp.sum(jnp.where(on_diag, up, 0.0), axis=1, keepdims=True)


def row_masks():
    lane = lax.broadcasted_iota(jnp.int32, (WT, CH), 1)
    ww = lax.broadcasted_iota(jnp.int32, (WT, JP), 0)
    jj = lax.broadcasted_iota(jnp.int32, (WT, JP), 1)
    level = (ww - jj + 2).astype(F32)
    inside = (jj <= ww + 2) & (jj >= ww - (WT - 3))
    on_diag = jj == ww + 2
    wcol = lax.broadcasted_iota(jnp.int32, (WT, 1), 0).astype(F32)
    zeros_count = jnp.maximum(float(WT - 3) - wcol, 0.0)
    zeros_mean = (wcol + float(WT + 2)) * 0.5
    return lane, level, inside, on_diag, wcol, zeros_count, zeros_mean


def logits_of(ls, rb, wc_ref, ab, acc):
    for rho in range(5):
        rows = [q for q in range(3) if 0 <= rho - q <= 2]
        left = [ls[rho, 7 + b : 7 + b + WT] for b in range(3)]
        for i, q in enumerate(rows):
            weighted(rho - q, left, wc_ref, ab.at[rho], 3 * WT * i)
        part = dot(ab[rho, 0 : 3 * WT * len(rows)], rb[:, 5 * rho * CH : 5 * (rho + 1) * CH], NT)
        for i, q in enumerate(rows):
            at = 3 * WT * i
            total = part[at : at + WT] + part[at + WT : at + 2 * WT] + part[at + 2 * WT : at + 3 * WT]
            acc[q] = total if rho == q else acc[q] + total


def main_kernel(*refs):
    recv, wc_ref = refs[:8], refs[8]
    sums_ref, kept_ref, given_ref = refs[9:12]
    ls, rs, rb, ms, ab, acc, ub, diags, ks, lb, xs, ys, out_ref, fanned, sem = refs[12:]
    fill_meta(fill(recv, 0, 5, ls, rs, rb), ms)
    ks[...] = jnp.zeros(ks.shape, F32)
    xs[...] = jnp.zeros(xs.shape, F32)
    masks = row_masks()
    logits_of(ls, rb, wc_ref, ab, acc)
    for q in range(3):
        diag = None
        for a in range(3):
            for b in range(3):
                term = wc_ref[a, 3 * b : 3 * b + 1] * ls[q + a, 7 + b : 7 + b + WT] * rs[q + a, 8 + b : 8 + b + WT]
                diag = term if diag is None else diag + term
        up, resid, usable = row_gradient(q, acc[q], jnp.sum(diag, axis=1, keepdims=True), ms, masks)
        ub[2 * WT * q : 2 * WT * q + WT], ub[2 * WT * q + WT : 2 * WT * (q + 1)] = split2(up)
        diags[q] = jnp.broadcast_to(diagonal(up, masks[3]), (WT, CH))
        if q == 1:
            size = jnp.abs(resid)
            smooth = jnp.where(size < 1.0, 0.5 * resid * resid, size - 0.5)
            loss_sum = jnp.sum(usable * smooth, axis=0, keepdims=True)
            count_sum = jnp.sum(usable, axis=0, keepdims=True)
    for b in range(3):
        shifted = ls[2, 7 + b : 7 + b + WT].astype(BF16)
        lb[0:WT, b * CH : (b + 1) * CH] = shifted
        lb[WT:, b * CH : (b + 1) * CH] = shifted

    def tap(q, b, e):
        return wc_ref[2 - q, 3 * b + e : 3 * b + e + 1]

    terms = dot(ub[...], rb[:, 10 * CH : 15 * CH])
    for b in range(3):
        own_left, own_right = ls[2, 7 + b : 7 + b + WT], rs[2, 8 + b : 8 + b + WT]
        total = None
        spread = None
        for q in range(3):
            term = tap(q, b, 0) * diags[q]
            spread = term if spread is None else spread + term
            for e in range(3):
                at, si = 2 * WT * q, b - e + 2
                value = terms[at : at + WT, si * CH : (si + 1) * CH]
                value = value + terms[at + WT : at + 2 * WT, si * CH : (si + 1) * CH]
                if e == 0:
                    value = value - diags[q] * own_right
                at = 9 * (2 - q) + 3 * b + e
                ks[at : at + 1] = jnp.sum(own_left * value, axis=0, keepdims=True)
                term = tap(q, b, e) * value
                total = term if total is None else total + term
        xs[b, 8 : 8 + WT] = total
        xs[3 + b, 8 : 8 + WT] = spread * own_left
    channel = lax.broadcasted_iota(jnp.int32, (8, CH), 1)
    member = group_member().astype(BF16)
    parts = [dot(member, part, NT) for part in split3(ks[...])]
    sums = (parts[0] + (parts[1] + parts[2])) * (1.0 / 16.0)
    sums = jnp.where(channel == LOSS_LANE, loss_sum, sums)
    sums = jnp.where(channel == COUNT_LANE, count_sum, sums)
    sums = jnp.where(channel < SHARE, sums, 0.0)
    quarter = lax.broadcasted_iota(jnp.int32, (8, CH), 0) & 3
    placed = jnp.where(quarter == 0, sums, 0.0)
    for i in range(1, 4):
        placed = placed + jnp.where(quarter == i, pltpu.roll(sums, SHARE * i, 1), 0.0)
    packed = jnp.concatenate([jnp.sum(placed[4 * i : 4 * i + 4], axis=0, keepdims=True) for i in range(2)], axis=1)
    for i in range(sums_ref.shape[0]):
        fanned[i] = packed
    sending = pltpu.make_async_copy(fanned, sums_ref, sem)
    sending.start()
    for q in range(3):
        terms = dot(ub[2 * WT * q : 2 * WT * (q + 1)], lb[...], TN)
        for si in range(5):
            total = None
            for b in range(3):
                e = b - (si - 2)
                if 0 <= e <= 2:
                    term = tap(q, b, e) * terms[:, b * CH : (b + 1) * CH]
                    total = term if total is None else total + term
            ys[si] = total if q == 0 else ys[si] + total
    grad_left = xs[0, 9 : 9 + WT] + xs[1, 8 : 8 + WT] + xs[2, 7 : 7 + WT]
    grad_right = ys[0, 4 : 4 + WT]
    for si in range(1, 5):
        grad_right = grad_right + ys[si, 4 - si : 4 - si + WT]
    for b in range(3):
        grad_right = grad_right - xs[3 + b, 8 - b : 8 - b + WT]
    for dst in range(WA):
        out_ref[dst, 0] = grad_left[TILE * dst : TILE * (dst + 1)].astype(BF16)
        out_ref[dst, 1] = grad_right[TILE * dst : TILE * (dst + 1)].astype(BF16)
    chip, core = position()
    for ref, holder in ((kept_ref, core), (given_ref, 1 - core)):
        beside = chip_at(chip, ahead(holder))
        opposite = chip_at(chip, 2)
        places = (2 * beside + holder, 2 * beside + 1 - holder, 2 * opposite + holder, 2 * chip + holder)
        for i, tile in enumerate(places):
            for side in range(2):
                ref[2 * i + side] = out_ref[tile, side]
    sending.wait()


def ahead(core):
    return 1 - 2 * core


def chip_at(chip, step):
    return (chip + step + CHIPS) & (CHIPS - 1)


def pack_back_kernel(places, kept_ref, got_ref, *refs):
    for place, out_ref in zip(places, refs[-len(places) :]):
        for row, ref in enumerate((kept_ref, got_ref)):
            for side in range(2):
                out_ref[2 * row + side] = ref[2 * place + side]


def finish_kernel(kept, got, near, far, across, sums_ref, left_ref, right_ref, weight_ref, loss_ref):
    chip, core = position()
    other = 1 - core
    before, after, opposite = chip_at(chip, -ahead(core)), chip_at(chip, ahead(core)), chip_at(chip, 2)
    partial = [sums_ref[i] for i in range(8)]
    for i in range(8, sums_ref.shape[0]):
        partial[i % 8] = partial[i % 8] + sums_ref[i]
    while len(partial) > 1:
        partial = [x + y for x, y in zip(partial[0::2], partial[1::2])]
    placed = jnp.concatenate([partial[0][:, 0:CH], partial[0][:, CH:]], axis=0)
    total = jnp.concatenate(
        [pltpu.roll(jnp.broadcast_to(placed[g // 4 : g // 4 + 1], (8, CH)), (CH - SHARE * (g % 4)) % CH, 1)[0:1] for g in range(8)],
        axis=0,
    )
    norm = 1.0 / jnp.maximum(total[0:1, COUNT_LANE : COUNT_LANE + 1], 1.0)
    blocks = (
        (kept, 6, 2 * chip + core),
        (got, 6, 2 * chip + other),
        (near, 0, 2 * before + core),
        (near, 2, 2 * before + other),
        (far, 0, 2 * after + other),
        (far, 2, 2 * after + core),
        (across, 0, 2 * opposite + core),
        (across, 2, 2 * opposite + other),
    )
    for ref, at, row in blocks:
        left_ref[row] = ref[at].astype(F32) * norm
        right_ref[row] = ref[at + 1].astype(F32) * norm
    loss_ref[...] = total[0:1, LOSS_LANE : LOSS_LANE + 1] * norm
    by_tap = jnp.concatenate([total * norm, jnp.zeros((CH - 8, CH), F32)], axis=0).T
    for a in range(3):
        for b in range(3):
            at = 9 * a + 3 * b
            weight_ref[a, b] = by_tap[at : at + 3, 0:8]


def call(kernel, out_shape, *args, scratch=(), flops=0, params=VMEM):
    cost = pl.CostEstimate(flops=flops, bytes_accessed=1 << 20, transcendentals=0)
    return pl.pallas_call(
        kernel, out_shape=out_shape, scratch_shapes=list(scratch), compiler_params=params, cost_estimate=cost
    )(*args)


def swapped(value):
    return lax.ppermute(value, "wa", [(i, i ^ 1) for i in range(WA)])


def shards(left_feat, right_feat, conv_weight, disparity_gt, valid_mask):
    left, right = left_feat[0], right_feat[0]
    gt, valid = disparity_gt[0], valid_mask[0]
    ha_count = lax.axis_size("ha")
    halo = jax.ShapeDtypeStruct((5, TILE, CH), BF16)
    own = jax.ShapeDtypeStruct((2 * ROWS + 1, TILE, CH), BF16)
    args = (left, right, gt, valid, jnp.transpose(conv_weight, (1, 2, 3, 0)))
    args = [pltpu.with_memory_space_constraint(arg, pltpu.HBM) for arg in args]
    arg_copies = (
        pltpu.VMEM((ROWS, TILE, CH), BF16),
        pltpu.VMEM((ROWS, TILE, CH), BF16),
        pltpu.VMEM((ROWS, TILE), jnp.int32),
        pltpu.VMEM((ROWS, TILE), jnp.int32),
        pltpu.VMEM((3, 3, 3, 8), F32),
    )
    up, down = pl.pallas_call(
        halo_kernel,
        out_shape=(halo, halo),
        in_specs=[pl.BlockSpec(memory_space=pltpu.HBM)] * 4,
        scratch_shapes=arg_copies[:4] + (pltpu.SemaphoreType.DMA((4,)),),
        compiler_params=VMEM,
    )(*args[:4])
    own, taps = pl.pallas_call(
        own_tile_kernel,
        out_shape=(own, jax.ShapeDtypeStruct((3, 16, CH), F32)),
        in_specs=[pl.BlockSpec(memory_space=pltpu.HBM)] * 5,
        scratch_shapes=arg_copies + (pltpu.SemaphoreType.DMA((5,)),),
        compiler_params=VMEM,
        cost_estimate=pl.CostEstimate(flops=1 << 30, bytes_accessed=1 << 18, transcendentals=0),
    )(*args)
    before = lax.ppermute(up, "ha", [(i, (i + 1) % ha_count) for i in range(ha_count)])
    after = lax.ppermute(down, "ha", [((i + 1) % ha_count, i) for i in range(ha_count)])
    block = jax.ShapeDtypeStruct((13, TILE, CH), BF16)
    blocks = call(
        pack_kernel,
        (block,) * CHIPS,
        own,
        before,
        after,
        scratch=(pltpu.VMEM((24, TILE, CH), BF16),),
    )
    same_core = [blocks[0]]
    for hop in range(1, CHIPS):
        same_core.append(lax.ppermute(blocks[hop], "wa", [(i, (i + 2 * hop) % WA) for i in range(WA)]))
    other_core = [lax.ppermute(value, "wa", [(i, i ^ 1) for i in range(WA)]) for value in same_core]
    tiles = same_core + other_core
    others = lax.axis_size("dp") * ha_count * WA
    half = jax.ShapeDtypeStruct((8, TILE, CH), BF16)
    sums, kept, given = pl.pallas_call(
        main_kernel,
        out_shape=(jax.ShapeDtypeStruct((others, 1, 2 * CH), F32), half, half),
        out_specs=(pl.BlockSpec(memory_space=pltpu.HBM), pl.BlockSpec(memory_space=pltpu.VMEM), pl.BlockSpec(memory_space=pltpu.VMEM)),
        scratch_shapes=(
            pltpu.VMEM((5, WT + 16, CH), F32),
            pltpu.VMEM((5, WT + 80, CH), F32),
            pltpu.VMEM((JP, 25 * CH), BF16),
            pltpu.VMEM((WT, CH), F32),
            pltpu.VMEM((5, 9 * WT, 5 * CH), BF16),
            pltpu.VMEM((3, WT, JP), F32),
            pltpu.VMEM((6 * WT, JP), BF16),
            pltpu.VMEM((3, WT, CH), F32),
            pltpu.VMEM((CH, CH), F32),
            pltpu.VMEM((2 * WT, 3 * CH), BF16),
            pltpu.VMEM((6, WT + 16, CH), F32),
            pltpu.VMEM((5, JP, CH), F32),
            pltpu.VMEM((WA, 2, TILE, CH), BF16),
            pltpu.VMEM((others, 1, 2 * CH), F32),
            pltpu.SemaphoreType.DMA,
        ),
        compiler_params=VMEM,
        cost_estimate=pl.CostEstimate(flops=5 << 30, bytes_accessed=1 << 20, transcendentals=0),
    )(*tiles, taps)
    sums = lax.all_to_all(sums, ("dp", "ha", "wa"), 0, 0, tiled=True)
    got = swapped(given)
    block = jax.ShapeDtypeStruct((4, TILE, CH), BF16)
    (opposite,) = call(functools.partial(pack_back_kernel, (2,)), (block,), kept, got)
    across = lax.ppermute(opposite, "wa", [(i, (i + 4) % WA) for i in range(WA)])
    beside, beside_other = call(
        functools.partial(pack_back_kernel, (0, 1)), (block,) * 2, kept, got, opposite, flops=1 << 31
    )
    near = lax.ppermute(beside, "wa", [(i, (i + 2 - 4 * (i % 2)) % WA) for i in range(WA)])
    far = lax.ppermute(beside_other, "wa", [(i, (i + 3 - 6 * (i % 2)) % WA) for i in range(WA)])
    tile = jax.ShapeDtypeStruct((ROWS, TILE, CH), F32)
    grad_left, grad_right, weight, loss = call(
        finish_kernel,
        (tile, tile, jax.ShapeDtypeStruct((3, 3, 3, 8), F32), jax.ShapeDtypeStruct((1, 1), F32)),
        kept,
        got,
        near,
        far,
        across,
        sums,
    )
    return (loss[0, 0], grad_left[None], grad_right[None], jnp.transpose(weight, (3, 0, 1, 2)))


def solution(mesh):
    placed = (
        P("dp", "ha", "wa", None),
        P("dp", "ha", "wa", None),
        P(),
        P("dp", "ha", "wa"),
        P("dp", "ha", "wa"),
    )
    return jax.shard_map(
        shards,
        mesh=mesh,
        in_specs=placed,
        out_specs=(P(), P("dp", "ha", "wa", None), P("dp", "ha", "wa", None), P()),
        check_vma=False,
    )
```
